256 devices in a mesh: ctx: 64 (over z, x, core), tp: 4 (over y).
Axes of the slice: x: 4, y: 4, z: 8, core: 2. Of those that a mesh axis runs over, the one named last changes fastest.
Arguments:
- query: bfloat16 [16384, 8192], P('ctx', 'tp'), may hold values from -26 to 26
- key_in: bfloat16 [16384, 8192], P('ctx', 'tp'), may hold values from -6 to 6
- value_in: bfloat16 [16384, 8192], P('ctx', 'tp'), may hold values from -6 to 6
- out_grad: bfloat16 [16384, 8192], P('ctx', 'tp'), may hold values from -6 to 6
- mr_filter: bfloat16 [128, 512], P(None, 'tp'), may hold values from -0.5 to 0.5
- se_filter: bfloat16 [7, 8192], P(None, 'tp'), may hold values from -2 to 2
- gain: float32 [8192], P('tp'), may hold values from 0.1 to 1.9
Outputs:
- query_grad: bfloat16 [16384, 8192], P('ctx', 'tp')
- key_grad: bfloat16 [16384, 8192], P('ctx', 'tp')
- value_grad: bfloat16 [16384, 8192], P('ctx', 'tp')
- mr_filter_grad: float32 [128, 512], P(None, 'tp')
- se_filter_grad: float32 [7, 8192], P(None, 'tp')
- gain_grad: float32 [8192], P('tp')
The draws below stay inside these ranges and needn't reach their ends.
All inputs are finite; a program needn't handle non-finite values.
Results may differ from the reference program's by a relative error of at most 0.0057.
Values may be sent and summed in bfloat16 or wider, within the bound.
No kernel may reach another device: no remote copies, remote signals or barrier semaphores. Data moves between devices by JAX's collectives and lax.ppermute only.
A program may use at most 128 MiB of HBM per device.

```python
import jax
import jax.numpy as jnp
from jax import lax

D = 8192
GROUP = 16
MR_LEN = 128
SE_LEN = 7
TOKENS = 16384
GROUPS = 512


def draw_query(key, part):
    key = jax.random.fold_in(key, 11)
    key_base, key_chan = jax.random.split(key, 2)
    rising = 3.0 ** (jnp.arange(D, dtype=jnp.float32) / D)
    channel_scale = jax.random.uniform(key_chan, (D,), jnp.float32, 0.7, 1.4)
    base_draw = jnp.clip(jax.random.normal(key_base, (TOKENS, D), jnp.float32), -6.0, 6.0)
    return (base_draw * rising * channel_scale).astype(jnp.bfloat16)


def steps_of(key, shape, cuts, least, largest):
    level = 1.0
    for position, blocks in cuts:
        steps = jax.random.uniform(jax.random.fold_in(jax.random.fold_in(key, 6), position), (blocks,), jnp.float32, least / len(cuts), largest / len(cuts))
        level = level * jnp.repeat(jnp.exp(steps), shape[position] // blocks).reshape((-1,) + (1,) * (len(shape) - 1 - position))
    return level


def scatter_about(rng, dims, deviation, most, cuts=(), kind=jnp.bfloat16):
    values = jax.random.normal(rng, dims, jnp.float32) * deviation
    if len(cuts) > 0:
        values = steps_of(rng, dims, cuts, -0.22, 0.18) * values
    return jnp.clip(values, min=-most, max=most).astype(kind)


def setup_inputs(seed: int = 0) -> dict:
    splits = jax.random.split(jax.random.key(seed), 8)
    query = draw_query(jax.random.fold_in(splits[7], 71), 0)
    key_in = scatter_about(splits[1], (TOKENS, D), 1.0, 6.0, ((0, 64), (1, 4)))
    value_in = scatter_about(splits[2], (TOKENS, D), 1.0, 6.0, ((0, 64), (1, 4)))
    out_grad = scatter_about(splits[3], (TOKENS, D), 1.0, 6.0, ((0, 64), (1, 4)))
    mr_filter = scatter_about(splits[4], (MR_LEN, GROUPS), MR_LEN ** -0.5, 0.5, ((1, 4),))
    se_filter = scatter_about(splits[5], (SE_LEN, D), SE_LEN ** -0.5, 2.0, ((1, 4),))
    gain = jnp.clip(1.0 + 0.18 * jax.random.normal(splits[6], (D,), jnp.float32), 0.1, 1.9)
    return dict(query=query, key_in=key_in, value_in=value_in, out_grad=out_grad, mr_filter=mr_filter, se_filter=se_filter, gain=gain)


EPS = 1e-06

def filter_tables(mr_filter):
    row_ids = jnp.arange(MR_LEN)[:, None]
    col_ids = jnp.arange(MR_LEN)[None, :]
    index = (row_ids - col_ids) % MR_LEN
    spread = mr_filter.astype(jnp.float32).T[:, index]
    blank = jnp.zeros_like(spread)
    return (jnp.where(row_ids >= col_ids, spread, blank), jnp.where(row_ids < col_ids, spread, blank))

def medium_conv(extended, present, earlier):
    count = extended.shape[0] - MR_LEN
    channels = extended.shape[1]
    blocks = extended.astype(jnp.float32).reshape(-1, MR_LEN, channels // GROUP, GROUP)
    result = jnp.einsum('grm,bmgi->brgi', present, blocks[1:]) + jnp.einsum('grm,bmgi->brgi', earlier, blocks[:-1])
    return result.reshape(count, channels)

def medium_corr(extended, present, earlier):
    count = extended.shape[0] - MR_LEN
    channels = extended.shape[1]
    blocks = extended.astype(jnp.float32).reshape(-1, MR_LEN, channels // GROUP, GROUP)
    result = jnp.einsum('grm,brgi->bmgi', present, blocks[:-1]) + jnp.einsum('grm,brgi->bmgi', earlier, blocks[1:])
    return result.reshape(count, channels)

def diagonal_sums(current, previous):
    groups = current.shape[0]
    front = jnp.pad(current.reshape(groups, MR_LEN * MR_LEN), ((0, 0), (MR_LEN, 0))).reshape(groups, MR_LEN, MR_LEN + 1)
    back = jnp.pad(previous.reshape(groups, MR_LEN * MR_LEN), ((0, 0), (0, MR_LEN))).reshape(groups, MR_LEN, MR_LEN + 1)
    sums = lax.optimization_barrier(jnp.sum(front[:, :, 1:] + back[:, :, 1:], axis=1))
    return jnp.flip(sums, axis=1).T

def medium_filter_grad(grads, extended):
    channels = extended.shape[1]
    grad_blocks = grads.astype(jnp.float32).reshape(-1, MR_LEN, channels // GROUP, GROUP)
    blocks = extended.astype(jnp.float32).reshape(-1, MR_LEN, channels // GROUP, GROUP)
    current = jnp.einsum('brgi,bmgi->grm', grad_blocks, blocks[1:])
    previous = jnp.einsum('brgi,bmgi->grm', grad_blocks, blocks[:-1])
    row_ids = jnp.arange(MR_LEN)[:, None]
    col_ids = jnp.arange(MR_LEN)[None, :]
    current = jnp.where(row_ids >= col_ids, current, jnp.zeros_like(current))
    previous = jnp.where(row_ids < col_ids, previous, jnp.zeros_like(previous))
    return diagonal_sums(current, previous)

def short_conv(padded, se_filter, count):
    total = jnp.zeros((count, padded.shape[1]), jnp.float32)
    for tap in range(SE_LEN):
        start = SE_LEN - 1 - tap
        total = total + se_filter[tap].astype(jnp.float32) * padded[start:start + count].astype(jnp.float32)
    return total

def short_corr(padded, se_filter, count):
    total = jnp.zeros((count, padded.shape[1]), jnp.float32)
    for tap in range(SE_LEN):
        total = total + se_filter[tap].astype(jnp.float32) * padded[tap:tap + count]
    return total

def short_filter_grad(grads, padded):
    count = grads.shape[0]
    rows_out = []
    for tap in range(SE_LEN):
        start = SE_LEN - 1 - tap
        rows_out.append(lax.optimization_barrier(jnp.sum(grads * padded[start:start + count].astype(jnp.float32), axis=0)))
    return jnp.stack(rows_out)

def reference(query, key_in, value_in, out_grad, mr_filter, se_filter, gain):
    gated = (key_in.astype(jnp.float32) * value_in.astype(jnp.float32)).astype(jnp.bfloat16)
    gated_pad = jnp.concatenate([jnp.zeros((SE_LEN - 1, D), gated.dtype), gated])
    short_mix = short_conv(gated_pad, se_filter, TOKENS).astype(jnp.bfloat16)
    short_ext = jnp.concatenate([jnp.zeros((MR_LEN, D), short_mix.dtype), short_mix])
    present, earlier = filter_tables(mr_filter)
    medium_mix = medium_conv(short_ext, present, earlier)
    mixed = query.astype(jnp.float32) * medium_mix
    norm_grad = out_grad.astype(jnp.float32) * gain.astype(jnp.float32)
    inv_rms = lax.rsqrt(lax.optimization_barrier(jnp.sum(mixed * mixed, axis=1)) / D + EPS)
    inner = lax.optimization_barrier(jnp.sum(norm_grad * mixed, axis=1))
    mixed_grad = inv_rms[:, None] * norm_grad - mixed * (inv_rms ** 3 * inner / D)[:, None]
    query_grad = (mixed_grad * medium_mix).astype(jnp.bfloat16)
    medium_grad = (mixed_grad * query.astype(jnp.float32)).astype(jnp.bfloat16)
    gain_grad = lax.optimization_barrier(jnp.sum(out_grad.astype(jnp.float32) * mixed * inv_rms[:, None], axis=0)) / jnp.sqrt(jnp.float32(TOKENS))
    grad_ext = jnp.concatenate([medium_grad, jnp.zeros((MR_LEN, D), medium_grad.dtype)])
    short_grad = medium_corr(grad_ext, present, earlier)
    short_pad = jnp.concatenate([short_grad, jnp.zeros((SE_LEN - 1, D), short_grad.dtype)])
    gated_grad = short_corr(short_pad, se_filter, TOKENS)
    key_grad = (gated_grad * value_in.astype(jnp.float32)).astype(jnp.bfloat16)
    value_grad = (gated_grad * key_in.astype(jnp.float32)).astype(jnp.bfloat16)
    se_filter_grad = short_filter_grad(short_grad, gated_pad) / jnp.sqrt(jnp.float32(TOKENS))
    mr_filter_grad = medium_filter_grad(medium_grad, short_ext) / jnp.sqrt(jnp.float32(TOKENS * GROUP))
    return (query_grad, key_grad, value_grad, mr_filter_grad, se_filter_grad, gain_grad)
```

```python
import functools

import jax
import jax.numpy as jnp
from jax import lax
from jax.experimental import pallas as pl
from jax.experimental.pallas import tpu as pltpu
from jax.sharding import PartitionSpec as P

D = 8192
GROUP = 16
MR_LEN = 128
SE_LEN = 7
EPS = 1e-06

LANES = 128
HALO = 144
S = 32
W = S + MR_LEN
GT = LANES // GROUP
F32 = jnp.float32
BF16 = jnp.bfloat16


def params(limit=48):
    return pltpu.CompilerParams(vmem_limit_bytes=limit * 1024 * 1024)


def shifted(x, by):
    peers = lax.axis_size("ctx")
    return lax.ppermute(x, "ctx", [(i, i + by) for i in range(peers) if 0 <= i + by < peers])


def group_of_lane(rows):
    return lax.broadcasted_iota(jnp.int32, (rows, LANES), 1) // GROUP


def toeplitz(table, windows):
    results = []
    which = group_of_lane(S)
    for first in range(0, len(windows), 2):
        pair = windows[first : first + 2]
        rhs = jnp.concatenate(pair, axis=1) if len(pair) == 2 else pair[0]
        out = jnp.dot(table, rhs, preferred_element_type=F32)
        for n in range(len(pair)):
            total = out[:S, n * LANES : (n + 1) * LANES]
            for g in range(1, GT):
                part = out[g * S : (g + 1) * S, n * LANES : (n + 1) * LANES]
                total = jnp.where(which == g, part, total)
            results.append(total)
    return results


def table_kernel(front_ref, back_ref, front_out, back_out, scratch):
    for source, target in ((front_ref, front_out), (back_ref, back_out)):
        row = source[...]
        for s in range(S):
            turned = pltpu.roll(row, s, 1) if s else row
            for n in range(2):
                scratch[pl.ds(n * GT * S + s, GT, stride=S), :] = turned[:, n * LANES : (n + 1) * LANES]
        for n in range(2):
            at = slice(n * LANES, (n + 1) * LANES)
            target[:, at] = scratch[n * GT * S : (n + 1) * GT * S, :].astype(BF16)


def tables(front, back):
    groups = front.shape[0]
    tiles = groups // GT
    spec_in = pl.BlockSpec((GT, 2 * LANES), lambda i: (i, 0))
    spec_out = pl.BlockSpec((GT * S, 2 * LANES), lambda i: (i, 0))
    shape = jax.ShapeDtypeStruct((groups * S, 2 * LANES), BF16)
    return pl.pallas_call(
        table_kernel,
        grid=(tiles,),
        in_specs=[spec_in, spec_in],
        out_specs=[spec_out, spec_out],
        out_shape=[shape, shape],
        scratch_shapes=[pltpu.VMEM((2 * GT * S, LANES), F32)],
        compiler_params=params(),
        name="filter_tables",
    )(front, back)


def forward_kernel(
    halo_ref,
    key_ref,
    value_ref,
    query_ref,
    out_grad_ref,
    se_ref,
    gain_ref,
    table_ref,
    medium_out,
    short_out,
    sums_out,
    gated_ref,
    square_ref,
    inner_ref,
):
    tok = key_ref.shape[0]
    step = pl.program_id(0)
    gated_ref[:HALO, :] = halo_ref[...].astype(F32)
    gated = (key_ref[...].astype(F32) * value_ref[...].astype(F32)).astype(BF16)
    gated_ref[HALO:, :] = gated.astype(F32)
    rows = tok + MR_LEN
    base = HALO - MR_LEN
    short = jnp.zeros((rows, LANES), F32)
    for tap in range(SE_LEN):
        short = short + se_ref[tap : tap + 1, :] * gated_ref[base - tap : base - tap + rows, :]
    short_out[...] = short.astype(BF16)
    table = table_ref[:, :W]
    windows = [short_out[S * b : S * b + W, :] for b in range(tok // S)]
    parts = toeplitz(table, windows)
    gain = gain_ref[...]

    @pl.when(step == 0)
    def _():
        square_ref[...] = jnp.zeros_like(square_ref)
        inner_ref[...] = jnp.zeros_like(inner_ref)

    for b, medium in enumerate(parts):
        at = slice(S * b, S * b + S)
        medium_out[at, :] = medium
        mixed = query_ref[at, :].astype(F32) * medium
        norm_grad = out_grad_ref[at, :].astype(F32) * gain
        square_ref[at, :] += mixed * mixed
        inner_ref[at, :] += norm_grad * mixed

    @pl.when(step == pl.num_programs(0) - 1)
    def _():
        square = jnp.sum(square_ref[...].T, axis=0, keepdims=True)
        inner = jnp.sum(inner_ref[...].T, axis=0, keepdims=True)
        sums_out[0:1, :] = square
        sums_out[1:2, :] = inner


def forward(halo, key_in, value_in, query, out_grad, se, gain, table):
    tok, channels = key_in.shape
    tiles = channels // LANES
    col = lambda rows: pl.BlockSpec((rows, LANES), lambda i: (0, i))
    return pl.pallas_call(
        forward_kernel,
        grid=(tiles,),
        in_specs=[
            col(HALO),
            col(tok),
            col(tok),
            col(tok),
            col(tok),
            col(8),
            col(1),
            pl.BlockSpec((GT * S, 2 * LANES), lambda i: (i, 0)),
        ],
        out_specs=[col(tok), col(tok + MR_LEN), pl.BlockSpec((2, tok), lambda i: (0, 0))],
        out_shape=[
            jax.ShapeDtypeStruct((tok, channels), F32),
            jax.ShapeDtypeStruct((tok + MR_LEN, channels), BF16),
            jax.ShapeDtypeStruct((2, tok), F32),
        ],
        scratch_shapes=[
            pltpu.VMEM((HALO + tok, LANES), F32),
            pltpu.VMEM((tok, LANES), F32),
            pltpu.VMEM((tok, LANES), F32),
        ],
        compiler_params=params(),
        name="forward",
    )(halo, key_in, value_in, query, out_grad, se, gain, table)


def spread_sums(sums, scale_ref, slope_ref, rows):
    square = jnp.broadcast_to(sums[0:1, :], (LANES, sums.shape[1])).T[:rows]
    inner = jnp.broadcast_to(sums[1:2, :], (LANES, sums.shape[1])).T[:rows]
    inv = lax.rsqrt(square / D + EPS)
    scale_ref[...] = inv
    slope_ref[...] = inv * inv * inv * inner / D


def head_kernel(sums_ref, query_ref, out_grad_ref, medium_ref, gain_ref, head_out, scale_ref, slope_ref):
    @pl.when(pl.program_id(0) == 0)
    def _():
        spread_sums(sums_ref[...], scale_ref, slope_ref, HALO)

    for n in range(query_ref.shape[1] // LANES):
        at = slice(n * LANES, (n + 1) * LANES)
        query = query_ref[:, at].astype(F32)
        norm_grad = out_grad_ref[:, at].astype(F32) * gain_ref[:, at]
        mixed = query * medium_ref[:, at]
        mixed_grad = scale_ref[...] * norm_grad - mixed * slope_ref[...]
        head_out[:, at] = (mixed_grad * query).astype(BF16)


def head(sums, query, out_grad, medium, gain):
    tok, channels = query.shape
    width = 512
    col = lambda rows: pl.BlockSpec((rows, width), lambda i: (0, i))
    return pl.pallas_call(
        head_kernel,
        grid=(channels // width,),
        in_specs=[pl.BlockSpec((2, tok), lambda i: (0, 0)), col(HALO), col(HALO), col(HALO), col(1)],
        out_specs=col(HALO),
        out_shape=jax.ShapeDtypeStruct((HALO, channels), BF16),
        scratch_shapes=[pltpu.VMEM((HALO, LANES), F32), pltpu.VMEM((HALO, LANES), F32)],
        compiler_params=params(),
        name="head_rows",
    )(sums, query, out_grad, medium, gain)


def wide_kernel(halo_ref, key_ref, value_ref, table_ref, wide_out, gated_ref):
    tok = key_ref.shape[0]
    lead = W - HALO
    gated_ref[:lead, :] = jnp.zeros((lead, LANES), BF16)
    gated_ref[lead:W, :] = halo_ref[...]
    gated_ref[W:, :] = (key_ref[...].astype(F32) * value_ref[...].astype(F32)).astype(BF16)
    windows = [gated_ref[S * b : S * b + W, :] for b in range(tok // S + 1)]
    for b, part in enumerate(toeplitz(table_ref[:, :W], windows)):
        wide_out[S * b : S * b + S, :] = part


def wide(halo, key_in, value_in, table):
    tok, channels = key_in.shape
    col = lambda rows: pl.BlockSpec((rows, LANES), lambda i: (0, i))
    return pl.pallas_call(
        wide_kernel,
        grid=(channels // LANES,),
        in_specs=[col(HALO), col(tok), col(tok), pl.BlockSpec((GT * S, 2 * LANES), lambda i: (i, 0))],
        out_specs=col(tok + S),
        out_shape=jax.ShapeDtypeStruct((tok + S, channels), F32),
        scratch_shapes=[pltpu.VMEM((W + tok, LANES), BF16)],
        compiler_params=params(),
        name="wide_gated",
    )(halo, key_in, value_in, table)


def grads_kernel(
    sums_ref,
    query_ref,
    out_grad_ref,
    medium_ref,
    gain_ref,
    short_ref,
    wide_ref,
    query_grad_out,
    medium_grad_out,
    packed_out,
    scale_ref,
    slope_ref,
    cross_ref,
):
    tok = query_ref.shape[0]

    @pl.when(pl.program_id(0) == 0)
    def _():
        spread_sums(sums_ref[...], scale_ref, slope_ref, tok)

    query = query_ref[...].astype(F32)
    out_grad = out_grad_ref[...].astype(F32)
    medium = medium_ref[...]
    inv = scale_ref[...]
    norm_grad = out_grad * gain_ref[...]
    mixed = query * medium
    mixed_grad = inv * norm_grad - mixed * slope_ref[...]
    query_grad_out[...] = (mixed_grad * medium).astype(BF16)
    medium_grad = (mixed_grad * query).astype(BF16)
    medium_grad_out[...] = medium_grad
    gain_row = jnp.sum(out_grad * mixed * inv, axis=0, keepdims=True)
    wide_grad = medium_grad.astype(F32)
    for tap in range(SE_LEN):
        packed_out[GT + tap : GT + tap + 1, :] = jnp.sum(
            wide_grad * wide_ref[S - tap : S - tap + tok, :], axis=0, keepdims=True
        )
    packed_out[GT + SE_LEN : GT + SE_LEN + 1, :] = gain_row
    blocks = tok // S
    lhs_rows = jnp.concatenate([medium_grad[S * b : S * b + S, :] for b in range(blocks)], axis=1)
    which = lax.broadcasted_iota(jnp.int32, lhs_rows.shape, 1) % LANES // GROUP
    lhs = jnp.concatenate(
        [jnp.where(which == g, lhs_rows, jnp.zeros_like(lhs_rows)) for g in range(GT)], axis=0
    )
    rhs = jnp.concatenate([short_ref[S * b : S * b + W, :] for b in range(blocks)], axis=1)
    cross = lax.dot_general(lhs, rhs, (((1,), (1,)), ((), ())), preferred_element_type=F32)
    cross_ref[: GT * S, :] = cross[:, :LANES]
    cross_ref[GT * S :, :S] = cross[:, LANES:]
    total = jnp.zeros((GT, 2 * LANES), F32)
    for s in range(S):
        part = jnp.concatenate(
            [cross_ref[pl.ds(n * GT * S + s, GT, stride=S), :] for n in range(2)], axis=1
        )
        total = total + pltpu.roll(part, 2 * LANES - 1 - s, 1)
    packed_out[:GT, :] = total[:, :LANES]


def grads(sums, query, out_grad, medium, gain, short, wide_rows):
    tok, channels = query.shape
    tiles = channels // LANES
    col = lambda rows: pl.BlockSpec((rows, LANES), lambda i: (0, i))
    return pl.pallas_call(
        grads_kernel,
        grid=(tiles,),
        in_specs=[
            pl.BlockSpec((2, tok), lambda i: (0, 0)),
            col(tok),
            col(tok),
            col(tok),
            col(1),
            col(tok + MR_LEN),
            col(tok + S),
        ],
        out_specs=[col(tok), col(tok), pl.BlockSpec((2 * GT, LANES), lambda i: (i, 0))],
        out_shape=[
            jax.ShapeDtypeStruct((tok, channels), BF16),
            jax.ShapeDtypeStruct((tok, channels), BF16),
            jax.ShapeDtypeStruct((2 * GT * tiles, LANES), F32),
        ],
        scratch_shapes=[
            pltpu.VMEM((tok, LANES), F32),
            pltpu.VMEM((tok, LANES), F32),
            pltpu.VMEM((2 * GT * S, LANES), F32),
        ],
        compiler_params=params(),
        name="gradients",
    )(sums, query, out_grad, medium, gain, short, wide_rows)


def backward_kernel(
    grad_ref, halo_ref, se_ref, key_ref, value_ref, table_ref, key_out, value_out, ext_ref, short_ref
):
    tok = key_ref.shape[0]
    ext_ref[:tok, :] = grad_ref[...]
    ext_ref[tok : tok + HALO, :] = halo_ref[...]
    ext_ref[tok + HALO :, :] = jnp.zeros((W - HALO, LANES), BF16)
    windows = [ext_ref[S * b : S * b + W, :] for b in range(tok // S + 1)]
    for b, part in enumerate(toeplitz(table_ref[:, :W], windows)):
        short_ref[S * b : S * b + S, :] = part
    total = jnp.zeros((tok, LANES), F32)
    for tap in range(SE_LEN):
        total = total + se_ref[tap : tap + 1, :] * short_ref[tap : tap + tok, :]
    key_out[...] = (total * value_ref[...].astype(F32)).astype(BF16)
    value_out[...] = (total * key_ref[...].astype(F32)).astype(BF16)


def backward(medium_grad, halo, se, key_in, value_in, table):
    tok, channels = key_in.shape
    col = lambda rows: pl.BlockSpec((rows, LANES), lambda i: (0, i))
    shape = jax.ShapeDtypeStruct((tok, channels), BF16)
    return pl.pallas_call(
        backward_kernel,
        grid=(channels // LANES,),
        in_specs=[
            col(tok),
            col(HALO),
            col(8),
            col(tok),
            col(tok),
            pl.BlockSpec((GT * S, 2 * LANES), lambda i: (i, 0)),
        ],
        out_specs=[col(tok), col(tok)],
        out_shape=[shape, shape],
        scratch_shapes=[pltpu.VMEM((tok + W, LANES), BF16), pltpu.VMEM((tok + S, LANES), F32)],
        compiler_params=params(),
        name="backward",
    )(medium_grad, halo, se, key_in, value_in, table)


def finish_kernel(tokens, packed_ref, mr_out, se_out, gain_out):
    tiles = packed_ref.shape[0] // (2 * GT)
    rows = jnp.concatenate([packed_ref[2 * GT * i : 2 * GT * i + GT, :] for i in range(tiles)], axis=0)
    row_ids = lax.broadcasted_iota(jnp.int32, (MR_LEN, MR_LEN), 0)
    col_ids = lax.broadcasted_iota(jnp.int32, (MR_LEN, MR_LEN), 1)
    flip = jnp.where(row_ids + col_ids == MR_LEN - 1, 1.0, 0.0).astype(F32)
    mr_out[...] = lax.dot_general(
        flip, rows, (((1,), (1,)), ((), ())), preferred_element_type=F32, precision=lax.Precision.HIGHEST
    ) * (1.0 / (tokens * GROUP) ** 0.5)
    for i in range(tiles):
        at = slice(i * LANES, (i + 1) * LANES)
        low = 2 * GT * i + GT
        se_out[:, at] = packed_ref[low : low + SE_LEN, :] * (1.0 / tokens**0.5)
        gain_out[:, at] = packed_ref[low + SE_LEN : low + SE_LEN + 1, :] * (1.0 / tokens**0.5)


def finish(packed, tokens, channels):
    return pl.pallas_call(
        functools.partial(finish_kernel, tokens),
        out_shape=[
            jax.ShapeDtypeStruct((MR_LEN, channels // GROUP), F32),
            jax.ShapeDtypeStruct((SE_LEN, channels), F32),
            jax.ShapeDtypeStruct((1, channels), F32),
        ],
        compiler_params=params(),
        name="finish",
    )(packed)


def sum_over_ctx(packed):
    peers = lax.axis_size("ctx")
    parts = packed.reshape(peers, packed.shape[0] // peers, packed.shape[1])
    mine = jnp.sum(lax.all_to_all(parts, "ctx", 0, 0), axis=0)
    everyone = lax.all_to_all(jnp.broadcast_to(mine[None], parts.shape), "ctx", 0, 0)
    return everyone.reshape(packed.shape)


def local(query, key_in, value_in, out_grad, mr_filter, se_filter, gain):
    tok, channels = query.shape
    tokens_all = tok * lax.axis_size("ctx")
    tail = (key_in[-HALO:].astype(F32) * value_in[-HALO:].astype(F32)).astype(BF16)
    gated_halo = shifted(tail, 1)
    taps = mr_filter.astype(F32).T
    front = jnp.pad(jnp.flip(taps, axis=1), ((0, 0), (1, LANES - 1)))
    back = jnp.pad(taps, ((0, 0), (0, LANES)))
    front_table, back_table = tables(front, back)
    se = jnp.pad(se_filter.astype(F32), ((0, 1), (0, 0)))
    gain_row = gain[None, :]
    medium, short, sums = forward(
        gated_halo, key_in, value_in, query, out_grad, se, gain_row, front_table
    )
    sums = lax.psum(sums, "tp")
    wide_rows = wide(gated_halo, key_in, value_in, front_table)
    head_rows = head(sums, query, out_grad, medium, gain_row)
    grad_halo = shifted(head_rows, -1)
    query_grad, medium_grad, packed = grads(
        sums, query, out_grad, medium, gain_row, short, wide_rows
    )
    packed = sum_over_ctx(packed)
    key_grad, value_grad = backward(medium_grad, grad_halo, se, key_in, value_in, back_table)
    mr_grad, se_grad, gain_grad = finish(packed, tokens_all, channels)
    return query_grad, key_grad, value_grad, mr_grad, se_grad, gain_grad[0]


def solution(mesh):
    return jax.shard_map(
        local,
        mesh=mesh,
        in_specs=(
            P("ctx", "tp"),
            P("ctx", "tp"),
            P("ctx", "tp"),
            P("ctx", "tp"),
            P(None, "tp"),
            P(None, "tp"),
            P("tp"),
        ),
        out_specs=(
            P("ctx", "tp"),
            P("ctx", "tp"),
            P("ctx", "tp"),
            P(None, "tp"),
            P(None, "tp"),
            P("tp"),
        ),
        check_vma=False,
    )
```

```python
import functools

import jax
import jax.numpy as jnp
from jax import lax
from jax.experimental import pallas as pl
from jax.experimental.pallas import tpu as pltpu
from jax.sharding import PartitionSpec as P

D = 8192
GROUP = 16
MR_LEN = 128
SE_LEN = 7
EPS = 1e-06

LANES = 128
HALO = 144
S = 32
W = S + MR_LEN
GT = LANES // GROUP
EARLY = S + MR_LEN
F32 = jnp.float32
BF16 = jnp.bfloat16


UNROLL = 4
VMEM = pl.BlockSpec(memory_space=pltpu.VMEM)


def params(limit=24):
    return pltpu.CompilerParams(vmem_limit_bytes=limit * 1024 * 1024)


def each_tile(channels, body):
    def step(i, carry):
        for slot in range(UNROLL):
            tile = i * UNROLL + slot
            body(pl.ds(pl.multiple_of(tile * LANES, LANES), LANES), tile, slot)
        return carry

    lax.fori_loop(0, channels // LANES // UNROLL, step, 0)


def of_tile(tile, rows):
    return pl.ds(pl.multiple_of(tile * rows, rows), rows)


def call(body, name, outs, scratch, *args):
    return pl.pallas_call(
        body,
        in_specs=[VMEM] * len(args),
        out_specs=[VMEM] * len(outs),
        out_shape=[jax.ShapeDtypeStruct(shape, dtype) for shape, dtype in outs],
        scratch_shapes=scratch,
        compiler_params=params(),
        name=name,
    )(*args)


def shifted(x, by):
    peers = lax.axis_size("ctx")
    return lax.ppermute(x, "ctx", [(i, i + by) for i in range(peers) if 0 <= i + by < peers])


def group_of_lane(rows):
    return lax.broadcasted_iota(jnp.int32, (rows, LANES), 1) // GROUP


def toeplitz(table, windows):
    results = []
    which = group_of_lane(S)
    for first in range(0, len(windows), 2):
        pair = windows[first : first + 2]
        rhs = jnp.concatenate(pair, axis=1) if len(pair) == 2 else pair[0]
        out = jnp.dot(table, rhs, preferred_element_type=F32)
        for n in range(len(pair)):
            total = out[:S, n * LANES : (n + 1) * LANES]
            for g in range(1, GT):
                part = out[g * S : (g + 1) * S, n * LANES : (n + 1) * LANES]
                total = jnp.where(which == g, part, total)
            results.append(total)
    return results


def table_kernel(front_ref, back_ref, front_out, back_out):
    def one(g, carry):
        for source, target in ((front_ref, front_out), (back_ref, back_out)):
            rows = source[of_tile(g, GT), :]
            for k in range(GT):
                row = jnp.broadcast_to(rows[k : k + 1, :], (S, 2 * LANES))
                turned = pltpu.roll(row, 0, 1, stride=1, stride_axis=0).astype(BF16)
                target[of_tile(g * GT + k, S), :] = turned
        return carry

    lax.fori_loop(0, front_ref.shape[0] // GT, one, 0)


def tables(front, back):
    shape = ((front.shape[0] * S, 2 * LANES), BF16)
    return call(table_kernel, "filter_tables", [shape, shape], [], front, back)


def short_filter(se_ref, at, gated_ref, first, rows):
    total = jnp.zeros((rows, LANES), F32)
    for tap in range(SE_LEN):
        total = total + se_ref[tap : tap + 1, at] * gated_ref[first - tap : first - tap + rows, :]
    return total.astype(BF16)


def gate(key_ref, value_ref, rows, at):
    return (key_ref[rows, at].astype(F32) * value_ref[rows, at].astype(F32)).astype(BF16)


def early_kernel(
    key_ref,
    value_ref,
    query_ref,
    out_grad_ref,
    se_ref,
    gain_ref,
    table_ref,
    medium_out,
    short_out,
    wide_out,
    square_out,
    inner_out,
    gated_ref,
):
    tok, channels = key_ref.shape
    square_out[...] = jnp.zeros_like(square_out)
    inner_out[...] = jnp.zeros_like(inner_out)

    def body(at, tile, slot):
        wide_ref = gated_ref.at[slot]
        gated = gate(key_ref, value_ref, slice(None), at)
        wide_ref[...] = gated.astype(F32)
        short_out[:S, at] = jnp.zeros((S, LANES), BF16)
        short_out[S:, at] = short_filter(se_ref, at, wide_ref, S, tok - S)
        short_out[16:S, at] = short_filter(se_ref, at, wide_ref, 16, S - 16)
        table = table_ref[of_tile(tile, GT * S), :W]
        first = [t for t in range(EARLY, tok, S)]
        windows = [short_out[t - MR_LEN : t + S, at] for t in first]
        also = [t for t in range(MR_LEN, tok, S)]
        windows += [gated[t - MR_LEN : t + S, :] for t in also]
        parts = toeplitz(table, windows)
        gain = gain_ref[:, at]
        for t, medium in zip(first, parts):
            down = slice(t - EARLY, t - EARLY + S)
            medium_out[down, at] = medium
            mixed = query_ref[t : t + S, at].astype(F32) * medium
            norm_grad = out_grad_ref[t : t + S, at].astype(F32) * gain
            square_out[down, :] += mixed * mixed
            inner_out[down, :] += norm_grad * mixed
        for t, part in zip(also, parts[len(first) :]):
            wide_out[t - MR_LEN : t - MR_LEN + S, at] = part

    each_tile(channels, body)


def early(key_in, value_in, query, out_grad, se, gain, table):
    tok, channels = key_in.shape
    outs = [
        ((tok - EARLY, channels), F32),
        ((tok, channels), BF16),
        ((tok - MR_LEN, channels), F32),
        ((tok - EARLY, LANES), F32),
        ((tok - EARLY, LANES), F32),
    ]
    scratch = [pltpu.VMEM((UNROLL, tok, LANES), F32)]
    return call(early_kernel, "early", outs, scratch, key_in, value_in, query, out_grad, se, gain, table)


def window(low_ref, high_ref, b, at):
    if b * S >= EARLY:
        return high_ref[b * S - MR_LEN : b * S + S, at]
    if b == 0:
        return low_ref[:, at]
    return jnp.concatenate([low_ref[S * b :, at], high_ref[S : S * b + S, at]], axis=0)


def late_kernel(
    halo_ref,
    key_ref,
    value_ref,
    query_ref,
    out_grad_ref,
    se_ref,
    gain_ref,
    table_ref,
    high_ref,
    square_in,
    inner_in,
    medium_out,
    low_out,
    sums_out,
    gated_ref,
    square_ref,
    inner_ref,
):
    channels = key_ref.shape[1]
    square_ref[:EARLY, :] = jnp.zeros((EARLY, LANES), F32)
    inner_ref[:EARLY, :] = jnp.zeros((EARLY, LANES), F32)
    square_ref[EARLY:, :] = square_in[...]
    inner_ref[EARLY:, :] = inner_in[...]

    def body(at, tile, slot):
        rows = gated_ref.at[slot]
        rows[:HALO, :] = halo_ref[:, at].astype(F32)
        rows[HALO:, :] = gate(key_ref, value_ref, slice(0, S), at).astype(F32)
        low_out[:, at] = short_filter(se_ref, at, rows, HALO - MR_LEN, MR_LEN + S)
        table = table_ref[of_tile(tile, GT * S), :W]
        windows = [window(low_out, high_ref, b, at) for b in range(EARLY // S)]
        gain = gain_ref[:, at]
        for b, medium in enumerate(toeplitz(table, windows)):
            down = slice(S * b, S * b + S)
            medium_out[down, at] = medium
            mixed = query_ref[down, at].astype(F32) * medium
            norm_grad = out_grad_ref[down, at].astype(F32) * gain
            square_ref[down, :] += mixed * mixed
            inner_ref[down, :] += norm_grad * mixed

    each_tile(channels, body)
    sums_out[0:1, :] = jnp.sum(square_ref[...].T, axis=0, keepdims=True)
    sums_out[1:2, :] = jnp.sum(inner_ref[...].T, axis=0, keepdims=True)


def late(halo, key_in, value_in, query, out_grad, se, gain, table, short_high, square, inner):
    tok, channels = key_in.shape
    outs = [((EARLY, channels), F32), ((MR_LEN + S, channels), BF16), ((2, tok), F32)]
    scratch = [
        pltpu.VMEM((UNROLL, HALO + S, LANES), F32),
        pltpu.VMEM((tok, LANES), F32),
        pltpu.VMEM((tok, LANES), F32),
    ]
    return call(
        late_kernel,
        "late",
        outs,
        scratch,
        halo,
        key_in,
        value_in,
        query,
        out_grad,
        se,
        gain,
        table,
        short_high,
        square,
        inner,
    )


def spread_sums(parts, scale_ref, slope_ref, rows):
    sums = functools.reduce(jnp.add, [part[...] for part in parts])
    square = jnp.broadcast_to(sums[0:1, :], (LANES, sums.shape[1])).T[:rows]
    inner = jnp.broadcast_to(sums[1:2, :], (LANES, sums.shape[1])).T[:rows]
    inv = lax.rsqrt(square / D + EPS)
    scale_ref[...] = inv
    slope_ref[...] = inv * inv * inv * inner / D


def head_kernel(query_ref, out_grad_ref, medium_ref, gain_ref, *rest):
    sums, (head_out, scale_ref, slope_ref) = rest[:-3], rest[-3:]
    spread_sums(sums, scale_ref, slope_ref, HALO)

    def body(at, tile, slot):
        query = query_ref[:HALO, at].astype(F32)
        norm_grad = out_grad_ref[:HALO, at].astype(F32) * gain_ref[:, at]
        mixed = query * medium_ref[:HALO, at]
        mixed_grad = scale_ref[...] * norm_grad - mixed * slope_ref[...]
        head_out[:, at] = (mixed_grad * query).astype(BF16)

    each_tile(query_ref.shape[1], body)


def head(sums, query, out_grad, medium_low, gain):
    outs = [((HALO, query.shape[1]), BF16)]
    scratch = [pltpu.VMEM((HALO, LANES), F32), pltpu.VMEM((HALO, LANES), F32)]
    return call(head_kernel, "head_rows", outs, scratch, query, out_grad, medium_low, gain, *sums)[0]


def wide_kernel(halo_ref, key_ref, value_ref, table_ref, wide_out, gated_ref):
    lead = W - HALO

    def body(at, tile, slot):
        rows = gated_ref.at[slot]
        rows[:lead, :] = jnp.zeros((lead, LANES), BF16)
        rows[lead:W, :] = halo_ref[:, at]
        rows[W:, :] = gate(key_ref, value_ref, slice(0, MR_LEN), at)
        windows = [rows[S * b : S * b + W, :] for b in range(MR_LEN // S + 1)]
        for b, part in enumerate(toeplitz(table_ref[of_tile(tile, GT * S), :W], windows)):
            wide_out[S * b : S * b + S, at] = part

    each_tile(key_ref.shape[1], body)


def wide(halo, key_in, value_in, table):
    outs = [((MR_LEN + S, key_in.shape[1]), F32)]
    scratch = [pltpu.VMEM((UNROLL, W + MR_LEN, LANES), BF16)]
    return call(wide_kernel, "wide_gated", outs, scratch, halo, key_in, value_in, table)[0]


def grads_kernel(
    query_ref,
    out_grad_ref,
    medium_low_ref,
    medium_high_ref,
    gain_ref,
    short_low_ref,
    short_high_ref,
    wide_low_ref,
    wide_high_ref,
    *rest,
):
    query_grad_out, medium_grad_out, packed_out, scale_ref, slope_ref, cross_ref, wide_ref = rest[-7:]
    tok, channels = query_ref.shape
    spread_sums(rest[:-7], scale_ref, slope_ref, tok)
    blocks = tok // S
    side = GT * S

    def body(at, tile, slot):
        query = query_ref[:, at].astype(F32)
        out_grad = out_grad_ref[:, at].astype(F32)
        medium = jnp.concatenate([medium_low_ref[:, at], medium_high_ref[:, at]], axis=0)
        inv = scale_ref[...]
        norm_grad = out_grad * gain_ref[:, at]
        mixed = query * medium
        mixed_grad = inv * norm_grad - mixed * slope_ref[...]
        query_grad_out[:, at] = (mixed_grad * medium).astype(BF16)
        medium_grad = (mixed_grad * query).astype(BF16)
        medium_grad_out[:, at] = medium_grad
        gain_row = jnp.sum(out_grad * mixed * inv, axis=0, keepdims=True)
        wide_grad = medium_grad.astype(F32)
        rows = wide_ref.at[slot]
        rows[: MR_LEN + S, :] = wide_low_ref[:, at]
        rows[MR_LEN + S :, :] = wide_high_ref[:, at]
        lines = [
            jnp.sum(wide_grad * rows[S - tap : S - tap + tok, :], axis=0, keepdims=True)
            for tap in range(SE_LEN)
        ]
        lhs_rows = jnp.concatenate([medium_grad[S * b : S * b + S, :] for b in range(blocks)], axis=1)
        which = lax.broadcasted_iota(jnp.int32, lhs_rows.shape, 1) % LANES // GROUP
        lhs = jnp.concatenate(
            [jnp.where(which == g, lhs_rows, jnp.zeros_like(lhs_rows)) for g in range(GT)], axis=0
        )
        rhs = jnp.concatenate(
            [window(short_low_ref, short_high_ref, b, at) for b in range(blocks)], axis=1
        )
        cross = lax.dot_general(lhs, rhs, (((1,), (1,)), ((), ())), preferred_element_type=F32)
        held = cross_ref.at[slot]
        held[:side, :] = cross[:, :LANES]
        held[side:, :S] = cross[:, LANES:]
        total = jnp.zeros((GT, 2 * LANES), F32)
        for s in range(S):
            part = jnp.concatenate(
                [held[pl.ds(m * side + s, GT, stride=S), :] for m in range(2)], axis=1
            )
            total = total + pltpu.roll(part, 2 * LANES - 1 - s, 1)
        packed_out[of_tile(tile, 2 * GT), :] = jnp.concatenate(
            [total[:, :LANES]] + lines + [gain_row], axis=0
        )

    each_tile(channels, body)


def grads(sums, query, out_grad, medium_low, medium_high, gain, short_low, short_high, wide_low, wide_high):
    tok, channels = query.shape
    outs = [
        ((tok, channels), BF16),
        ((tok, channels), BF16),
        ((2 * GT * channels // LANES, LANES), F32),
    ]
    scratch = [
        pltpu.VMEM((tok, LANES), F32),
        pltpu.VMEM((tok, LANES), F32),
        pltpu.VMEM((UNROLL, 2 * GT * S, LANES), F32),
        pltpu.VMEM((UNROLL, tok + S, LANES), F32),
    ]
    return call(
        grads_kernel,
        "gradients",
        outs,
        scratch,
        query,
        out_grad,
        medium_low,
        medium_high,
        gain,
        short_low,
        short_high,
        wide_low,
        wide_high,
        *sums,
    )


def backward_kernel(
    grad_ref, halo_ref, se_ref, key_ref, value_ref, table_ref, key_out, value_out, ext_ref, short_ref
):
    tok = key_ref.shape[0]

    def body(at, tile, slot):
        ext = ext_ref.at[slot]
        short = short_ref.at[slot]
        ext[:tok, :] = grad_ref[:, at]
        ext[tok : tok + HALO, :] = halo_ref[:, at]
        ext[tok + HALO :, :] = jnp.zeros((W - HALO, LANES), BF16)
        windows = [ext[S * b : S * b + W, :] for b in range(tok // S + 1)]
        for b, part in enumerate(toeplitz(table_ref[of_tile(tile, GT * S), :W], windows)):
            short[S * b : S * b + S, :] = part
        total = jnp.zeros((tok, LANES), F32)
        for tap in range(SE_LEN):
            total = total + se_ref[tap : tap + 1, at] * short[tap : tap + tok, :]
        key_out[:, at] = (total * value_ref[:, at].astype(F32)).astype(BF16)
        value_out[:, at] = (total * key_ref[:, at].astype(F32)).astype(BF16)

    each_tile(key_ref.shape[1], body)


def backward(medium_grad, halo, se, key_in, value_in, table):
    tok, channels = key_in.shape
    outs = [((tok, channels), BF16), ((tok, channels), BF16)]
    scratch = [
        pltpu.VMEM((UNROLL, tok + W, LANES), BF16),
        pltpu.VMEM((UNROLL, tok + S, LANES), F32),
    ]
    return call(backward_kernel, "backward", outs, scratch, medium_grad, halo, se, key_in, value_in, table)


def finish_kernel(tokens, packed_ref, mr_out, se_out, gain_out):
    tiles = packed_ref.shape[0] // (2 * GT)
    rows = jnp.concatenate([packed_ref[2 * GT * i : 2 * GT * i + GT, :] for i in range(tiles)], axis=0)
    row_ids = lax.broadcasted_iota(jnp.int32, (MR_LEN, MR_LEN), 0)
    col_ids = lax.broadcasted_iota(jnp.int32, (MR_LEN, MR_LEN), 1)
    flip = jnp.where(row_ids + col_ids == MR_LEN - 1, 1.0, 0.0).astype(F32)
    mr_out[...] = lax.dot_general(
        flip, rows, (((1,), (1,)), ((), ())), preferred_element_type=F32, precision=lax.Precision.HIGHEST
    ) * (1.0 / (tokens * GROUP) ** 0.5)
    for i in range(tiles):
        at = slice(i * LANES, (i + 1) * LANES)
        low = 2 * GT * i + GT
        se_out[:, at] = packed_ref[low : low + SE_LEN, :] * (1.0 / tokens**0.5)
        gain_out[:, at] = packed_ref[low + SE_LEN : low + SE_LEN + 1, :] * (1.0 / tokens**0.5)


def finish(packed, tokens, channels):
    return pl.pallas_call(
        functools.partial(finish_kernel, tokens),
        out_shape=[
            jax.ShapeDtypeStruct((MR_LEN, channels // GROUP), F32),
            jax.ShapeDtypeStruct((SE_LEN, channels), F32),
            jax.ShapeDtypeStruct((1, channels), F32),
        ],
        compiler_params=params(),
        name="finish",
    )(packed)


def from_peers(x, axis):
    peers = lax.axis_size(axis)
    return [lax.ppermute(x, axis, [(i, (i + k) % peers) for i in range(peers)]) for k in range(1, peers)]


def sum_over_ctx(packed, beside):
    peers = lax.axis_size("ctx")
    parts = packed.reshape(peers, packed.shape[0] // peers, packed.shape[1])
    arrived, other = lax.optimization_barrier((lax.all_to_all(parts, "ctx", 0, 0), beside()))
    mine = jnp.sum(arrived, axis=0)
    everyone = lax.all_to_all(jnp.broadcast_to(mine[None], parts.shape), "ctx", 0, 0)
    return everyone.reshape(packed.shape), other


def local(query, key_in, value_in, out_grad, mr_filter, se_filter, gain):
    tok, channels = query.shape
    tokens_all = tok * lax.axis_size("ctx")
    tail = (key_in[-HALO:].astype(F32) * value_in[-HALO:].astype(F32)).astype(BF16)
    gated_halo = shifted(tail, 1)
    taps = mr_filter.astype(F32).T
    front = jnp.pad(jnp.flip(taps, axis=1), ((0, 0), (1, LANES - 1)))
    back = jnp.pad(taps, ((0, 0), (0, LANES)))
    front_table, back_table = tables(front, back)
    se = jnp.pad(se_filter.astype(F32), ((0, 1), (0, 0)))
    gain_row = gain[None, :]
    medium_high, short_high, wide_high, square, inner = early(
        key_in, value_in, query, out_grad, se, gain_row, front_table
    )
    medium_low, short_low, sums = late(
        gated_halo,
        key_in,
        value_in,
        query,
        out_grad,
        se,
        gain_row,
        front_table,
        short_high,
        square,
        inner,
    )
    sums = [sums] + from_peers(sums, "tp")
    wide_low = wide(gated_halo, key_in, value_in, front_table)
    sums, wide_low = lax.optimization_barrier((sums, wide_low))
    head_rows = head(sums, query, out_grad, medium_low, gain_row)
    grad_halo = shifted(head_rows, -1)
    query_grad, medium_grad, packed = grads(
        sums,
        query,
        out_grad,
        medium_low,
        medium_high,
        gain_row,
        short_low,
        short_high,
        wide_low,
        wide_high,
    )
    packed, (key_grad, value_grad) = sum_over_ctx(
        packed, lambda: backward(medium_grad, grad_halo, se, key_in, value_in, back_table)
    )
    mr_grad, se_grad, gain_grad = finish(packed, tokens_all, channels)
    return query_grad, key_grad, value_grad, mr_grad, se_grad, gain_grad[0]


def solution(mesh):
    return jax.shard_map(
        local,
        mesh=mesh,
        in_specs=(
            P("ctx", "tp"),
            P("ctx", "tp"),
            P("ctx", "tp"),
            P("ctx", "tp"),
            P(None, "tp"),
            P(None, "tp"),
            P("tp"),
        ),
        out_specs=(
            P("ctx", "tp"),
            P("ctx", "tp"),
            P("ctx", "tp"),
            P(None, "tp"),
            P(None, "tp"),
            P("tp"),
        ),
        check_vma=False,
    )
```

```python
import functools

import jax
import jax.numpy as jnp
from jax import lax
from jax.experimental import pallas as pl
from jax.experimental.pallas import tpu as pltpu
from jax.sharding import PartitionSpec as P

D = 8192
GROUP = 16
MR_LEN = 128
SE_LEN = 7
EPS = 1e-06

LANES = 128
HALO = 144
S = 32
W = S + MR_LEN
SG = 16
GT = LANES // GROUP
EARLY = S + MR_LEN
F32 = jnp.float32
BF16 = jnp.bfloat16


UNROLL = 8
TAIL_PARTS = 4
VMEM = pl.BlockSpec(memory_space=pltpu.VMEM)


def params(limit=24):
    return pltpu.CompilerParams(vmem_limit_bytes=limit * 1024 * 1024)


def cost(micros):
    return pl.CostEstimate(flops=int(micros * 1e9), bytes_accessed=0, transcendentals=0)


def each_tile(channels, body):
    def step(i, carry):
        for slot in range(UNROLL):
            tile = i * UNROLL + slot
            body(pl.ds(pl.multiple_of(tile * LANES, LANES), LANES), tile, slot)
        return carry

    lax.fori_loop(0, channels // LANES // UNROLL, step, 0)


def of_tile(tile, rows):
    return pl.ds(pl.multiple_of(tile * rows, rows), rows)


def call(body, name, micros, outs, scratch, *args):
    return pl.pallas_call(
        body,
        in_specs=[VMEM] * len(args),
        out_specs=[VMEM] * len(outs),
        out_shape=[jax.ShapeDtypeStruct(shape, dtype) for shape, dtype in outs],
        scratch_shapes=scratch,
        compiler_params=params(),
        cost_estimate=cost(micros),
        name=name,
    )(*args)


def shifted(x, by):
    peers = lax.axis_size("ctx")
    return lax.ppermute(x, "ctx", [(i, i + by) for i in range(peers) if 0 <= i + by < peers])


def group_of_lane(rows):
    return lax.broadcasted_iota(jnp.int32, (rows, LANES), 1) // GROUP


def toeplitz(table, windows):
    results = []
    which = group_of_lane(S)
    for first in range(0, len(windows), 2):
        pair = windows[first : first + 2]
        rhs = jnp.concatenate(pair, axis=1) if len(pair) == 2 else pair[0]
        out = jnp.dot(table, rhs, preferred_element_type=F32)
        for n in range(len(pair)):
            total = out[:S, n * LANES : (n + 1) * LANES]
            for g in range(1, GT):
                part = out[g * S : (g + 1) * S, n * LANES : (n + 1) * LANES]
                total = jnp.where(which == g, part, total)
            results.append(total)
    return results


def table_kernel(taps_ref, front_out, back_out, rows_ref):
    taps = taps_ref[...]
    row_ids = lax.broadcasted_iota(jnp.int32, (MR_LEN, 2 * LANES), 0)
    col_ids = lax.broadcasted_iota(jnp.int32, (MR_LEN, 2 * LANES), 1)
    for n, place in enumerate((MR_LEN - row_ids, row_ids)):
        pick = jnp.where(col_ids == place, 1.0, 0.0).astype(BF16)
        rows_ref[n] = lax.dot_general(taps, pick, (((0,), (0,)), ((), ())), preferred_element_type=F32)

    def one(g, carry):
        for n, target in enumerate((front_out, back_out)):
            rows = rows_ref[n, of_tile(g, GT), :]
            for k in range(GT):
                row = jnp.broadcast_to(rows[k : k + 1, :], (S, 2 * LANES))
                turned = pltpu.roll(row, 0, 1, stride=1, stride_axis=0).astype(BF16)
                target[of_tile(g * GT + k, S), :] = turned
        return carry

    lax.fori_loop(0, taps_ref.shape[1] // GT, one, 0)


def tables(mr_filter):
    groups = mr_filter.shape[1]
    shape = ((groups * S, 2 * LANES), BF16)
    scratch = [pltpu.VMEM((2, groups, 2 * LANES), F32)]
    return call(table_kernel, "filter_tables", 2.4, [shape, shape], scratch, mr_filter)


def short_filter(se_ref, at, gated_ref, first, rows):
    total = jnp.zeros((rows, LANES), F32)
    se = se_ref[:, at].astype(F32)
    for tap in range(SE_LEN):
        total = total + se[tap : tap + 1, :] * gated_ref[first - tap : first - tap + rows, :]
    return total.astype(BF16)


def gate(key_ref, value_ref, rows, at):
    return (key_ref[rows, at].astype(F32) * value_ref[rows, at].astype(F32)).astype(BF16)


def tail_kernel(key_ref, value_ref, tail_out, held_ref, sems):
    tok, channels = key_ref.shape
    width = channels // TAIL_PARTS
    copies = []
    for n in range(TAIL_PARTS):
        at = slice(n * width, (n + 1) * width)
        for m, source in enumerate((key_ref, value_ref)):
            copy = pltpu.make_async_copy(
                source.at[tok - HALO :, at], held_ref.at[m, :, at], sems.at[m, n]
            )
            copy.start()
            copies.append(copy)
    for n in range(TAIL_PARTS):
        copies[2 * n].wait()
        copies[2 * n + 1].wait()
        at = slice(n * width, (n + 1) * width)
        tail_out[:, at] = (held_ref[0, :, at].astype(F32) * held_ref[1, :, at].astype(F32)).astype(BF16)


def tail_rows(key_in, value_in):
    channels = key_in.shape[1]
    anywhere = pl.BlockSpec(memory_space=pltpu.HBM)
    return pl.pallas_call(
        tail_kernel,
        in_specs=[anywhere, anywhere],
        out_specs=VMEM,
        out_shape=jax.ShapeDtypeStruct((HALO, channels), BF16),
        scratch_shapes=[
            pltpu.VMEM((2, HALO, channels), BF16),
            pltpu.SemaphoreType.DMA((2, TAIL_PARTS)),
        ],
        compiler_params=params(63),
        cost_estimate=cost(1.2),
        name="tail_rows",
    )(key_in, value_in)


def early_kernel(
    key_ref,
    value_ref,
    query_ref,
    out_grad_ref,
    se_ref,
    gain_ref,
    table_ref,
    medium_out,
    short_out,
    wide_out,
    square_out,
    inner_out,
    gated_ref,
):
    tok, channels = key_ref.shape
    square_out[...] = jnp.zeros_like(square_out)
    inner_out[...] = jnp.zeros_like(inner_out)

    def body(at, tile, slot):
        wide_ref = gated_ref.at[slot]
        gated = gate(key_ref, value_ref, slice(None), at)
        wide_ref[...] = gated.astype(F32)
        short_out[:S, at] = jnp.zeros((S, LANES), BF16)
        short_out[S:, at] = short_filter(se_ref, at, wide_ref, S, tok - S)
        short_out[16:S, at] = short_filter(se_ref, at, wide_ref, 16, S - 16)
        table = table_ref[of_tile(tile, GT * S), :W]
        first = [t for t in range(EARLY, tok, S)]
        windows = [short_out[t - MR_LEN : t + S, at] for t in first]
        also = [t for t in range(MR_LEN, tok, S)]
        windows += [gated[t - MR_LEN : t + S, :] for t in also]
        parts = toeplitz(table, windows)
        gain = gain_ref[:, at]
        for t, medium in zip(first, parts):
            down = slice(t - EARLY, t - EARLY + S)
            medium_out[down, at] = medium
            mixed = query_ref[t : t + S, at].astype(F32) * medium
            norm_grad = out_grad_ref[t : t + S, at].astype(F32) * gain
            square_out[down, :] += mixed * mixed
            inner_out[down, :] += norm_grad * mixed
        for t, part in zip(also, parts[len(first) :]):
            wide_out[t - MR_LEN : t - MR_LEN + S, at] = part

    each_tile(channels, body)


def early(key_in, value_in, query, out_grad, se, gain, table):
    tok, channels = key_in.shape
    outs = [
        ((tok - EARLY, channels), F32),
        ((tok, channels), BF16),
        ((tok - MR_LEN, channels), F32),
        ((tok - EARLY, LANES), F32),
        ((tok - EARLY, LANES), F32),
    ]
    scratch = [pltpu.VMEM((UNROLL, tok, LANES), F32)]
    return call(early_kernel, "early", 4.2, outs, scratch, key_in, value_in, query, out_grad, se, gain, table)


def window(low_ref, high_ref, b, at):
    if b * S >= EARLY:
        return high_ref[b * S - MR_LEN : b * S + S, at]
    if b == 0:
        return low_ref[:, at]
    return jnp.concatenate([low_ref[S * b :, at], high_ref[S : S * b + S, at]], axis=0)


def late_kernel(
    halo_ref,
    key_ref,
    value_ref,
    query_ref,
    out_grad_ref,
    se_ref,
    gain_ref,
    table_ref,
    high_ref,
    square_in,
    inner_in,
    medium_out,
    low_out,
    sums_out,
    gated_ref,
    square_ref,
    inner_ref,
):
    channels = key_ref.shape[1]
    square_ref[:EARLY, :] = jnp.zeros((EARLY, LANES), F32)
    inner_ref[:EARLY, :] = jnp.zeros((EARLY, LANES), F32)
    square_ref[EARLY:, :] = square_in[...]
    inner_ref[EARLY:, :] = inner_in[...]

    def body(at, tile, slot):
        rows = gated_ref.at[slot]
        rows[:HALO, :] = halo_ref[:, at].astype(F32)
        rows[HALO:, :] = gate(key_ref, value_ref, slice(0, S), at).astype(F32)
        low_out[:, at] = short_filter(se_ref, at, rows, HALO - MR_LEN, MR_LEN + S)
        table = table_ref[of_tile(tile, GT * S), :W]
        windows = [window(low_out, high_ref, b, at) for b in range(EARLY // S)]
        gain = gain_ref[:, at]
        for b, medium in enumerate(toeplitz(table, windows)):
            down = slice(S * b, S * b + S)
            medium_out[down, at] = medium
            mixed = query_ref[down, at].astype(F32) * medium
            norm_grad = out_grad_ref[down, at].astype(F32) * gain
            square_ref[down, :] += mixed * mixed
            inner_ref[down, :] += norm_grad * mixed

    each_tile(channels, body)
    sums_out[0:1, :] = jnp.sum(square_ref[...].T, axis=0, keepdims=True)
    sums_out[1:2, :] = jnp.sum(inner_ref[...].T, axis=0, keepdims=True)


def late(halo, key_in, value_in, query, out_grad, se, gain, table, short_high, square, inner):
    tok, channels = key_in.shape
    outs = [((EARLY, channels), F32), ((MR_LEN + S, channels), BF16), ((2, tok), F32)]
    scratch = [
        pltpu.VMEM((UNROLL, HALO + S, LANES), F32),
        pltpu.VMEM((tok, LANES), F32),
        pltpu.VMEM((tok, LANES), F32),
    ]
    return call(
        late_kernel,
        "late",
        2.9,
        outs,
        scratch,
        halo,
        key_in,
        value_in,
        query,
        out_grad,
        se,
        gain,
        table,
        short_high,
        square,
        inner,
    )


def spread_sums(parts, scale_ref, slope_ref, rows):
    sums = functools.reduce(jnp.add, [part[...] for part in parts])
    square = jnp.broadcast_to(sums[0:1, :], (LANES, sums.shape[1])).T[:rows]
    inner = jnp.broadcast_to(sums[1:2, :], (LANES, sums.shape[1])).T[:rows]
    inv = lax.rsqrt(square / D + EPS)
    scale_ref[...] = inv
    slope_ref[...] = inv * inv * inv * inner / D


def head_kernel(query_ref, out_grad_ref, medium_ref, gain_ref, *rest):
    sums, (head_out, scale_ref, slope_ref) = rest[:-3], rest[-3:]
    spread_sums(sums, scale_ref, slope_ref, HALO)

    def body(at, tile, slot):
        query = query_ref[:HALO, at].astype(F32)
        norm_grad = out_grad_ref[:HALO, at].astype(F32) * gain_ref[:, at]
        mixed = query * medium_ref[:HALO, at]
        mixed_grad = scale_ref[...] * norm_grad - mixed * slope_ref[...]
        head_out[:, at] = (mixed_grad * query).astype(BF16)

    each_tile(query_ref.shape[1], body)


def head(sums, query, out_grad, medium_low, gain):
    outs = [((HALO, query.shape[1]), BF16)]
    scratch = [pltpu.VMEM((HALO, LANES), F32), pltpu.VMEM((HALO, LANES), F32)]
    return call(head_kernel, "head_rows", 0.9, outs, scratch, query, out_grad, medium_low, gain, *sums)[0]


def wide_kernel(halo_ref, key_ref, value_ref, table_ref, wide_out, gated_ref):
    lead = W - HALO

    def body(at, tile, slot):
        rows = gated_ref.at[slot]
        rows[:lead, :] = jnp.zeros((lead, LANES), BF16)
        rows[lead:W, :] = halo_ref[:, at]
        rows[W:, :] = gate(key_ref, value_ref, slice(0, MR_LEN), at)
        windows = [rows[S * b : S * b + W, :] for b in range(MR_LEN // S + 1)]
        for b, part in enumerate(toeplitz(table_ref[of_tile(tile, GT * S), :W], windows)):
            wide_out[S * b : S * b + S, at] = part

    each_tile(key_ref.shape[1], body)


def wide(halo, key_in, value_in, table):
    outs = [((MR_LEN + S, key_in.shape[1]), F32)]
    scratch = [pltpu.VMEM((UNROLL, W + MR_LEN, LANES), BF16)]
    return call(wide_kernel, "wide_gated", 2.0, outs, scratch, halo, key_in, value_in, table)[0]


def grads_kernel(
    query_ref,
    out_grad_ref,
    medium_low_ref,
    medium_high_ref,
    gain_ref,
    short_low_ref,
    short_high_ref,
    wide_low_ref,
    wide_high_ref,
    *rest,
):
    query_grad_out, medium_grad_out, packed_out, scale_ref, slope_ref, cross_ref, wide_ref = rest[-7:]
    tok, channels = query_ref.shape
    spread_sums(rest[:-7], scale_ref, slope_ref, tok)
    blocks = tok // SG
    side = GT * SG

    def body(at, tile, slot):
        query = query_ref[:, at].astype(F32)
        out_grad = out_grad_ref[:, at].astype(F32)
        medium = jnp.concatenate([medium_low_ref[:, at], medium_high_ref[:, at]], axis=0)
        inv = scale_ref[...]
        norm_grad = out_grad * gain_ref[:, at]
        mixed = query * medium
        mixed_grad = inv * norm_grad - mixed * slope_ref[...]
        query_grad_out[:, at] = (mixed_grad * medium).astype(BF16)
        medium_grad = (mixed_grad * query).astype(BF16)
        medium_grad_out[:, at] = medium_grad
        gain_row = jnp.sum(out_grad * mixed * inv, axis=0, keepdims=True)
        wide_grad = medium_grad.astype(F32)
        rows = wide_ref.at[slot]
        rows[: MR_LEN + S, :] = wide_low_ref[:, at]
        rows[MR_LEN + S :, :] = wide_high_ref[:, at]
        lines = [
            jnp.sum(wide_grad * rows[S - tap : S - tap + tok, :], axis=0, keepdims=True)
            for tap in range(SE_LEN)
        ]
        lhs_rows = jnp.concatenate([medium_grad[SG * b : SG * b + SG, :] for b in range(blocks)], axis=1)
        which = lax.broadcasted_iota(jnp.int32, lhs_rows.shape, 1) % LANES // GROUP
        lhs = jnp.concatenate(
            [jnp.where(which == g, lhs_rows, jnp.zeros_like(lhs_rows)) for g in range(GT)], axis=0
        )
        short = jnp.concatenate([short_low_ref[:, at], short_high_ref[S:, at]], axis=0)
        rhs = jnp.concatenate([short[SG * b : SG * b + SG + MR_LEN, :] for b in range(blocks)], axis=1)
        cross = lax.dot_general(lhs, rhs, (((1,), (1,)), ((), ())), preferred_element_type=F32)
        held = cross_ref.at[slot]
        held[:side, :] = cross[:, :LANES]
        held[side:, :SG] = cross[:, LANES:]
        total = jnp.zeros((GT, 2 * LANES), F32)
        for s in range(SG):
            part = jnp.concatenate(
                [held[pl.ds(m * side + s, GT, stride=SG), :] for m in range(2)], axis=1
            )
            total = total + pltpu.roll(part, 2 * LANES - 1 - s, 1)
        packed_out[of_tile(tile, 2 * GT), :] = jnp.concatenate(
            [total[:, :LANES]] + lines + [gain_row], axis=0
        )

    each_tile(channels, body)


def grads(sums, query, out_grad, medium_low, medium_high, gain, short_low, short_high, wide_low, wide_high):
    tok, channels = query.shape
    outs = [
        ((tok, channels), BF16),
        ((tok, channels), BF16),
        ((2 * GT * channels // LANES, LANES), F32),
    ]
    scratch = [
        pltpu.VMEM((tok, LANES), F32),
        pltpu.VMEM((tok, LANES), F32),
        pltpu.VMEM((UNROLL, 2 * GT * SG, LANES), F32),
        pltpu.VMEM((UNROLL, tok + S, LANES), F32),
    ]
    return call(
        grads_kernel,
        "gradients",
        6.6,
        outs,
        scratch,
        query,
        out_grad,
        medium_low,
        medium_high,
        gain,
        short_low,
        short_high,
        wide_low,
        wide_high,
        *sums,
    )


def backward_kernel(
    grad_ref, halo_ref, se_ref, key_ref, value_ref, table_ref, key_out, value_out, ext_ref, short_ref
):
    tok = key_ref.shape[0]

    def body(at, tile, slot):
        ext = ext_ref.at[slot]
        short = short_ref.at[slot]
        ext[:tok, :] = grad_ref[:, at]
        ext[tok : tok + HALO, :] = halo_ref[:, at]
        ext[tok + HALO :, :] = jnp.zeros((W - HALO, LANES), BF16)
        windows = [ext[S * b : S * b + W, :] for b in range(tok // S + 1)]
        for b, part in enumerate(toeplitz(table_ref[of_tile(tile, GT * S), :W], windows)):
            short[S * b : S * b + S, :] = part
        total = jnp.zeros((tok, LANES), F32)
        se = se_ref[:, at].astype(F32)
        for tap in range(SE_LEN):
            total = total + se[tap : tap + 1, :] * short[tap : tap + tok, :]
        key_out[:, at] = (total * value_ref[:, at].astype(F32)).astype(BF16)
        value_out[:, at] = (total * key_ref[:, at].astype(F32)).astype(BF16)

    each_tile(key_ref.shape[1], body)


def backward(medium_grad, halo, se, key_in, value_in, table):
    tok, channels = key_in.shape
    outs = [((tok, channels), BF16), ((tok, channels), BF16)]
    scratch = [
        pltpu.VMEM((UNROLL, tok + W, LANES), BF16),
        pltpu.VMEM((UNROLL, tok + S, LANES), F32),
    ]
    return call(backward_kernel, "backward", 5.4, outs, scratch, medium_grad, halo, se, key_in, value_in, table)


def finish_kernel(tokens, low_ref, high_ref, mr_out, se_out, gain_out):
    packed = jnp.concatenate([low_ref[...], high_ref[...]], axis=0)
    tiles = packed.shape[0] // (2 * GT)
    rows = jnp.concatenate([packed[2 * GT * i : 2 * GT * i + GT, :] for i in range(tiles)], axis=0)
    row_ids = lax.broadcasted_iota(jnp.int32, (MR_LEN, MR_LEN), 0)
    col_ids = lax.broadcasted_iota(jnp.int32, (MR_LEN, MR_LEN), 1)
    flip = jnp.where(row_ids + col_ids == MR_LEN - 1, 1.0, 0.0).astype(F32)
    mr_out[...] = lax.dot_general(
        flip, rows, (((1,), (1,)), ((), ())), preferred_element_type=F32, precision=lax.Precision.HIGHEST
    ) * (1.0 / (tokens * GROUP) ** 0.5)
    for i in range(tiles):
        at = slice(i * LANES, (i + 1) * LANES)
        low = 2 * GT * i + GT
        se_out[:, at] = packed[low : low + SE_LEN, :] * (1.0 / tokens**0.5)
        gain_out[:, at] = packed[low + SE_LEN : low + SE_LEN + 1, :] * (1.0 / tokens**0.5)


def finish(low, high, tokens, channels):
    return pl.pallas_call(
        functools.partial(finish_kernel, tokens),
        out_shape=[
            jax.ShapeDtypeStruct((MR_LEN, channels // GROUP), F32),
            jax.ShapeDtypeStruct((SE_LEN, channels), F32),
            jax.ShapeDtypeStruct((1, channels), F32),
        ],
        compiler_params=params(),
        cost_estimate=cost(0.9),
        name="finish",
    )(low, high)


def from_peers(x, axis):
    peers = lax.axis_size(axis)
    return [lax.ppermute(x, axis, [(i, (i + k) % peers) for i in range(peers)]) for k in range(1, peers)]


def sum_over_ctx(packed):
    peers = lax.axis_size("ctx")
    half, lanes = packed.shape[0] // 2, packed.shape[1]
    swap = [(i, i ^ 1) for i in range(peers)]
    side = lax.axis_index("ctx") % 2
    pair = packed + lax.ppermute(packed, "ctx", swap)
    groups = [list(range(k, peers, 2)) for k in range(2)]
    exchange = lambda x: lax.all_to_all(x, "ctx", 0, 0, axis_index_groups=groups)
    parts = lax.dynamic_slice_in_dim(pair, side * half, half).reshape(peers // 2, 2 * half // peers, lanes)
    mine = jnp.sum(exchange(parts), axis=0)
    own = exchange(jnp.broadcast_to(mine[None], parts.shape)).reshape(half, lanes)
    other = lax.ppermute(own, "ctx", swap)
    return jnp.where(side == 0, own, other), jnp.where(side == 0, other, own)


def local(query, key_in, value_in, out_grad, mr_filter, se_filter, gain):
    tok, channels = query.shape
    tokens_all = tok * lax.axis_size("ctx")
    gated_halo = shifted(tail_rows(key_in, value_in), 1)
    front_table, back_table = tables(mr_filter)
    se = se_filter
    gain_row = gain[None, :]
    medium_high, short_high, wide_high, square, inner = early(
        key_in, value_in, query, out_grad, se, gain_row, front_table
    )
    medium_low, short_low, sums = late(
        gated_halo,
        key_in,
        value_in,
        query,
        out_grad,
        se,
        gain_row,
        front_table,
        short_high,
        square,
        inner,
    )
    sums = [sums] + from_peers(sums, "tp")
    wide_low = wide(gated_halo, key_in, value_in, front_table)
    sums, wide_low = lax.optimization_barrier((sums, wide_low))
    head_rows = head(sums, query, out_grad, medium_low, gain_row)
    grad_halo = shifted(head_rows, -1)
    query_grad, medium_grad, packed = grads(
        sums,
        query,
        out_grad,
        medium_low,
        medium_high,
        gain_row,
        short_low,
        short_high,
        wide_low,
        wide_high,
    )
    key_grad, value_grad = backward(medium_grad, grad_halo, se, key_in, value_in, back_table)
    packed, key_grad = lax.optimization_barrier((packed, key_grad))
    low, high = sum_over_ctx(packed)
    mr_grad, se_grad, gain_grad = finish(low, high, tokens_all, channels)
    return query_grad, key_grad, value_grad, mr_grad, se_grad, gain_grad[0]


def solution(mesh):
    return jax.shard_map(
        local,
        mesh=mesh,
        in_specs=(
            P("ctx", "tp"),
            P("ctx", "tp"),
            P("ctx", "tp"),
            P("ctx", "tp"),
            P(None, "tp"),
            P(None, "tp"),
            P("tp"),
        ),
        out_specs=(
            P("ctx", "tp"),
            P("ctx", "tp"),
            P("ctx", "tp"),
            P(None, "tp"),
            P(None, "tp"),
            P("tp"),
        ),
        check_vma=False,
    )
```

```python
import functools

import jax
import jax.numpy as jnp
from jax import lax
from jax.experimental import pallas as pl
from jax.experimental.pallas import tpu as pltpu
from jax.sharding import PartitionSpec as P

D = 8192
GROUP = 16
MR_LEN = 128
SE_LEN = 7
EPS = 1e-06

LANES = 128
HALO = 144
S = 32
W = S + MR_LEN
SG = 16
GT = LANES // GROUP
EARLY = S + MR_LEN
F32 = jnp.float32
BF16 = jnp.bfloat16


UNROLL = 8
TAIL_PARTS = 4
BW = 512
PARTS = 2
NEAR = 8
VMEM = pl.BlockSpec(memory_space=pltpu.VMEM)


def params(limit=24):
    return pltpu.CompilerParams(vmem_limit_bytes=limit * 1024 * 1024)


def cost(micros):
    return pl.CostEstimate(flops=int(micros * 1e9), bytes_accessed=0, transcendentals=0)


def each_tile(channels, body):
    unroll = min(UNROLL, channels // LANES)

    def step(i, carry):
        for slot in range(unroll):
            tile = i * unroll + slot
            body(pl.ds(pl.multiple_of(tile * LANES, LANES), LANES), tile, slot)
        return carry

    lax.fori_loop(0, channels // LANES // unroll, step, 0)


def of_tile(tile, rows):
    return pl.ds(pl.multiple_of(tile * rows, rows), rows)


def call(body, name, micros, outs, scratch, *args):
    return pl.pallas_call(
        body,
        in_specs=[VMEM] * len(args),
        out_specs=[VMEM] * len(outs),
        out_shape=[jax.ShapeDtypeStruct(shape, dtype) for shape, dtype in outs],
        scratch_shapes=scratch,
        compiler_params=params(),
        cost_estimate=cost(micros),
        name=name,
    )(*args)


def shifted(x, by):
    peers = lax.axis_size("ctx")
    return lax.ppermute(x, "ctx", [(i, i + by) for i in range(peers) if 0 <= i + by < peers])


def group_of_lane(rows):
    return lax.broadcasted_iota(jnp.int32, (rows, LANES), 1) // GROUP


def toeplitz(table, windows):
    results = []
    which = group_of_lane(S)
    for first in range(0, len(windows), 2):
        pair = windows[first : first + 2]
        rhs = jnp.concatenate(pair, axis=1) if len(pair) == 2 else pair[0]
        out = jnp.dot(table, rhs, preferred_element_type=F32)
        for n in range(len(pair)):
            total = out[:S, n * LANES : (n + 1) * LANES]
            for g in range(1, GT):
                part = out[g * S : (g + 1) * S, n * LANES : (n + 1) * LANES]
                total = jnp.where(which == g, part, total)
            results.append(total)
    return results


def table_kernel(taps_ref, front_out, back_out, rows_ref):
    taps = taps_ref[...]
    row_ids = lax.broadcasted_iota(jnp.int32, (MR_LEN, 2 * LANES), 0)
    col_ids = lax.broadcasted_iota(jnp.int32, (MR_LEN, 2 * LANES), 1)
    for n, place in enumerate((MR_LEN - row_ids, row_ids)):
        pick = jnp.where(col_ids == place, 1.0, 0.0).astype(BF16)
        rows_ref[n] = lax.dot_general(taps, pick, (((0,), (0,)), ((), ())), preferred_element_type=F32)

    def one(g, carry):
        for n, target in enumerate((front_out, back_out)):
            rows = rows_ref[n, of_tile(g, GT), :]
            for k in range(GT):
                row = jnp.broadcast_to(rows[k : k + 1, :], (S, 2 * LANES))
                turned = pltpu.roll(row, 0, 1, stride=1, stride_axis=0).astype(BF16)
                target[of_tile(g * GT + k, S), :] = turned
        return carry

    lax.fori_loop(0, taps_ref.shape[1] // GT, one, 0)


def tables(mr_filter):
    groups = mr_filter.shape[1]
    shape = ((groups * S, 2 * LANES), BF16)
    scratch = [pltpu.VMEM((2, groups, 2 * LANES), F32)]
    return call(table_kernel, "filter_tables", 2.4, [shape, shape], scratch, mr_filter)


def short_filter(se_ref, at, gated_ref, first, rows):
    total = jnp.zeros((rows, LANES), F32)
    se = se_ref[:, at].astype(F32)
    for tap in range(SE_LEN):
        total = total + se[tap : tap + 1, :] * gated_ref[first - tap : first - tap + rows, :]
    return total.astype(BF16)


def gate(key_ref, value_ref, rows, at):
    return (key_ref[rows, at].astype(F32) * value_ref[rows, at].astype(F32)).astype(BF16)


def tail_kernel(key_ref, value_ref, tail_out, held_ref, sems):
    tok, channels = key_ref.shape
    width = channels // TAIL_PARTS
    copies = []
    for n in range(TAIL_PARTS):
        at = slice(n * width, (n + 1) * width)
        for m, source in enumerate((key_ref, value_ref)):
            copy = pltpu.make_async_copy(
                source.at[tok - HALO :, at], held_ref.at[m, :, at], sems.at[m, n]
            )
            copy.start()
            copies.append(copy)
    for n in range(TAIL_PARTS):
        copies[2 * n].wait()
        copies[2 * n + 1].wait()
        at = slice(n * width, (n + 1) * width)
        tail_out[:, at] = (held_ref[0, :, at].astype(F32) * held_ref[1, :, at].astype(F32)).astype(BF16)


def tail_rows(key_in, value_in):
    channels = key_in.shape[1]
    anywhere = pl.BlockSpec(memory_space=pltpu.HBM)
    return pl.pallas_call(
        tail_kernel,
        in_specs=[anywhere, anywhere],
        out_specs=VMEM,
        out_shape=jax.ShapeDtypeStruct((HALO, channels), BF16),
        scratch_shapes=[
            pltpu.VMEM((2, HALO, channels), BF16),
            pltpu.SemaphoreType.DMA((2, TAIL_PARTS)),
        ],
        compiler_params=params(63),
        cost_estimate=cost(1.2),
        name="tail_rows",
    )(key_in, value_in)


def early_kernel(
    key_ref,
    value_ref,
    query_ref,
    out_grad_ref,
    se_ref,
    gain_ref,
    table_ref,
    medium_out,
    short_out,
    wide_out,
    square_out,
    inner_out,
    gated_ref,
):
    tok, channels = key_ref.shape
    square_out[...] = jnp.zeros_like(square_out)
    inner_out[...] = jnp.zeros_like(inner_out)

    def body(at, tile, slot):
        wide_ref = gated_ref.at[slot]
        gated = gate(key_ref, value_ref, slice(None), at)
        wide_ref[...] = gated.astype(F32)
        short_out[:S, at] = jnp.zeros((S, LANES), BF16)
        short_out[S:, at] = short_filter(se_ref, at, wide_ref, S, tok - S)
        short_out[16:S, at] = short_filter(se_ref, at, wide_ref, 16, S - 16)
        table = table_ref[of_tile(tile, GT * S), :W]
        first = [t for t in range(EARLY, tok, S)]
        windows = [short_out[t - MR_LEN : t + S, at] for t in first]
        also = [t for t in range(MR_LEN, tok, S)]
        windows += [gated[t - MR_LEN : t + S, :] for t in also]
        parts = toeplitz(table, windows)
        gain = gain_ref[:, at]
        for t, medium in zip(first, parts):
            down = slice(t - EARLY, t - EARLY + S)
            medium_out[down, at] = medium
            mixed = query_ref[t : t + S, at].astype(F32) * medium
            norm_grad = out_grad_ref[t : t + S, at].astype(F32) * gain
            square_out[down, :] += mixed * mixed
            inner_out[down, :] += norm_grad * mixed
        for t, part in zip(also, parts[len(first) :]):
            wide_out[t - MR_LEN : t - MR_LEN + S, at] = part

    each_tile(channels, body)


def early(key_in, value_in, query, out_grad, se, gain, table):
    tok, channels = key_in.shape
    outs = [
        ((tok - EARLY, channels), F32),
        ((tok, channels), BF16),
        ((tok - MR_LEN, channels), F32),
        ((tok - EARLY, LANES), F32),
        ((tok - EARLY, LANES), F32),
    ]
    scratch = [pltpu.VMEM((UNROLL, tok, LANES), F32)]
    return call(early_kernel, "early", 4.2, outs, scratch, key_in, value_in, query, out_grad, se, gain, table)


def window(low_ref, high_ref, b, at):
    if b * S >= EARLY:
        return high_ref[b * S - MR_LEN : b * S + S, at]
    if b == 0:
        return low_ref[:, at]
    return jnp.concatenate([low_ref[S * b :, at], high_ref[S : S * b + S, at]], axis=0)


def late_kernel(
    halo_ref,
    key_ref,
    value_ref,
    query_ref,
    out_grad_ref,
    se_ref,
    gain_ref,
    table_ref,
    high_ref,
    square_in,
    inner_in,
    medium_out,
    low_out,
    sums_out,
    gated_ref,
    square_ref,
    inner_ref,
):
    channels = key_ref.shape[1]
    square_ref[:EARLY, :] = jnp.zeros((EARLY, LANES), F32)
    inner_ref[:EARLY, :] = jnp.zeros((EARLY, LANES), F32)
    square_ref[EARLY:, :] = square_in[...]
    inner_ref[EARLY:, :] = inner_in[...]

    def body(at, tile, slot):
        rows = gated_ref.at[slot]
        rows[:HALO, :] = halo_ref[:, at].astype(F32)
        rows[HALO:, :] = gate(key_ref, value_ref, slice(0, S), at).astype(F32)
        low_out[:, at] = short_filter(se_ref, at, rows, HALO - MR_LEN, MR_LEN + S)
        table = table_ref[of_tile(tile, GT * S), :W]
        windows = [window(low_out, high_ref, b, at) for b in range(EARLY // S)]
        gain = gain_ref[:, at]
        for b, medium in enumerate(toeplitz(table, windows)):
            down = slice(S * b, S * b + S)
            medium_out[down, at] = medium
            mixed = query_ref[down, at].astype(F32) * medium
            norm_grad = out_grad_ref[down, at].astype(F32) * gain
            square_ref[down, :] += mixed * mixed
            inner_ref[down, :] += norm_grad * mixed

    each_tile(channels, body)
    sums_out[0:1, :] = jnp.sum(square_ref[...].T, axis=0, keepdims=True)
    sums_out[1:2, :] = jnp.sum(inner_ref[...].T, axis=0, keepdims=True)


def late(halo, key_in, value_in, query, out_grad, se, gain, table, short_high, square, inner):
    tok, channels = key_in.shape
    outs = [((EARLY, channels), F32), ((MR_LEN + S, channels), BF16), ((2, tok), F32)]
    scratch = [
        pltpu.VMEM((UNROLL, HALO + S, LANES), F32),
        pltpu.VMEM((tok, LANES), F32),
        pltpu.VMEM((tok, LANES), F32),
    ]
    return call(
        late_kernel,
        "late",
        2.9,
        outs,
        scratch,
        halo,
        key_in,
        value_in,
        query,
        out_grad,
        se,
        gain,
        table,
        short_high,
        square,
        inner,
    )


def spread_sums(parts, scale_ref, slope_ref, rows):
    sums = functools.reduce(jnp.add, [part[...] for part in parts])
    square = jnp.broadcast_to(sums[0:1, :], (LANES, sums.shape[1])).T[:rows]
    inner = jnp.broadcast_to(sums[1:2, :], (LANES, sums.shape[1])).T[:rows]
    inv = lax.rsqrt(square / D + EPS)
    scale_ref[...] = inv
    slope_ref[...] = inv * inv * inv * inner / D


def head_kernel(query_ref, out_grad_ref, medium_ref, gain_ref, *rest):
    sums, (head_out, scale_ref, slope_ref) = rest[:-3], rest[-3:]
    spread_sums(sums, scale_ref, slope_ref, HALO)

    def body(at, tile, slot):
        query = query_ref[:HALO, at].astype(F32)
        norm_grad = out_grad_ref[:HALO, at].astype(F32) * gain_ref[:, at]
        mixed = query * medium_ref[:HALO, at]
        mixed_grad = scale_ref[...] * norm_grad - mixed * slope_ref[...]
        head_out[:, at] = (mixed_grad * query).astype(BF16)

    each_tile(query_ref.shape[1], body)


def head(sums, query, out_grad, medium_low, gain):
    outs = [((HALO, query.shape[1]), BF16)]
    scratch = [pltpu.VMEM((HALO, LANES), F32), pltpu.VMEM((HALO, LANES), F32)]
    return call(head_kernel, "head_rows", 0.9, outs, scratch, query, out_grad, medium_low, gain, *sums)[0]


def wide_kernel(halo_ref, key_ref, value_ref, table_ref, wide_out, gated_ref):
    lead = W - HALO

    def body(at, tile, slot):
        rows = gated_ref.at[slot]
        rows[:lead, :] = jnp.zeros((lead, LANES), BF16)
        rows[lead:W, :] = halo_ref[:, at]
        rows[W:, :] = gate(key_ref, value_ref, slice(0, MR_LEN), at)
        windows = [rows[S * b : S * b + W, :] for b in range(MR_LEN // S + 1)]
        for b, part in enumerate(toeplitz(table_ref[of_tile(tile, GT * S), :W], windows)):
            wide_out[S * b : S * b + S, at] = part

    each_tile(key_ref.shape[1], body)


def wide(halo, key_in, value_in, table):
    outs = [((MR_LEN + S, key_in.shape[1]), F32)]
    scratch = [pltpu.VMEM((UNROLL, W + MR_LEN, LANES), BF16)]
    return call(wide_kernel, "wide_gated", 2.0, outs, scratch, halo, key_in, value_in, table)[0]


def grads_kernel(
    query_ref,
    out_grad_ref,
    medium_low_ref,
    medium_high_ref,
    gain_ref,
    short_low_ref,
    short_high_ref,
    wide_low_ref,
    wide_high_ref,
    *rest,
):
    query_grad_out, medium_grad_out, packed_out, scale_ref, slope_ref, cross_ref, wide_ref = rest[-7:]
    tok, channels = query_ref.shape
    spread_sums(rest[:-7], scale_ref, slope_ref, tok)
    blocks = tok // SG
    side = GT * SG

    def body(at, tile, slot):
        query = query_ref[:, at].astype(F32)
        out_grad = out_grad_ref[:, at].astype(F32)
        medium = jnp.concatenate([medium_low_ref[:, at], medium_high_ref[:, at]], axis=0)
        inv = scale_ref[...]
        norm_grad = out_grad * gain_ref[:, at]
        mixed = query * medium
        mixed_grad = inv * norm_grad - mixed * slope_ref[...]
        query_grad_out[:, at] = (mixed_grad * medium).astype(BF16)
        medium_grad = (mixed_grad * query).astype(BF16)
        medium_grad_out[:, at] = medium_grad
        gain_row = jnp.sum(out_grad * mixed * inv, axis=0, keepdims=True)
        wide_grad = medium_grad.astype(F32)
        rows = wide_ref.at[slot]
        rows[: MR_LEN + S, :] = wide_low_ref[:, at]
        rows[MR_LEN + S :, :] = wide_high_ref[:, at]
        lines = [
            jnp.sum(wide_grad * rows[S - tap : S - tap + tok, :], axis=0, keepdims=True)
            for tap in range(SE_LEN)
        ]
        lhs_rows = jnp.concatenate([medium_grad[SG * b : SG * b + SG, :] for b in range(blocks)], axis=1)
        which = lax.broadcasted_iota(jnp.int32, lhs_rows.shape, 1) % LANES // GROUP
        lhs = jnp.concatenate(
            [jnp.where(which == g, lhs_rows, jnp.zeros_like(lhs_rows)) for g in range(GT)], axis=0
        )
        short = jnp.concatenate([short_low_ref[:, at], short_high_ref[S:, at]], axis=0)
        rhs = jnp.concatenate([short[SG * b : SG * b + SG + MR_LEN, :] for b in range(blocks)], axis=1)
        cross = lax.dot_general(lhs, rhs, (((1,), (1,)), ((), ())), preferred_element_type=F32)
        held = cross_ref.at[slot]
        held[:side, :] = cross[:, :LANES]
        held[side:, :SG] = cross[:, LANES:]
        total = jnp.zeros((GT, 2 * LANES), F32)
        for s in range(SG):
            part = jnp.concatenate(
                [held[pl.ds(m * side + s, GT, stride=SG), :] for m in range(2)], axis=1
            )
            total = total + pltpu.roll(part, 2 * LANES - 1 - s, 1)
        packed_out[of_tile(tile, 2 * GT), :] = jnp.concatenate(
            [total[:, :LANES]] + lines + [gain_row], axis=0
        )

    each_tile(channels, body)


def grads(sums, query, out_grad, medium_low, medium_high, gain, short_low, short_high, wide_low, wide_high):
    tok, channels = query.shape
    outs = [
        ((tok, channels), BF16),
        ((tok, channels), BF16),
        ((2 * GT * channels // LANES, LANES), F32),
    ]
    scratch = [
        pltpu.VMEM((tok, LANES), F32),
        pltpu.VMEM((tok, LANES), F32),
        pltpu.VMEM((UNROLL, 2 * GT * SG, LANES), F32),
        pltpu.VMEM((UNROLL, tok + S, LANES), F32),
    ]
    return call(
        grads_kernel,
        "gradients",
        6.6,
        outs,
        scratch,
        query,
        out_grad,
        medium_low,
        medium_high,
        gain,
        short_low,
        short_high,
        wide_low,
        wide_high,
        *sums,
    )


def backward_kernel(grad_ref, halo_ref, se_ref, key_ref, value_ref, table_ref, *rest):
    key_out, value_out, ext_ref, short_ref = rest[-4:]
    tok = key_ref.shape[0]

    def body(at, tile, slot):
        ext = ext_ref.at[slot]
        short = short_ref.at[slot]
        ext[:tok, :] = grad_ref[:, at]
        ext[tok : tok + HALO, :] = halo_ref[:, at]
        ext[tok + HALO :, :] = jnp.zeros((W - HALO, LANES), BF16)
        windows = [ext[S * b : S * b + W, :] for b in range(tok // S + 1)]
        for b, part in enumerate(toeplitz(table_ref[of_tile(tile, GT * S), :W], windows)):
            short[S * b : S * b + S, :] = part
        total = jnp.zeros((tok, LANES), F32)
        se = se_ref[:, at].astype(F32)
        for tap in range(SE_LEN):
            total = total + se[tap : tap + 1, :] * short[tap : tap + tok, :]
        key_out[:, at] = (total * value_ref[:, at].astype(F32)).astype(BF16)
        value_out[:, at] = (total * key_ref[:, at].astype(F32)).astype(BF16)

    each_tile(key_ref.shape[1], body)


def backward(medium_grad, halo, se, key_in, value_in, table, part, done=()):
    tok, channels = key_in.shape
    steps = channels // BW // PARTS
    first = part * steps
    col = lambda rows: pl.BlockSpec((rows, BW), lambda i: (0, first + i))
    tiles = BW // LANES
    shape = jax.ShapeDtypeStruct((tok, channels), BF16)
    return pl.pallas_call(
        backward_kernel,
        grid=(steps,),
        in_specs=[
            col(tok),
            col(HALO),
            col(SE_LEN),
            col(tok),
            col(tok),
            pl.BlockSpec((tiles * GT * S, 2 * LANES), lambda i: (first + i, 0)),
        ]
        + [pl.BlockSpec(memory_space=pltpu.HBM)] * len(done),
        out_specs=[col(tok), col(tok)],
        out_shape=[shape, shape],
        scratch_shapes=[
            pltpu.VMEM((tiles, tok + W, LANES), BF16),
            pltpu.VMEM((tiles, tok + S, LANES), F32),
        ],
        input_output_aliases={6 + n: n for n in range(len(done))},
        compiler_params=params(62),
        cost_estimate=cost(3.5),
        name="backward",
    )(medium_grad, halo, se, key_in, value_in, table, *done)


def finish_kernel(tokens, packed_ref, mr_out, se_out, gain_out):
    packed = packed_ref[...]
    tiles = packed.shape[0] // (2 * GT)
    rows = jnp.concatenate([packed[2 * GT * i : 2 * GT * i + GT, :] for i in range(tiles)], axis=0)
    row_ids = lax.broadcasted_iota(jnp.int32, (MR_LEN, MR_LEN), 0)
    col_ids = lax.broadcasted_iota(jnp.int32, (MR_LEN, MR_LEN), 1)
    flip = jnp.where(row_ids + col_ids == MR_LEN - 1, 1.0, 0.0).astype(F32)
    mr_out[...] = lax.dot_general(
        flip, rows, (((1,), (1,)), ((), ())), preferred_element_type=F32, precision=lax.Precision.HIGHEST
    ) * (1.0 / (tokens * GROUP) ** 0.5)
    for i in range(tiles):
        at = slice(i * LANES, (i + 1) * LANES)
        low = 2 * GT * i + GT
        se_out[:, at] = packed[low : low + SE_LEN, :] * (1.0 / tokens**0.5)
        gain_out[:, at] = packed[low + SE_LEN : low + SE_LEN + 1, :] * (1.0 / tokens**0.5)


def finish(packed, tokens, channels):
    return pl.pallas_call(
        functools.partial(finish_kernel, tokens),
        out_shape=[
            jax.ShapeDtypeStruct((MR_LEN, channels // GROUP), F32),
            jax.ShapeDtypeStruct((SE_LEN, channels), F32),
            jax.ShapeDtypeStruct((1, channels), F32),
        ],
        compiler_params=params(),
        cost_estimate=cost(0.9),
        name="finish",
    )(packed)


def add_kernel(one_ref, other_ref, total_out):
    total_out[...] = one_ref[...] + other_ref[...]


def pair_up(x, partner):
    return lax.ppermute(x, "tp", [(i, partner(i)) for i in range(lax.axis_size("tp"))])


def spread(x, groups):
    everyone = jnp.broadcast_to(x[None], (len(groups[0]),) + x.shape)
    return lax.all_to_all(everyone, "ctx", 0, 0, axis_index_groups=groups)


def sum_over_ctx(packed, beside):
    peers = lax.axis_size("ctx")
    near = [list(range(first, first + NEAR)) for first in range(0, peers, NEAR)]
    far = [list(range(first, peers, NEAR)) for first in range(NEAR)]
    parts = packed.reshape(NEAR, packed.shape[0] // NEAR, packed.shape[1])
    arrived = lax.all_to_all(parts, "ctx", 0, 0, axis_index_groups=near)
    arrived, done = lax.optimization_barrier((arrived, beside(0)))
    mine, done = lax.optimization_barrier((jnp.sum(arrived, axis=0), done))
    arrived = spread(mine, far)
    arrived, done = lax.optimization_barrier((arrived, beside(1, done)))
    return spread(jnp.sum(arrived, axis=0), near).reshape(packed.shape), done


def local(query, key_in, value_in, out_grad, mr_filter, se_filter, gain):
    tok, channels = query.shape
    tokens_all = tok * lax.axis_size("ctx")
    gated_halo = shifted(tail_rows(key_in, value_in), 1)
    front_table, back_table = tables(mr_filter)
    se = se_filter
    gain_row = gain[None, :]
    medium_high, short_high, wide_high, square, inner = early(
        key_in, value_in, query, out_grad, se, gain_row, front_table
    )
    medium_low, short_low, sums = late(
        gated_halo,
        key_in,
        value_in,
        query,
        out_grad,
        se,
        gain_row,
        front_table,
        short_high,
        square,
        inner,
    )
    sums = call(add_kernel, "pair_sums", 0.2, [((2, tok), F32)], [], sums, pair_up(sums, lambda i: i ^ 1))[0]
    sums = [sums, pair_up(sums, lambda i: lax.axis_size("tp") - 1 - i)]
    wide_low = wide(gated_halo, key_in, value_in, front_table)
    sums, wide_low = lax.optimization_barrier((sums, wide_low))
    head_rows = head(sums, query, out_grad, medium_low, gain_row)
    grad_halo = shifted(head_rows, -1)
    query_grad, medium_grad, packed = grads(
        sums,
        query,
        out_grad,
        medium_low,
        medium_high,
        gain_row,
        short_low,
        short_high,
        wide_low,
        wide_high,
    )
    packed, (key_grad, value_grad) = sum_over_ctx(
        packed, functools.partial(backward, medium_grad, grad_halo, se, key_in, value_in, back_table)
    )
    mr_grad, se_grad, gain_grad = finish(packed, tokens_all, channels)
    return query_grad, key_grad, value_grad, mr_grad, se_grad, gain_grad[0]


def solution(mesh):
    return jax.shard_map(
        local,
        mesh=mesh,
        in_specs=(
            P("ctx", "tp"),
            P("ctx", "tp"),
            P("ctx", "tp"),
            P("ctx", "tp"),
            P(None, "tp"),
            P(None, "tp"),
            P("tp"),
        ),
        out_specs=(
            P("ctx", "tp"),
            P("ctx", "tp"),
            P("ctx", "tp"),
            P(None, "tp"),
            P(None, "tp"),
            P("tp"),
        ),
        check_vma=False,
    )
```

```python
import functools

import jax
import jax.numpy as jnp
from jax import lax
from jax.experimental import pallas as pl
from jax.experimental.pallas import tpu as pltpu
from jax.sharding import PartitionSpec as P

D = 8192
GROUP = 16
MR_LEN = 128
SE_LEN = 7
EPS = 1e-06

LANES = 128
HALO = 144
S = 32
W = S + MR_LEN
SG = 16
GT = LANES // GROUP
EARLY = S + MR_LEN
F32 = jnp.float32
BF16 = jnp.bfloat16


UNROLL = 8
TAIL_PARTS = 4
BW = 512
PARTS = 2
NEAR = 8
VMEM = pl.BlockSpec(memory_space=pltpu.VMEM)
HBM = pl.BlockSpec(memory_space=pltpu.HBM)


def params(limit=24):
    return pltpu.CompilerParams(vmem_limit_bytes=int(limit * 1024 * 1024))


def cost(micros):
    return pl.CostEstimate(flops=int(micros * 1e9), bytes_accessed=0, transcendentals=0)


def each_tile(channels, body, after=None):
    unroll = min(UNROLL, channels // LANES)

    def step(i, carry):
        for slot in range(unroll):
            tile = i * unroll + slot
            body(pl.ds(pl.multiple_of(tile * LANES, LANES), LANES), tile, slot)
        if after is not None:
            after(i)
        return carry

    lax.fori_loop(0, channels // LANES // unroll, step, 0)


def of_tile(tile, rows):
    return pl.ds(pl.multiple_of(tile * rows, rows), rows)


def call(body, name, micros, outs, scratch, *args, out_specs=None):
    return pl.pallas_call(
        body,
        in_specs=[VMEM] * len(args),
        out_specs=out_specs or [VMEM] * len(outs),
        out_shape=[
            (pltpu.HBM if out_specs and spec is HBM else jax.ShapeDtypeStruct)(shape, dtype)
            for (shape, dtype), spec in zip(outs, out_specs or [VMEM] * len(outs))
        ],
        scratch_shapes=scratch,
        compiler_params=params(),
        cost_estimate=cost(micros),
        name=name,
    )(*args)


def shifted(x, by):
    peers = lax.axis_size("ctx")
    return lax.ppermute(x, "ctx", [(i, i + by) for i in range(peers) if 0 <= i + by < peers])


def group_of_lane(rows):
    return lax.broadcasted_iota(jnp.int32, (rows, LANES), 1) // GROUP


def toeplitz(table, windows):
    results = []
    which = group_of_lane(S)
    for first in range(0, len(windows), 2):
        pair = windows[first : first + 2]
        rhs = jnp.concatenate(pair, axis=1) if len(pair) == 2 else pair[0]
        out = jnp.dot(table, rhs, preferred_element_type=F32)
        for n in range(len(pair)):
            total = out[:S, n * LANES : (n + 1) * LANES]
            for g in range(1, GT):
                part = out[g * S : (g + 1) * S, n * LANES : (n + 1) * LANES]
                total = jnp.where(which == g, part, total)
            results.append(total)
    return results


def table_kernel(taps_ref, front_out, back_out, rows_ref, back_ref, sem):
    taps = taps_ref[...]
    row_ids = lax.broadcasted_iota(jnp.int32, (MR_LEN, 2 * LANES), 0)
    col_ids = lax.broadcasted_iota(jnp.int32, (MR_LEN, 2 * LANES), 1)
    for n, place in enumerate((MR_LEN - row_ids, row_ids)):
        pick = jnp.where(col_ids == place, 1.0, 0.0).astype(BF16)
        rows_ref[n] = lax.dot_general(taps, pick, (((0,), (0,)), ((), ())), preferred_element_type=F32)

    def fill(n, target):
        def one(g, carry):
            rows = rows_ref[n, of_tile(g, GT), :]
            for k in range(GT):
                row = jnp.broadcast_to(rows[k : k + 1, :], (S, 2 * LANES))
                turned = pltpu.roll(row, 0, 1, stride=1, stride_axis=0).astype(BF16)
                target[of_tile(g * GT + k, S), :] = turned
            return carry

        lax.fori_loop(0, taps_ref.shape[1] // GT, one, 0)

    fill(1, back_ref)
    copy = pltpu.make_async_copy(back_ref, back_out, sem)
    copy.start()
    fill(0, front_out)
    copy.wait()


def tables(mr_filter):
    groups = mr_filter.shape[1]
    shape = ((groups * S, 2 * LANES), BF16)
    scratch = [
        pltpu.VMEM((2, groups, 2 * LANES), F32),
        pltpu.VMEM((groups * S, 2 * LANES), BF16),
        pltpu.SemaphoreType.DMA,
    ]
    specs = [VMEM, HBM]
    return call(table_kernel, "filter_tables", 2.4, [shape, shape], scratch, mr_filter, out_specs=specs)


def short_filter(se_ref, at, gated_ref, first, rows):
    total = jnp.zeros((rows, LANES), F32)
    se = se_ref[:, at].astype(F32)
    for tap in range(SE_LEN):
        total = total + se[tap : tap + 1, :] * gated_ref[first - tap : first - tap + rows, :]
    return total.astype(BF16)


def gate(key_ref, value_ref, rows, at):
    return (key_ref[rows, at].astype(F32) * value_ref[rows, at].astype(F32)).astype(BF16)


def tail_kernel(key_ref, value_ref, tail_out, held_ref, sems):
    tok, channels = key_ref.shape
    width = channels // TAIL_PARTS
    copies = []
    for n in range(TAIL_PARTS):
        at = slice(n * width, (n + 1) * width)
        for m, source in enumerate((key_ref, value_ref)):
            copy = pltpu.make_async_copy(
                source.at[tok - HALO :, at], held_ref.at[m, :, at], sems.at[m, n]
            )
            copy.start()
            copies.append(copy)
    for n in range(TAIL_PARTS):
        copies[2 * n].wait()
        copies[2 * n + 1].wait()
        at = slice(n * width, (n + 1) * width)
        tail_out[:, at] = (held_ref[0, :, at].astype(F32) * held_ref[1, :, at].astype(F32)).astype(BF16)


def tail_rows(key_in, value_in):
    channels = key_in.shape[1]
    return pl.pallas_call(
        tail_kernel,
        in_specs=[HBM, HBM],
        out_specs=VMEM,
        out_shape=pltpu.VMEM((HALO, channels), BF16),
        scratch_shapes=[
            pltpu.VMEM((2, HALO, channels), BF16),
            pltpu.SemaphoreType.DMA((2, TAIL_PARTS)),
        ],
        compiler_params=params(62),
        cost_estimate=cost(1.2),
        name="tail_rows",
    )(key_in, value_in)


def early_kernel(
    key_ref,
    value_ref,
    query_ref,
    out_grad_ref,
    se_ref,
    gain_ref,
    table_ref,
    medium_out,
    short_out,
    wide_out,
    square_out,
    inner_out,
    gated_ref,
):
    tok, channels = key_ref.shape
    square_out[...] = jnp.zeros_like(square_out)
    inner_out[...] = jnp.zeros_like(inner_out)

    def body(at, tile, slot):
        wide_ref = gated_ref.at[slot]
        gated = gate(key_ref, value_ref, slice(None), at)
        wide_ref[...] = gated.astype(F32)
        short_out[:S, at] = jnp.zeros((S, LANES), BF16)
        short_out[S:, at] = short_filter(se_ref, at, wide_ref, S, tok - S)
        short_out[16:S, at] = short_filter(se_ref, at, wide_ref, 16, S - 16)
        table = table_ref[of_tile(tile, GT * S), :W]
        first = [t for t in range(EARLY, tok, S)]
        windows = [short_out[t - MR_LEN : t + S, at] for t in first]
        also = [t for t in range(MR_LEN, tok, S)]
        windows += [gated[t - MR_LEN : t + S, :] for t in also]
        parts = toeplitz(table, windows)
        gain = gain_ref[:, at]
        for t, medium in zip(first, parts):
            down = slice(t - EARLY, t - EARLY + S)
            medium_out[down, at] = medium
            mixed = query_ref[t : t + S, at].astype(F32) * medium
            norm_grad = out_grad_ref[t : t + S, at].astype(F32) * gain
            square_out[down, :] += mixed * mixed
            inner_out[down, :] += norm_grad * mixed
        for t, part in zip(also, parts[len(first) :]):
            wide_out[t - MR_LEN : t - MR_LEN + S, at] = part

    each_tile(channels, body)


def early(key_in, value_in, query, out_grad, se, gain, table):
    tok, channels = key_in.shape
    outs = [
        ((tok - EARLY, channels), F32),
        ((tok, channels), BF16),
        ((tok - MR_LEN, channels), F32),
        ((tok - EARLY, LANES), F32),
        ((tok - EARLY, LANES), F32),
    ]
    scratch = [pltpu.VMEM((UNROLL, tok, LANES), F32)]
    return call(early_kernel, "early", 4.2, outs, scratch, key_in, value_in, query, out_grad, se, gain, table)


def window(low_ref, high_ref, b, at):
    if b * S >= EARLY:
        return high_ref[b * S - MR_LEN : b * S + S, at]
    if b == 0:
        return low_ref[:, at]
    return jnp.concatenate([low_ref[S * b :, at], high_ref[S : S * b + S, at]], axis=0)


def late_kernel(
    halo_ref,
    key_ref,
    value_ref,
    query_ref,
    out_grad_ref,
    se_ref,
    gain_ref,
    table_ref,
    high_ref,
    square_in,
    inner_in,
    medium_out,
    low_out,
    sums_out,
    gated_ref,
    square_ref,
    inner_ref,
):
    channels = key_ref.shape[1]
    square_ref[:EARLY, :] = jnp.zeros((EARLY, LANES), F32)
    inner_ref[:EARLY, :] = jnp.zeros((EARLY, LANES), F32)
    square_ref[EARLY:, :] = square_in[...]
    inner_ref[EARLY:, :] = inner_in[...]

    def body(at, tile, slot):
        rows = gated_ref.at[slot]
        rows[:HALO, :] = halo_ref[:, at].astype(F32)
        rows[HALO:, :] = gate(key_ref, value_ref, slice(0, S), at).astype(F32)
        low_out[:, at] = short_filter(se_ref, at, rows, HALO - MR_LEN, MR_LEN + S)
        table = table_ref[of_tile(tile, GT * S), :W]
        windows = [window(low_out, high_ref, b, at) for b in range(EARLY // S)]
        gain = gain_ref[:, at]
        for b, medium in enumerate(toeplitz(table, windows)):
            down = slice(S * b, S * b + S)
            medium_out[down, at] = medium
            mixed = query_ref[down, at].astype(F32) * medium
            norm_grad = out_grad_ref[down, at].astype(F32) * gain
            square_ref[down, :] += mixed * mixed
            inner_ref[down, :] += norm_grad * mixed

    each_tile(channels, body)
    sums_out[0:1, :] = jnp.sum(square_ref[...].T, axis=0, keepdims=True)
    sums_out[1:2, :] = jnp.sum(inner_ref[...].T, axis=0, keepdims=True)


def late(halo, key_in, value_in, query, out_grad, se, gain, table, short_high, square, inner):
    tok, channels = key_in.shape
    outs = [((EARLY, channels), F32), ((MR_LEN + S, channels), BF16), ((2, tok), F32)]
    scratch = [
        pltpu.VMEM((UNROLL, HALO + S, LANES), F32),
        pltpu.VMEM((tok, LANES), F32),
        pltpu.VMEM((tok, LANES), F32),
    ]
    return call(
        late_kernel,
        "late",
        2.9,
        outs,
        scratch,
        halo,
        key_in,
        value_in,
        query,
        out_grad,
        se,
        gain,
        table,
        short_high,
        square,
        inner,
    )


def spread_sums(parts, scale_ref, slope_ref, rows):
    sums = functools.reduce(jnp.add, [part[...] for part in parts])
    square = jnp.broadcast_to(sums[0:1, :], (LANES, sums.shape[1])).T[:rows]
    inner = jnp.broadcast_to(sums[1:2, :], (LANES, sums.shape[1])).T[:rows]
    inv = lax.rsqrt(square / D + EPS)
    scale_ref[...] = inv
    slope_ref[...] = inv * inv * inv * inner / D


def head_kernel(query_ref, out_grad_ref, medium_ref, gain_ref, *rest):
    sums, (head_out, scale_ref, slope_ref) = rest[:-3], rest[-3:]
    spread_sums(sums, scale_ref, slope_ref, HALO)

    def body(at, tile, slot):
        query = query_ref[:HALO, at].astype(F32)
        norm_grad = out_grad_ref[:HALO, at].astype(F32) * gain_ref[:, at]
        mixed = query * medium_ref[:HALO, at]
        mixed_grad = scale_ref[...] * norm_grad - mixed * slope_ref[...]
        head_out[:, at] = (mixed_grad * query).astype(BF16)

    each_tile(query_ref.shape[1], body)


def head(sums, query, out_grad, medium_low, gain):
    outs = [((HALO, query.shape[1]), BF16)]
    scratch = [pltpu.VMEM((HALO, LANES), F32), pltpu.VMEM((HALO, LANES), F32)]
    return call(head_kernel, "head_rows", 0.9, outs, scratch, query, out_grad, medium_low, gain, *sums)[0]


def wide_kernel(halo_ref, key_ref, value_ref, table_ref, wide_out, gated_ref):
    lead = W - HALO

    def body(at, tile, slot):
        rows = gated_ref.at[slot]
        rows[:lead, :] = jnp.zeros((lead, LANES), BF16)
        rows[lead:W, :] = halo_ref[:, at]
        rows[W:, :] = gate(key_ref, value_ref, slice(0, MR_LEN), at)
        windows = [rows[S * b : S * b + W, :] for b in range(MR_LEN // S + 1)]
        for b, part in enumerate(toeplitz(table_ref[of_tile(tile, GT * S), :W], windows)):
            wide_out[S * b : S * b + S, at] = part

    each_tile(key_ref.shape[1], body)


def wide(halo, key_in, value_in, table):
    outs = [((MR_LEN + S, key_in.shape[1]), F32)]
    scratch = [pltpu.VMEM((UNROLL, W + MR_LEN, LANES), BF16)]
    return call(wide_kernel, "wide_gated", 2.0, outs, scratch, halo, key_in, value_in, table)[0]


def grads_kernel(
    query_ref,
    out_grad_ref,
    medium_low_ref,
    medium_high_ref,
    gain_ref,
    short_low_ref,
    short_high_ref,
    wide_low_ref,
    wide_high_ref,
    *rest,
):
    *sums, query_grad_out, medium_grad_out, packed_out, scale_ref, slope_ref, cross_ref, wide_ref, held_ref, sems = rest
    tok, channels = query_ref.shape
    spread_sums(sums, scale_ref, slope_ref, tok)
    width = UNROLL * LANES

    def copies(i):
        at = of_tile(i, width)
        return [
            pltpu.make_async_copy(held_ref.at[n, :, at], target.at[:, at], sems.at[n, i])
            for n, target in enumerate((query_grad_out, medium_grad_out))
        ]

    def leave(i):
        for copy in copies(i):
            copy.start()

    blocks = tok // SG
    side = GT * SG

    def body(at, tile, slot):
        query = query_ref[:, at].astype(F32)
        out_grad = out_grad_ref[:, at].astype(F32)
        medium = jnp.concatenate([medium_low_ref[:, at], medium_high_ref[:, at]], axis=0)
        inv = scale_ref[...]
        norm_grad = out_grad * gain_ref[:, at]
        mixed = query * medium
        mixed_grad = inv * norm_grad - mixed * slope_ref[...]
        held_ref[0, :, at] = (mixed_grad * medium).astype(BF16)
        medium_grad = (mixed_grad * query).astype(BF16)
        held_ref[1, :, at] = medium_grad
        gain_row = jnp.sum(out_grad * mixed * inv, axis=0, keepdims=True)
        wide_grad = medium_grad.astype(F32)
        rows = wide_ref.at[slot]
        rows[: MR_LEN + S, :] = wide_low_ref[:, at]
        rows[MR_LEN + S :, :] = wide_high_ref[:, at]
        lines = [
            jnp.sum(wide_grad * rows[S - tap : S - tap + tok, :], axis=0, keepdims=True)
            for tap in range(SE_LEN)
        ]
        lhs_rows = jnp.concatenate([medium_grad[SG * b : SG * b + SG, :] for b in range(blocks)], axis=1)
        which = lax.broadcasted_iota(jnp.int32, lhs_rows.shape, 1) % LANES // GROUP
        lhs = jnp.concatenate(
            [jnp.where(which == g, lhs_rows, jnp.zeros_like(lhs_rows)) for g in range(GT)], axis=0
        )
        short = jnp.concatenate([short_low_ref[:, at], short_high_ref[S:, at]], axis=0)
        rhs = jnp.concatenate([short[SG * b : SG * b + SG + MR_LEN, :] for b in range(blocks)], axis=1)
        cross = lax.dot_general(lhs, rhs, (((1,), (1,)), ((), ())), preferred_element_type=F32)
        held = cross_ref.at[slot]
        held[:side, :] = cross[:, :LANES]
        held[side:, :SG] = cross[:, LANES:]
        total = jnp.zeros((GT, 2 * LANES), F32)
        for s in range(SG):
            part = jnp.concatenate(
                [held[pl.ds(m * side + s, GT, stride=SG), :] for m in range(2)], axis=1
            )
            total = total + pltpu.roll(part, 2 * LANES - 1 - s, 1)
        packed_out[of_tile(tile, 2 * GT), :] = jnp.concatenate(
            [total[:, :LANES]] + lines + [gain_row], axis=0
        )

    each_tile(channels, body, leave)
    for i in range(channels // width):
        for copy in copies(i):
            copy.wait()


def grads(sums, query, out_grad, medium_low, medium_high, gain, short_low, short_high, wide_low, wide_high):
    tok, channels = query.shape
    outs = [
        ((tok, channels), BF16),
        ((tok, channels), BF16),
        ((2 * GT * channels // LANES, LANES), F32),
    ]
    scratch = [
        pltpu.VMEM((tok, LANES), F32),
        pltpu.VMEM((tok, LANES), F32),
        pltpu.VMEM((UNROLL, 2 * GT * SG, LANES), F32),
        pltpu.VMEM((UNROLL, tok + S, LANES), F32),
        pltpu.VMEM((2, tok, channels), BF16),
        pltpu.SemaphoreType.DMA((2, channels // LANES // UNROLL)),
    ]
    return call(
        grads_kernel,
        "gradients",
        6.6,
        outs,
        scratch,
        query,
        out_grad,
        medium_low,
        medium_high,
        gain,
        short_low,
        short_high,
        wide_low,
        wide_high,
        *sums,
        out_specs=[HBM, HBM, VMEM],
    )


def backward_kernel(grad_ref, halo_ref, se_ref, key_ref, value_ref, table_ref, *rest):
    key_out, value_out, ext_ref, short_ref = rest[-4:]
    tok = key_ref.shape[0]

    def body(at, tile, slot):
        ext = ext_ref.at[slot]
        short = short_ref.at[slot]
        ext[:tok, :] = grad_ref[:, at]
        ext[tok : tok + HALO, :] = halo_ref[:, at]
        ext[tok + HALO :, :] = jnp.zeros((W - HALO, LANES), BF16)
        windows = [ext[S * b : S * b + W, :] for b in range(tok // S + 1)]
        for b, part in enumerate(toeplitz(table_ref[of_tile(tile, GT * S), :W], windows)):
            short[S * b : S * b + S, :] = part
        total = jnp.zeros((tok, LANES), F32)
        se = se_ref[:, at].astype(F32)
        for tap in range(SE_LEN):
            total = total + se[tap : tap + 1, :] * short[tap : tap + tok, :]
        key_out[:, at] = (total * value_ref[:, at].astype(F32)).astype(BF16)
        value_out[:, at] = (total * key_ref[:, at].astype(F32)).astype(BF16)

    each_tile(key_ref.shape[1], body)


def backward(medium_grad, halo, se, key_in, value_in, table, part, done=()):
    tok, channels = key_in.shape
    steps = channels // BW // PARTS
    first = part * steps
    col = lambda rows: pl.BlockSpec((rows, BW), lambda i: (0, first + i))
    tiles = BW // LANES
    shape = jax.ShapeDtypeStruct((tok, channels), BF16)
    return pl.pallas_call(
        backward_kernel,
        grid=(steps,),
        in_specs=[
            col(tok),
            col(HALO),
            col(SE_LEN),
            col(tok),
            col(tok),
            pl.BlockSpec((tiles * GT * S, 2 * LANES), lambda i: (first + i, 0)),
        ]
        + [HBM] * len(done),
        out_specs=[col(tok), col(tok)],
        out_shape=[shape, shape],
        scratch_shapes=[
            pltpu.VMEM((tiles, tok + W, LANES), BF16),
            pltpu.VMEM((tiles, tok + S, LANES), F32),
        ],
        input_output_aliases={6 + n: n for n in range(len(done))},
        compiler_params=params(62),
        cost_estimate=cost(3.5),
        name="backward",
    )(medium_grad, halo, se, key_in, value_in, table, *done)


def finish_kernel(tokens, packed_ref, mr_out, se_out, gain_out):
    packed = packed_ref[...]
    tiles = packed.shape[0] // (2 * GT)
    rows = jnp.concatenate([packed[2 * GT * i : 2 * GT * i + GT, :] for i in range(tiles)], axis=0)
    row_ids = lax.broadcasted_iota(jnp.int32, (MR_LEN, MR_LEN), 0)
    col_ids = lax.broadcasted_iota(jnp.int32, (MR_LEN, MR_LEN), 1)
    flip = jnp.where(row_ids + col_ids == MR_LEN - 1, 1.0, 0.0).astype(F32)
    mr_out[...] = lax.dot_general(
        flip, rows, (((1,), (1,)), ((), ())), preferred_element_type=F32, precision=lax.Precision.HIGHEST
    ) * (1.0 / (tokens * GROUP) ** 0.5)
    for i in range(tiles):
        at = slice(i * LANES, (i + 1) * LANES)
        low = 2 * GT * i + GT
        se_out[:, at] = packed[low : low + SE_LEN, :] * (1.0 / tokens**0.5)
        gain_out[:, at] = packed[low + SE_LEN : low + SE_LEN + 1, :] * (1.0 / tokens**0.5)


def finish(packed, tokens, channels):
    return pl.pallas_call(
        functools.partial(finish_kernel, tokens),
        out_shape=[
            jax.ShapeDtypeStruct((MR_LEN, channels // GROUP), F32),
            jax.ShapeDtypeStruct((SE_LEN, channels), F32),
            jax.ShapeDtypeStruct((1, channels), F32),
        ],
        compiler_params=params(),
        cost_estimate=cost(0.9),
        name="finish",
    )(packed)


def add_kernel(one_ref, other_ref, total_out):
    total_out[...] = one_ref[...] + other_ref[...]


def pair_up(x, partner):
    return lax.ppermute(x, "tp", [(i, partner(i)) for i in range(lax.axis_size("tp"))])


def spread(x, groups):
    everyone = jnp.broadcast_to(x[None], (len(groups[0]),) + x.shape)
    return lax.all_to_all(everyone, "ctx", 0, 0, axis_index_groups=groups)


def sum_over_ctx(packed, beside):
    peers = lax.axis_size("ctx")
    near = [list(range(first, first + NEAR)) for first in range(0, peers, NEAR)]
    far = [list(range(first, peers, NEAR)) for first in range(NEAR)]
    parts = packed.reshape(NEAR, packed.shape[0] // NEAR, packed.shape[1])
    arrived = lax.all_to_all(parts, "ctx", 0, 0, axis_index_groups=near)
    arrived, done = lax.optimization_barrier((arrived, beside(0)))
    mine, done = lax.optimization_barrier((jnp.sum(arrived, axis=0), done))
    arrived = spread(mine, far)
    arrived, done = lax.optimization_barrier((arrived, beside(1, done)))
    return spread(jnp.sum(arrived, axis=0), near).reshape(packed.shape), done


def local(query, key_in, value_in, out_grad, mr_filter, se_filter, gain):
    tok, channels = query.shape
    tokens_all = tok * lax.axis_size("ctx")
    gated_halo = shifted(tail_rows(key_in, value_in), 1)
    front_table, back_table = tables(mr_filter)
    se = se_filter
    gain_row = gain[None, :]
    medium_high, short_high, wide_high, square, inner = early(
        key_in, value_in, query, out_grad, se, gain_row, front_table
    )
    medium_low, short_low, sums = late(
        gated_halo,
        key_in,
        value_in,
        query,
        out_grad,
        se,
        gain_row,
        front_table,
        short_high,
        square,
        inner,
    )
    sums = call(add_kernel, "pair_sums", 0.2, [((2, tok), F32)], [], sums, pair_up(sums, lambda i: i ^ 1))[0]
    sums = [sums, pair_up(sums, lambda i: lax.axis_size("tp") - 1 - i)]
    wide_low = wide(gated_halo, key_in, value_in, front_table)
    sums, wide_low = lax.optimization_barrier((sums, wide_low))
    head_rows = head(sums, query, out_grad, medium_low, gain_row)
    grad_halo = shifted(head_rows, -1)
    query_grad, medium_grad, packed = grads(
        sums,
        query,
        out_grad,
        medium_low,
        medium_high,
        gain_row,
        short_low,
        short_high,
        wide_low,
        wide_high,
    )
    packed, (key_grad, value_grad) = sum_over_ctx(
        packed, functools.partial(backward, medium_grad, grad_halo, se, key_in, value_in, back_table)
    )
    mr_grad, se_grad, gain_grad = finish(packed, tokens_all, channels)
    return query_grad, key_grad, value_grad, mr_grad, se_grad, gain_grad[0]


def solution(mesh):
    return jax.shard_map(
        local,
        mesh=mesh,
        in_specs=(
            P("ctx", "tp"),
            P("ctx", "tp"),
            P("ctx", "tp"),
            P("ctx", "tp"),
            P(None, "tp"),
            P(None, "tp"),
            P("tp"),
        ),
        out_specs=(
            P("ctx", "tp"),
            P("ctx", "tp"),
            P("ctx", "tp"),
            P(None, "tp"),
            P(None, "tp"),
            P("tp"),
        ),
        check_vma=False,
    )
```

```python
import functools

import jax
import jax.numpy as jnp
from jax import lax
from jax.experimental import pallas as pl
from jax.experimental.pallas import tpu as pltpu
from jax.sharding import PartitionSpec as P

D = 8192
GROUP = 16
MR_LEN = 128
SE_LEN = 7
EPS = 1e-06

LANES = 128
HALO = 144
S = 32
W = S + MR_LEN
SG = 16
GT = LANES // GROUP
EARLY = S + MR_LEN
F32 = jnp.float32
BF16 = jnp.bfloat16


UNROLL = 8
TAIL_PARTS = 4
BW = 512
PARTS = (0, 1, 3, 4)
NEAR = 8
VMEM = pl.BlockSpec(memory_space=pltpu.VMEM)
HBM = pl.BlockSpec(memory_space=pltpu.HBM)


def params(limit=24):
    return pltpu.CompilerParams(vmem_limit_bytes=int(limit * 1024 * 1024))


def cost(micros):
    return pl.CostEstimate(flops=int(micros * 1e9), bytes_accessed=0, transcendentals=0)


def each_tile(channels, body):
    unroll = min(UNROLL, channels // LANES)

    def step(i, carry):
        for slot in range(unroll):
            tile = i * unroll + slot
            body(pl.ds(pl.multiple_of(tile * LANES, LANES), LANES), tile, slot)
        return carry

    lax.fori_loop(0, channels // LANES // unroll, step, 0)


def of_tile(tile, rows):
    return pl.ds(pl.multiple_of(tile * rows, rows), rows)


def call(body, name, micros, outs, scratch, *args, out_specs=None, places=None):
    out_specs = out_specs or [VMEM] * len(outs)
    return pl.pallas_call(
        body,
        in_specs=[VMEM] * len(args),
        out_specs=out_specs,
        out_shape=[
            (pltpu.HBM if place is HBM else jax.ShapeDtypeStruct)(shape, dtype)
            for (shape, dtype), place in zip(outs, places or out_specs)
        ],
        scratch_shapes=scratch,
        compiler_params=params(),
        cost_estimate=cost(micros),
        name=name,
    )(*args)


def shifted(x, by):
    peers = lax.axis_size("ctx")
    return lax.ppermute(x, "ctx", [(i, i + by) for i in range(peers) if 0 <= i + by < peers])


def group_of_lane(rows):
    return lax.broadcasted_iota(jnp.int32, (rows, LANES), 1) // GROUP


def toeplitz(table, windows):
    results = []
    which = group_of_lane(S)
    for first in range(0, len(windows), 2):
        pair = windows[first : first + 2]
        rhs = jnp.concatenate(pair, axis=1) if len(pair) == 2 else pair[0]
        out = jnp.dot(table, rhs, preferred_element_type=F32)
        for n in range(len(pair)):
            total = out[:S, n * LANES : (n + 1) * LANES]
            for g in range(1, GT):
                part = out[g * S : (g + 1) * S, n * LANES : (n + 1) * LANES]
                total = jnp.where(which == g, part, total)
            results.append(total)
    return results


def table_kernel(taps_ref, front_out, back_out, rows_ref, back_ref, sem):
    taps = taps_ref[...]
    row_ids = lax.broadcasted_iota(jnp.int32, (MR_LEN, 2 * LANES), 0)
    col_ids = lax.broadcasted_iota(jnp.int32, (MR_LEN, 2 * LANES), 1)
    for n, place in enumerate((MR_LEN - row_ids, row_ids)):
        pick = jnp.where(col_ids == place, 1.0, 0.0).astype(BF16)
        rows_ref[n] = lax.dot_general(taps, pick, (((0,), (0,)), ((), ())), preferred_element_type=F32)

    def fill(n, target):
        def one(g, carry):
            rows = rows_ref[n, of_tile(g, GT), :]
            for k in range(GT):
                row = jnp.broadcast_to(rows[k : k + 1, :], (S, 2 * LANES))
                turned = pltpu.roll(row, 0, 1, stride=1, stride_axis=0).astype(BF16)
                target[of_tile(g * GT + k, S), :] = turned
            return carry

        lax.fori_loop(0, taps_ref.shape[1] // GT, one, 0)

    fill(1, back_ref)
    copy = pltpu.make_async_copy(back_ref, back_out, sem)
    copy.start()
    fill(0, front_out)
    copy.wait()


def tables(mr_filter):
    groups = mr_filter.shape[1]
    shape = ((groups * S, 2 * LANES), BF16)
    scratch = [
        pltpu.VMEM((2, groups, 2 * LANES), F32),
        pltpu.VMEM((groups * S, 2 * LANES), BF16),
        pltpu.SemaphoreType.DMA,
    ]
    specs = [VMEM, HBM]
    return call(table_kernel, "filter_tables", 2.4, [shape, shape], scratch, mr_filter, out_specs=specs)


def short_filter(se_ref, at, gated_ref, first, rows):
    total = jnp.zeros((rows, LANES), F32)
    se = se_ref[:, at].astype(F32)
    for tap in range(SE_LEN):
        total = total + se[tap : tap + 1, :] * gated_ref[first - tap : first - tap + rows, :]
    return total.astype(BF16)


def gate(key_ref, value_ref, rows, at):
    return (key_ref[rows, at].astype(F32) * value_ref[rows, at].astype(F32)).astype(BF16)


def tail_kernel(key_ref, value_ref, tail_out, held_ref, sems):
    tok, channels = key_ref.shape
    width = channels // TAIL_PARTS
    copies = []
    for n in range(TAIL_PARTS):
        at = slice(n * width, (n + 1) * width)
        for m, source in enumerate((key_ref, value_ref)):
            copy = pltpu.make_async_copy(
                source.at[tok - HALO :, at], held_ref.at[m, :, at], sems.at[m, n]
            )
            copy.start()
            copies.append(copy)
    for n in range(TAIL_PARTS):
        copies[2 * n].wait()
        copies[2 * n + 1].wait()
        at = slice(n * width, (n + 1) * width)
        tail_out[:, at] = (held_ref[0, :, at].astype(F32) * held_ref[1, :, at].astype(F32)).astype(BF16)


def tail_rows(key_in, value_in):
    channels = key_in.shape[1]
    return pl.pallas_call(
        tail_kernel,
        in_specs=[HBM, HBM],
        out_specs=VMEM,
        out_shape=pltpu.VMEM((HALO, channels), BF16),
        scratch_shapes=[
            pltpu.VMEM((2, HALO, channels), BF16),
            pltpu.SemaphoreType.DMA((2, TAIL_PARTS)),
        ],
        compiler_params=params(62),
        cost_estimate=cost(1.2),
        name="tail_rows",
    )(key_in, value_in)


def early_kernel(
    key_ref,
    value_ref,
    query_ref,
    out_grad_ref,
    se_ref,
    gain_ref,
    table_ref,
    medium_out,
    short_out,
    wide_out,
    square_out,
    inner_out,
    gated_ref,
):
    tok, channels = key_ref.shape
    square_out[...] = jnp.zeros_like(square_out)
    inner_out[...] = jnp.zeros_like(inner_out)

    def body(at, tile, slot):
        wide_ref = gated_ref.at[slot]
        gated = gate(key_ref, value_ref, slice(None), at)
        wide_ref[...] = gated.astype(F32)
        short_out[:S, at] = jnp.zeros((S, LANES), BF16)
        short_out[S:, at] = short_filter(se_ref, at, wide_ref, S, tok - S)
        short_out[16:S, at] = short_filter(se_ref, at, wide_ref, 16, S - 16)
        table = table_ref[of_tile(tile, GT * S), :W]
        first = [t for t in range(EARLY, tok, S)]
        windows = [short_out[t - MR_LEN : t + S, at] for t in first]
        also = [t for t in range(MR_LEN, tok, S)]
        windows += [gated[t - MR_LEN : t + S, :] for t in also]
        parts = toeplitz(table, windows)
        gain = gain_ref[:, at]
        for t, medium in zip(first, parts):
            down = slice(t - EARLY, t - EARLY + S)
            medium_out[down, at] = medium
            mixed = query_ref[t : t + S, at].astype(F32) * medium
            norm_grad = out_grad_ref[t : t + S, at].astype(F32) * gain
            square_out[down, :] += mixed * mixed
            inner_out[down, :] += norm_grad * mixed
        for t, part in zip(also, parts[len(first) :]):
            wide_out[t - MR_LEN : t - MR_LEN + S, at] = part

    each_tile(channels, body)


def early(key_in, value_in, query, out_grad, se, gain, table):
    tok, channels = key_in.shape
    outs = [
        ((tok - EARLY, channels), F32),
        ((tok, channels), BF16),
        ((tok - MR_LEN, channels), F32),
        ((tok - EARLY, LANES), F32),
        ((tok - EARLY, LANES), F32),
    ]
    scratch = [pltpu.VMEM((UNROLL, tok, LANES), F32)]
    return call(early_kernel, "early", 4.2, outs, scratch, key_in, value_in, query, out_grad, se, gain, table)


def window(low_ref, high_ref, b, at):
    if b * S >= EARLY:
        return high_ref[b * S - MR_LEN : b * S + S, at]
    if b == 0:
        return low_ref[:, at]
    return jnp.concatenate([low_ref[S * b :, at], high_ref[S : S * b + S, at]], axis=0)


def late_kernel(
    halo_ref,
    key_ref,
    value_ref,
    query_ref,
    out_grad_ref,
    se_ref,
    gain_ref,
    table_ref,
    high_ref,
    square_in,
    inner_in,
    medium_out,
    low_out,
    sums_out,
    gated_ref,
    square_ref,
    inner_ref,
):
    channels = key_ref.shape[1]
    square_ref[:EARLY, :] = jnp.zeros((EARLY, LANES), F32)
    inner_ref[:EARLY, :] = jnp.zeros((EARLY, LANES), F32)
    square_ref[EARLY:, :] = square_in[...]
    inner_ref[EARLY:, :] = inner_in[...]

    def body(at, tile, slot):
        rows = gated_ref.at[slot]
        rows[:HALO, :] = halo_ref[:, at].astype(F32)
        rows[HALO:, :] = gate(key_ref, value_ref, slice(0, S), at).astype(F32)
        low_out[:, at] = short_filter(se_ref, at, rows, HALO - MR_LEN, MR_LEN + S)
        table = table_ref[of_tile(tile, GT * S), :W]
        windows = [window(low_out, high_ref, b, at) for b in range(EARLY // S)]
        gain = gain_ref[:, at]
        for b, medium in enumerate(toeplitz(table, windows)):
            down = slice(S * b, S * b + S)
            medium_out[down, at] = medium
            mixed = query_ref[down, at].astype(F32) * medium
            norm_grad = out_grad_ref[down, at].astype(F32) * gain
            square_ref[down, :] += mixed * mixed
            inner_ref[down, :] += norm_grad * mixed

    each_tile(channels, body)
    sums_out[0:1, :] = jnp.sum(square_ref[...].T, axis=0, keepdims=True)
    sums_out[1:2, :] = jnp.sum(inner_ref[...].T, axis=0, keepdims=True)


def late(halo, key_in, value_in, query, out_grad, se, gain, table, short_high, square, inner):
    tok, channels = key_in.shape
    outs = [((EARLY, channels), F32), ((MR_LEN + S, channels), BF16), ((2, tok), F32)]
    scratch = [
        pltpu.VMEM((UNROLL, HALO + S, LANES), F32),
        pltpu.VMEM((tok, LANES), F32),
        pltpu.VMEM((tok, LANES), F32),
    ]
    return call(
        late_kernel,
        "late",
        2.9,
        outs,
        scratch,
        halo,
        key_in,
        value_in,
        query,
        out_grad,
        se,
        gain,
        table,
        short_high,
        square,
        inner,
    )


def spread_sums(parts, scale_ref, slope_ref, rows):
    sums = functools.reduce(jnp.add, [part[...] for part in parts])
    square = jnp.broadcast_to(sums[0:1, :], (LANES, sums.shape[1])).T[:rows]
    inner = jnp.broadcast_to(sums[1:2, :], (LANES, sums.shape[1])).T[:rows]
    inv = lax.rsqrt(square / D + EPS)
    scale_ref[...] = inv
    slope_ref[...] = inv * inv * inv * inner / D


def head_kernel(query_ref, out_grad_ref, medium_ref, gain_ref, *rest):
    sums, (head_out, scale_ref, slope_ref) = rest[:-3], rest[-3:]
    spread_sums(sums, scale_ref, slope_ref, HALO)

    def body(at, tile, slot):
        query = query_ref[:HALO, at].astype(F32)
        norm_grad = out_grad_ref[:HALO, at].astype(F32) * gain_ref[:, at]
        mixed = query * medium_ref[:HALO, at]
        mixed_grad = scale_ref[...] * norm_grad - mixed * slope_ref[...]
        head_out[:, at] = (mixed_grad * query).astype(BF16)

    each_tile(query_ref.shape[1], body)


def head(sums, query, out_grad, medium_low, gain):
    outs = [((HALO, query.shape[1]), BF16)]
    scratch = [pltpu.VMEM((HALO, LANES), F32), pltpu.VMEM((HALO, LANES), F32)]
    return call(head_kernel, "head_rows", 0.9, outs, scratch, query, out_grad, medium_low, gain, *sums)[0]


def wide_kernel(halo_ref, key_ref, value_ref, table_ref, wide_out, gated_ref):
    lead = W - HALO

    def body(at, tile, slot):
        rows = gated_ref.at[slot]
        rows[:lead, :] = jnp.zeros((lead, LANES), BF16)
        rows[lead:W, :] = halo_ref[:, at]
        rows[W:, :] = gate(key_ref, value_ref, slice(0, MR_LEN), at)
        windows = [rows[S * b : S * b + W, :] for b in range(MR_LEN // S + 1)]
        for b, part in enumerate(toeplitz(table_ref[of_tile(tile, GT * S), :W], windows)):
            wide_out[S * b : S * b + S, at] = part

    each_tile(key_ref.shape[1], body)


def wide(halo, key_in, value_in, table):
    outs = [((MR_LEN + S, key_in.shape[1]), F32)]
    scratch = [pltpu.VMEM((UNROLL, W + MR_LEN, LANES), BF16)]
    return call(wide_kernel, "wide_gated", 2.0, outs, scratch, halo, key_in, value_in, table)[0]


def grads_kernel(
    query_ref,
    out_grad_ref,
    medium_low_ref,
    medium_high_ref,
    gain_ref,
    short_low_ref,
    short_high_ref,
    wide_low_ref,
    wide_high_ref,
    *rest,
):
    query_grad_out, medium_grad_out, packed_out, scale_ref, slope_ref, cross_ref, wide_ref = rest[-7:]
    tok, channels = query_ref.shape
    spread_sums(rest[:-7], scale_ref, slope_ref, tok)
    blocks = tok // SG
    side = GT * SG

    def body(at, tile, slot):
        query = query_ref[:, at].astype(F32)
        out_grad = out_grad_ref[:, at].astype(F32)
        medium = jnp.concatenate([medium_low_ref[:, at], medium_high_ref[:, at]], axis=0)
        inv = scale_ref[...]
        norm_grad = out_grad * gain_ref[:, at]
        mixed = query * medium
        mixed_grad = inv * norm_grad - mixed * slope_ref[...]
        query_grad_out[:, at] = (mixed_grad * medium).astype(BF16)
        medium_grad = (mixed_grad * query).astype(BF16)
        medium_grad_out[:, at] = medium_grad
        gain_row = jnp.sum(out_grad * mixed * inv, axis=0, keepdims=True)
        wide_grad = medium_grad.astype(F32)
        rows = wide_ref.at[slot]
        rows[: MR_LEN + S, :] = wide_low_ref[:, at]
        rows[MR_LEN + S :, :] = wide_high_ref[:, at]
        lines = [
            jnp.sum(wide_grad * rows[S - tap : S - tap + tok, :], axis=0, keepdims=True)
            for tap in range(SE_LEN)
        ]
        lhs_rows = jnp.concatenate([medium_grad[SG * b : SG * b + SG, :] for b in range(blocks)], axis=1)
        which = lax.broadcasted_iota(jnp.int32, lhs_rows.shape, 1) % LANES // GROUP
        lhs = jnp.concatenate(
            [jnp.where(which == g, lhs_rows, jnp.zeros_like(lhs_rows)) for g in range(GT)], axis=0
        )
        short = jnp.concatenate([short_low_ref[:, at], short_high_ref[S:, at]], axis=0)
        rhs = jnp.concatenate([short[SG * b : SG * b + SG + MR_LEN, :] for b in range(blocks)], axis=1)
        cross = lax.dot_general(lhs, rhs, (((1,), (1,)), ((), ())), preferred_element_type=F32)
        held = cross_ref.at[slot]
        held[:side, :] = cross[:, :LANES]
        held[side:, :SG] = cross[:, LANES:]
        total = jnp.zeros((GT, 2 * LANES), F32)
        for s in range(SG):
            part = jnp.concatenate(
                [held[pl.ds(m * side + s, GT, stride=SG), :] for m in range(2)], axis=1
            )
            total = total + pltpu.roll(part, 2 * LANES - 1 - s, 1)
        packed_out[of_tile(tile, 2 * GT), :] = jnp.concatenate(
            [total[:, :LANES]] + lines + [gain_row], axis=0
        )

    each_tile(channels, body)


def grads(sums, query, out_grad, medium_low, medium_high, gain, short_low, short_high, wide_low, wide_high):
    tok, channels = query.shape
    outs = [
        ((tok, channels), BF16),
        ((tok, channels), BF16),
        ((2 * GT * channels // LANES, LANES), F32),
    ]
    scratch = [
        pltpu.VMEM((tok, LANES), F32),
        pltpu.VMEM((tok, LANES), F32),
        pltpu.VMEM((UNROLL, 2 * GT * SG, LANES), F32),
        pltpu.VMEM((UNROLL, tok + S, LANES), F32),
    ]
    return call(
        grads_kernel,
        "gradients",
        6.6,
        outs,
        scratch,
        query,
        out_grad,
        medium_low,
        medium_high,
        gain,
        short_low,
        short_high,
        wide_low,
        wide_high,
        *sums,
        places=[HBM, HBM, VMEM],
    )


def backward_kernel(grad_ref, halo_ref, se_ref, key_ref, value_ref, table_ref, *rest):
    key_out, value_out, ext_ref, short_ref = rest[-4:]
    tok = key_ref.shape[0]

    def body(at, tile, slot):
        ext = ext_ref.at[slot]
        short = short_ref.at[slot]
        ext[:tok, :] = grad_ref[:, at]
        ext[tok : tok + HALO, :] = halo_ref[:, at]
        ext[tok + HALO :, :] = jnp.zeros((W - HALO, LANES), BF16)
        windows = [ext[S * b : S * b + W, :] for b in range(tok // S + 1)]
        for b, part in enumerate(toeplitz(table_ref[of_tile(tile, GT * S), :W], windows)):
            short[S * b : S * b + S, :] = part
        total = jnp.zeros((tok, LANES), F32)
        se = se_ref[:, at].astype(F32)
        for tap in range(SE_LEN):
            total = total + se[tap : tap + 1, :] * short[tap : tap + tok, :]
        key_out[:, at] = (total * value_ref[:, at].astype(F32)).astype(BF16)
        value_out[:, at] = (total * key_ref[:, at].astype(F32)).astype(BF16)

    each_tile(key_ref.shape[1], body)


def backward(medium_grad, halo, se, key_in, value_in, table, part, done=()):
    tok, channels = key_in.shape
    first, steps = PARTS[part], PARTS[part + 1] - PARTS[part]
    col = lambda rows: pl.BlockSpec((rows, BW), lambda i: (0, first + i))
    tiles = BW // LANES
    shape = jax.ShapeDtypeStruct((tok, channels), BF16)
    return pl.pallas_call(
        backward_kernel,
        grid=(steps,),
        in_specs=[
            col(tok),
            col(HALO),
            col(SE_LEN),
            col(tok),
            col(tok),
            pl.BlockSpec((tiles * GT * S, 2 * LANES), lambda i: (first + i, 0)),
        ]
        + [HBM] * len(done),
        out_specs=[col(tok), col(tok)],
        out_shape=[shape, shape],
        scratch_shapes=[
            pltpu.VMEM((tiles, tok + W, LANES), BF16),
            pltpu.VMEM((tiles, tok + S, LANES), F32),
        ],
        input_output_aliases={6 + n: n for n in range(len(done))},
        compiler_params=params(62),
        cost_estimate=cost(2.0 * steps),
        name="backward",
    )(medium_grad, halo, se, key_in, value_in, table, *done)


def finish_kernel(tokens, packed_ref, mr_out, se_out, gain_out):
    packed = packed_ref[...]
    tiles = packed.shape[0] // (2 * GT)
    rows = jnp.concatenate([packed[2 * GT * i : 2 * GT * i + GT, :] for i in range(tiles)], axis=0)
    row_ids = lax.broadcasted_iota(jnp.int32, (MR_LEN, MR_LEN), 0)
    col_ids = lax.broadcasted_iota(jnp.int32, (MR_LEN, MR_LEN), 1)
    flip = jnp.where(row_ids + col_ids == MR_LEN - 1, 1.0, 0.0).astype(F32)
    mr_out[...] = lax.dot_general(
        flip, rows, (((1,), (1,)), ((), ())), preferred_element_type=F32, precision=lax.Precision.HIGHEST
    ) * (1.0 / (tokens * GROUP) ** 0.5)
    for i in range(tiles):
        at = slice(i * LANES, (i + 1) * LANES)
        low = 2 * GT * i + GT
        se_out[:, at] = packed[low : low + SE_LEN, :] * (1.0 / tokens**0.5)
        gain_out[:, at] = packed[low + SE_LEN : low + SE_LEN + 1, :] * (1.0 / tokens**0.5)


def finish(packed, tokens, channels):
    return pl.pallas_call(
        functools.partial(finish_kernel, tokens),
        out_shape=[
            jax.ShapeDtypeStruct((MR_LEN, channels // GROUP), F32),
            jax.ShapeDtypeStruct((SE_LEN, channels), F32),
            jax.ShapeDtypeStruct((1, channels), F32),
        ],
        compiler_params=params(),
        cost_estimate=cost(0.9),
        name="finish",
    )(packed)


def from_peers(x, axis):
    peers = lax.axis_size(axis)
    return [lax.ppermute(x, axis, [(i, (i + k) % peers) for i in range(peers)]) for k in range(1, peers)]


def spread(x, groups):
    everyone = jnp.broadcast_to(x[None], (len(groups[0]),) + x.shape)
    return lax.all_to_all(everyone, "ctx", 0, 0, axis_index_groups=groups)


def sum_over_ctx(packed, beside):
    peers = lax.axis_size("ctx")
    near = [list(range(first, first + NEAR)) for first in range(0, peers, NEAR)]
    far = [list(range(first, peers, NEAR)) for first in range(NEAR)]
    parts = packed.reshape(NEAR, packed.shape[0] // NEAR, packed.shape[1])
    arrived = lax.all_to_all(parts, "ctx", 0, 0, axis_index_groups=near)
    arrived, done = lax.optimization_barrier((arrived, beside(0)))
    mine, done = lax.optimization_barrier((jnp.sum(arrived, axis=0), done))
    arrived = spread(mine, far)
    arrived, done = lax.optimization_barrier((arrived, beside(1, done)))
    mine, done = lax.optimization_barrier((jnp.sum(arrived, axis=0), done))
    everyone, done = lax.optimization_barrier((spread(mine, near), beside(2, done)))
    return everyone.reshape(packed.shape), done


def local(query, key_in, value_in, out_grad, mr_filter, se_filter, gain):
    tok, channels = query.shape
    tokens_all = tok * lax.axis_size("ctx")
    gated_halo = shifted(tail_rows(key_in, value_in), 1)
    front_table, back_table = tables(mr_filter)
    se = se_filter
    gain_row = gain[None, :]
    medium_high, short_high, wide_high, square, inner = early(
        key_in, value_in, query, out_grad, se, gain_row, front_table
    )
    medium_low, short_low, sums = late(
        gated_halo,
        key_in,
        value_in,
        query,
        out_grad,
        se,
        gain_row,
        front_table,
        short_high,
        square,
        inner,
    )
    sums = [sums] + from_peers(sums, "tp")
    wide_low = wide(gated_halo, key_in, value_in, front_table)
    sums, wide_low = lax.optimization_barrier((sums, wide_low))
    head_rows = head(sums, query, out_grad, medium_low, gain_row)
    grad_halo = shifted(head_rows, -1)
    query_grad, medium_grad, packed = grads(
        sums,
        query,
        out_grad,
        medium_low,
        medium_high,
        gain_row,
        short_low,
        short_high,
        wide_low,
        wide_high,
    )
    packed, (key_grad, value_grad) = sum_over_ctx(
        packed, functools.partial(backward, medium_grad, grad_halo, se, key_in, value_in, back_table)
    )
    mr_grad, se_grad, gain_grad = finish(packed, tokens_all, channels)
    return query_grad, key_grad, value_grad, mr_grad, se_grad, gain_grad[0]


def solution(mesh):
    return jax.shard_map(
        local,
        mesh=mesh,
        in_specs=(
            P("ctx", "tp"),
            P("ctx", "tp"),
            P("ctx", "tp"),
            P("ctx", "tp"),
            P(None, "tp"),
            P(None, "tp"),
            P("tp"),
        ),
        out_specs=(
            P("ctx", "tp"),
            P("ctx", "tp"),
            P("ctx", "tp"),
            P(None, "tp"),
            P(None, "tp"),
            P("tp"),
        ),
        check_vma=False,
    )
```

```python
import functools

import jax
import jax.numpy as jnp
from jax import lax
from jax.experimental import pallas as pl
from jax.experimental.pallas import tpu as pltpu
from jax.sharding import PartitionSpec as P

D = 8192
GROUP = 16
MR_LEN = 128
SE_LEN = 7
EPS = 1e-06

LANES = 128
HALO = 144
S = 32
W = S + MR_LEN
SG = 16
GT = LANES // GROUP
EARLY = S + MR_LEN
F32 = jnp.float32
BF16 = jnp.bfloat16


UNROLL = 8
TAIL_PARTS = 4
BW = 512
PARTS = (0, 2, 4)
WIRE = jnp.bfloat16
VMEM = pl.BlockSpec(memory_space=pltpu.VMEM)
HBM = pl.BlockSpec(memory_space=pltpu.HBM)


def params(limit=24):
    return pltpu.CompilerParams(vmem_limit_bytes=int(limit * 1024 * 1024))


def cost(micros):
    return pl.CostEstimate(flops=int(micros * 1e9), bytes_accessed=0, transcendentals=0)


def each_tile(channels, body):
    unroll = min(UNROLL, channels // LANES)

    def step(i, carry):
        for slot in range(unroll):
            tile = i * unroll + slot
            body(pl.ds(pl.multiple_of(tile * LANES, LANES), LANES), tile, slot)
        return carry

    lax.fori_loop(0, channels // LANES // unroll, step, 0)


def of_tile(tile, rows):
    return pl.ds(pl.multiple_of(tile * rows, rows), rows)


def call(body, name, micros, outs, scratch, *args, out_specs=None, places=None):
    out_specs = out_specs or [VMEM] * len(outs)
    return pl.pallas_call(
        body,
        in_specs=[VMEM] * len(args),
        out_specs=out_specs,
        out_shape=[
            (pltpu.HBM if place is HBM else jax.ShapeDtypeStruct)(shape, dtype)
            for (shape, dtype), place in zip(outs, places or out_specs)
        ],
        scratch_shapes=scratch,
        compiler_params=params(),
        cost_estimate=cost(micros),
        name=name,
    )(*args)


def shifted(x, by):
    peers = lax.axis_size("ctx")
    return lax.ppermute(x, "ctx", [(i, i + by) for i in range(peers) if 0 <= i + by < peers])


def group_of_lane(rows):
    return lax.broadcasted_iota(jnp.int32, (rows, LANES), 1) // GROUP


def toeplitz(table, windows):
    results = []
    which = group_of_lane(S)
    for first in range(0, len(windows), 2):
        pair = windows[first : first + 2]
        rhs = jnp.concatenate(pair, axis=1) if len(pair) == 2 else pair[0]
        out = jnp.dot(table, rhs, preferred_element_type=F32)
        for n in range(len(pair)):
            total = out[:S, n * LANES : (n + 1) * LANES]
            for g in range(1, GT):
                part = out[g * S : (g + 1) * S, n * LANES : (n + 1) * LANES]
                total = jnp.where(which == g, part, total)
            results.append(total)
    return results


def table_kernel(taps_ref, front_out, back_out, rows_ref, back_ref, sem):
    taps = taps_ref[...]
    row_ids = lax.broadcasted_iota(jnp.int32, (MR_LEN, 2 * LANES), 0)
    col_ids = lax.broadcasted_iota(jnp.int32, (MR_LEN, 2 * LANES), 1)
    for n, place in enumerate((MR_LEN - row_ids, row_ids)):
        pick = jnp.where(col_ids == place, 1.0, 0.0).astype(BF16)
        rows_ref[n] = lax.dot_general(taps, pick, (((0,), (0,)), ((), ())), preferred_element_type=F32)

    def fill(n, target):
        def one(g, carry):
            rows = rows_ref[n, of_tile(g, GT), :]
            for k in range(GT):
                row = jnp.broadcast_to(rows[k : k + 1, :], (S, 2 * LANES))
                turned = pltpu.roll(row, 0, 1, stride=1, stride_axis=0).astype(BF16)
                target[of_tile(g * GT + k, S), :] = turned
            return carry

        lax.fori_loop(0, taps_ref.shape[1] // GT, one, 0)

    fill(1, back_ref)
    copy = pltpu.make_async_copy(back_ref, back_out, sem)
    copy.start()
    fill(0, front_out)
    copy.wait()


def tables(mr_filter):
    groups = mr_filter.shape[1]
    shape = ((groups * S, 2 * LANES), BF16)
    scratch = [
        pltpu.VMEM((2, groups, 2 * LANES), F32),
        pltpu.VMEM((groups * S, 2 * LANES), BF16),
        pltpu.SemaphoreType.DMA,
    ]
    specs = [VMEM, HBM]
    return call(table_kernel, "filter_tables", 2.4, [shape, shape], scratch, mr_filter, out_specs=specs)


def short_filter(se_ref, at, gated_ref, first, rows):
    total = jnp.zeros((rows, LANES), F32)
    se = se_ref[:, at].astype(F32)
    for tap in range(SE_LEN):
        total = total + se[tap : tap + 1, :] * gated_ref[first - tap : first - tap + rows, :]
    return total.astype(BF16)


def gate(key_ref, value_ref, rows, at):
    return (key_ref[rows, at].astype(F32) * value_ref[rows, at].astype(F32)).astype(BF16)


def tail_kernel(key_ref, value_ref, tail_out, held_ref, sems):
    tok, channels = key_ref.shape
    width = channels // TAIL_PARTS
    copies = []
    for n in range(TAIL_PARTS):
        at = slice(n * width, (n + 1) * width)
        for m, source in enumerate((key_ref, value_ref)):
            copy = pltpu.make_async_copy(
                source.at[tok - HALO :, at], held_ref.at[m, :, at], sems.at[m, n]
            )
            copy.start()
            copies.append(copy)
    for n in range(TAIL_PARTS):
        copies[2 * n].wait()
        copies[2 * n + 1].wait()
        at = slice(n * width, (n + 1) * width)
        tail_out[:, at] = (held_ref[0, :, at].astype(F32) * held_ref[1, :, at].astype(F32)).astype(BF16)


def tail_rows(key_in, value_in):
    channels = key_in.shape[1]
    return pl.pallas_call(
        tail_kernel,
        in_specs=[HBM, HBM],
        out_specs=VMEM,
        out_shape=pltpu.VMEM((HALO, channels), BF16),
        scratch_shapes=[
            pltpu.VMEM((2, HALO, channels), BF16),
            pltpu.SemaphoreType.DMA((2, TAIL_PARTS)),
        ],
        compiler_params=params(62),
        cost_estimate=cost(1.2),
        name="tail_rows",
    )(key_in, value_in)


def early_kernel(
    key_ref,
    value_ref,
    query_ref,
    out_grad_ref,
    se_ref,
    gain_ref,
    table_ref,
    medium_out,
    short_out,
    wide_out,
    square_out,
    inner_out,
    gated_ref,
):
    tok, channels = key_ref.shape
    square_out[...] = jnp.zeros_like(square_out)
    inner_out[...] = jnp.zeros_like(inner_out)

    def body(at, tile, slot):
        wide_ref = gated_ref.at[slot]
        gated = gate(key_ref, value_ref, slice(None), at)
        wide_ref[...] = gated.astype(F32)
        short_out[:S, at] = jnp.zeros((S, LANES), BF16)
        short_out[S:, at] = short_filter(se_ref, at, wide_ref, S, tok - S)
        short_out[16:S, at] = short_filter(se_ref, at, wide_ref, 16, S - 16)
        table = table_ref[of_tile(tile, GT * S), :W]
        first = [t for t in range(EARLY, tok, S)]
        windows = [short_out[t - MR_LEN : t + S, at] for t in first]
        also = [t for t in range(MR_LEN, tok, S)]
        windows += [gated[t - MR_LEN : t + S, :] for t in also]
        parts = toeplitz(table, windows)
        gain = gain_ref[:, at]
        for t, medium in zip(first, parts):
            down = slice(t - EARLY, t - EARLY + S)
            medium_out[down, at] = medium
            mixed = query_ref[t : t + S, at].astype(F32) * medium
            norm_grad = out_grad_ref[t : t + S, at].astype(F32) * gain
            square_out[down, :] += mixed * mixed
            inner_out[down, :] += norm_grad * mixed
        for t, part in zip(also, parts[len(first) :]):
            wide_out[t - MR_LEN : t - MR_LEN + S, at] = part

    each_tile(channels, body)


def early(key_in, value_in, query, out_grad, se, gain, table):
    tok, channels = key_in.shape
    outs = [
        ((tok - EARLY, channels), F32),
        ((tok, channels), BF16),
        ((tok - MR_LEN, channels), F32),
        ((tok - EARLY, LANES), F32),
        ((tok - EARLY, LANES), F32),
    ]
    scratch = [pltpu.VMEM((UNROLL, tok, LANES), F32)]
    return call(early_kernel, "early", 4.2, outs, scratch, key_in, value_in, query, out_grad, se, gain, table)


def window(low_ref, high_ref, b, at):
    if b * S >= EARLY:
        return high_ref[b * S - MR_LEN : b * S + S, at]
    if b == 0:
        return low_ref[:, at]
    return jnp.concatenate([low_ref[S * b :, at], high_ref[S : S * b + S, at]], axis=0)


def late_kernel(
    halo_ref,
    key_ref,
    value_ref,
    query_ref,
    out_grad_ref,
    se_ref,
    gain_ref,
    table_ref,
    high_ref,
    square_in,
    inner_in,
    medium_out,
    low_out,
    sums_out,
    gated_ref,
    square_ref,
    inner_ref,
):
    channels = key_ref.shape[1]
    square_ref[:EARLY, :] = jnp.zeros((EARLY, LANES), F32)
    inner_ref[:EARLY, :] = jnp.zeros((EARLY, LANES), F32)
    square_ref[EARLY:, :] = square_in[...]
    inner_ref[EARLY:, :] = inner_in[...]

    def body(at, tile, slot):
        rows = gated_ref.at[slot]
        rows[:HALO, :] = halo_ref[:, at].astype(F32)
        rows[HALO:, :] = gate(key_ref, value_ref, slice(0, S), at).astype(F32)
        low_out[:, at] = short_filter(se_ref, at, rows, HALO - MR_LEN, MR_LEN + S)
        table = table_ref[of_tile(tile, GT * S), :W]
        windows = [window(low_out, high_ref, b, at) for b in range(EARLY // S)]
        gain = gain_ref[:, at]
        for b, medium in enumerate(toeplitz(table, windows)):
            down = slice(S * b, S * b + S)
            medium_out[down, at] = medium
            mixed = query_ref[down, at].astype(F32) * medium
            norm_grad = out_grad_ref[down, at].astype(F32) * gain
            square_ref[down, :] += mixed * mixed
            inner_ref[down, :] += norm_grad * mixed

    each_tile(channels, body)
    sums_out[0:1, :] = jnp.sum(square_ref[...].T, axis=0, keepdims=True)
    sums_out[1:2, :] = jnp.sum(inner_ref[...].T, axis=0, keepdims=True)


def late(halo, key_in, value_in, query, out_grad, se, gain, table, short_high, square, inner):
    tok, channels = key_in.shape
    outs = [((EARLY, channels), F32), ((MR_LEN + S, channels), BF16), ((2, tok), F32)]
    scratch = [
        pltpu.VMEM((UNROLL, HALO + S, LANES), F32),
        pltpu.VMEM((tok, LANES), F32),
        pltpu.VMEM((tok, LANES), F32),
    ]
    return call(
        late_kernel,
        "late",
        2.9,
        outs,
        scratch,
        halo,
        key_in,
        value_in,
        query,
        out_grad,
        se,
        gain,
        table,
        short_high,
        square,
        inner,
    )


def spread_sums(parts, scale_ref, slope_ref, rows):
    sums = functools.reduce(jnp.add, [part[...] for part in parts])
    square = jnp.broadcast_to(sums[0:1, :], (LANES, sums.shape[1])).T[:rows]
    inner = jnp.broadcast_to(sums[1:2, :], (LANES, sums.shape[1])).T[:rows]
    inv = lax.rsqrt(square / D + EPS)
    scale_ref[...] = inv
    slope_ref[...] = inv * inv * inv * inner / D


def head_kernel(query_ref, out_grad_ref, medium_ref, gain_ref, *rest):
    sums, (head_out, scale_ref, slope_ref) = rest[:-3], rest[-3:]
    spread_sums(sums, scale_ref, slope_ref, HALO)

    def body(at, tile, slot):
        query = query_ref[:HALO, at].astype(F32)
        norm_grad = out_grad_ref[:HALO, at].astype(F32) * gain_ref[:, at]
        mixed = query * medium_ref[:HALO, at]
        mixed_grad = scale_ref[...] * norm_grad - mixed * slope_ref[...]
        head_out[:, at] = (mixed_grad * query).astype(BF16)

    each_tile(query_ref.shape[1], body)


def head(sums, query, out_grad, medium_low, gain):
    outs = [((HALO, query.shape[1]), BF16)]
    scratch = [pltpu.VMEM((HALO, LANES), F32), pltpu.VMEM((HALO, LANES), F32)]
    return call(head_kernel, "head_rows", 0.9, outs, scratch, query, out_grad, medium_low, gain, *sums)[0]


def wide_kernel(halo_ref, key_ref, value_ref, table_ref, wide_out, gated_ref):
    lead = W - HALO

    def body(at, tile, slot):
        rows = gated_ref.at[slot]
        rows[:lead, :] = jnp.zeros((lead, LANES), BF16)
        rows[lead:W, :] = halo_ref[:, at]
        rows[W:, :] = gate(key_ref, value_ref, slice(0, MR_LEN), at)
        windows = [rows[S * b : S * b + W, :] for b in range(MR_LEN // S + 1)]
        for b, part in enumerate(toeplitz(table_ref[of_tile(tile, GT * S), :W], windows)):
            wide_out[S * b : S * b + S, at] = part

    each_tile(key_ref.shape[1], body)


def wide(halo, key_in, value_in, table):
    outs = [((MR_LEN + S, key_in.shape[1]), F32)]
    scratch = [pltpu.VMEM((UNROLL, W + MR_LEN, LANES), BF16)]
    return call(wide_kernel, "wide_gated", 2.0, outs, scratch, halo, key_in, value_in, table)[0]


def grads_kernel(
    query_ref,
    out_grad_ref,
    medium_low_ref,
    medium_high_ref,
    gain_ref,
    short_low_ref,
    short_high_ref,
    wide_low_ref,
    wide_high_ref,
    *rest,
):
    query_grad_out, medium_grad_out, packed_out, scale_ref, slope_ref, cross_ref, wide_ref = rest[-7:]
    tok, channels = query_ref.shape
    spread_sums(rest[:-7], scale_ref, slope_ref, tok)
    blocks = tok // SG
    side = GT * SG

    def body(at, tile, slot):
        query = query_ref[:, at].astype(F32)
        out_grad = out_grad_ref[:, at].astype(F32)
        medium = jnp.concatenate([medium_low_ref[:, at], medium_high_ref[:, at]], axis=0)
        inv = scale_ref[...]
        norm_grad = out_grad * gain_ref[:, at]
        mixed = query * medium
        mixed_grad = inv * norm_grad - mixed * slope_ref[...]
        query_grad_out[:, at] = (mixed_grad * medium).astype(BF16)
        medium_grad = (mixed_grad * query).astype(BF16)
        medium_grad_out[:, at] = medium_grad
        gain_row = jnp.sum(out_grad * mixed * inv, axis=0, keepdims=True)
        wide_grad = medium_grad.astype(F32)
        rows = wide_ref.at[slot]
        rows[: MR_LEN + S, :] = wide_low_ref[:, at]
        rows[MR_LEN + S :, :] = wide_high_ref[:, at]
        lines = [
            jnp.sum(wide_grad * rows[S - tap : S - tap + tok, :], axis=0, keepdims=True)
            for tap in range(SE_LEN)
        ]
        lhs_rows = jnp.concatenate([medium_grad[SG * b : SG * b + SG, :] for b in range(blocks)], axis=1)
        which = lax.broadcasted_iota(jnp.int32, lhs_rows.shape, 1) % LANES // GROUP
        lhs = jnp.concatenate(
            [jnp.where(which == g, lhs_rows, jnp.zeros_like(lhs_rows)) for g in range(GT)], axis=0
        )
        short = jnp.concatenate([short_low_ref[:, at], short_high_ref[S:, at]], axis=0)
        rhs = jnp.concatenate([short[SG * b : SG * b + SG + MR_LEN, :] for b in range(blocks)], axis=1)
        cross = lax.dot_general(lhs, rhs, (((1,), (1,)), ((), ())), preferred_element_type=F32)
        held = cross_ref.at[slot]
        held[:side, :] = cross[:, :LANES]
        held[side:, :SG] = cross[:, LANES:]
        total = jnp.zeros((GT, 2 * LANES), F32)
        for s in range(SG):
            part = jnp.concatenate(
                [held[pl.ds(m * side + s, GT, stride=SG), :] for m in range(2)], axis=1
            )
            total = total + pltpu.roll(part, 2 * LANES - 1 - s, 1)
        packed_out[of_tile(tile, 2 * GT), :] = jnp.concatenate(
            [total[:, :LANES]] + lines + [gain_row], axis=0
        ).astype(WIRE)

    each_tile(channels, body)


def grads(sums, query, out_grad, medium_low, medium_high, gain, short_low, short_high, wide_low, wide_high):
    tok, channels = query.shape
    outs = [
        ((tok, channels), BF16),
        ((tok, channels), BF16),
        ((2 * GT * channels // LANES, LANES), WIRE),
    ]
    scratch = [
        pltpu.VMEM((tok, LANES), F32),
        pltpu.VMEM((tok, LANES), F32),
        pltpu.VMEM((UNROLL, 2 * GT * SG, LANES), F32),
        pltpu.VMEM((UNROLL, tok + S, LANES), F32),
    ]
    return call(
        grads_kernel,
        "gradients",
        6.6,
        outs,
        scratch,
        query,
        out_grad,
        medium_low,
        medium_high,
        gain,
        short_low,
        short_high,
        wide_low,
        wide_high,
        *sums,
        places=[HBM, HBM, VMEM],
    )


def backward_kernel(grad_ref, halo_ref, se_ref, key_ref, value_ref, table_ref, *rest):
    key_out, value_out, ext_ref, short_ref = rest[-4:]
    tok = key_ref.shape[0]

    def body(at, tile, slot):
        ext = ext_ref.at[slot]
        short = short_ref.at[slot]
        ext[:tok, :] = grad_ref[:, at]
        ext[tok : tok + HALO, :] = halo_ref[:, at]
        ext[tok + HALO :, :] = jnp.zeros((W - HALO, LANES), BF16)
        windows = [ext[S * b : S * b + W, :] for b in range(tok // S + 1)]
        for b, part in enumerate(toeplitz(table_ref[of_tile(tile, GT * S), :W], windows)):
            short[S * b : S * b + S, :] = part
        total = jnp.zeros((tok, LANES), F32)
        se = se_ref[:, at].astype(F32)
        for tap in range(SE_LEN):
            total = total + se[tap : tap + 1, :] * short[tap : tap + tok, :]
        key_out[:, at] = (total * value_ref[:, at].astype(F32)).astype(BF16)
        value_out[:, at] = (total * key_ref[:, at].astype(F32)).astype(BF16)

    each_tile(key_ref.shape[1], body)


def backward(medium_grad, halo, se, key_in, value_in, table, part, done=()):
    tok, channels = key_in.shape
    first, steps = PARTS[part], PARTS[part + 1] - PARTS[part]
    col = lambda rows: pl.BlockSpec((rows, BW), lambda i: (0, first + i))
    tiles = BW // LANES
    shape = jax.ShapeDtypeStruct((tok, channels), BF16)
    return pl.pallas_call(
        backward_kernel,
        grid=(steps,),
        in_specs=[
            col(tok),
            col(HALO),
            col(SE_LEN),
            col(tok),
            col(tok),
            pl.BlockSpec((tiles * GT * S, 2 * LANES), lambda i: (first + i, 0)),
        ]
        + [HBM] * len(done),
        out_specs=[col(tok), col(tok)],
        out_shape=[shape, shape],
        scratch_shapes=[
            pltpu.VMEM((tiles, tok + W, LANES), BF16),
            pltpu.VMEM((tiles, tok + S, LANES), F32),
        ],
        input_output_aliases={6 + n: n for n in range(len(done))},
        compiler_params=params(62),
        cost_estimate=cost(2.0 * steps),
        name="backward",
    )(medium_grad, halo, se, key_in, value_in, table, *done)


def finish_kernel(tokens, packed_ref, mr_out, se_out, gain_out):
    packed = packed_ref[...].astype(F32)
    tiles = packed.shape[0] // (2 * GT)
    rows = jnp.concatenate([packed[2 * GT * i : 2 * GT * i + GT, :] for i in range(tiles)], axis=0)
    row_ids = lax.broadcasted_iota(jnp.int32, (MR_LEN, MR_LEN), 0)
    col_ids = lax.broadcasted_iota(jnp.int32, (MR_LEN, MR_LEN), 1)
    flip = jnp.where(row_ids + col_ids == MR_LEN - 1, 1.0, 0.0).astype(WIRE)
    mr_out[...] = lax.dot_general(
        flip, rows.astype(WIRE), (((1,), (1,)), ((), ())), preferred_element_type=F32
    ) * (1.0 / (tokens * GROUP) ** 0.5)
    for i in range(tiles):
        at = slice(i * LANES, (i + 1) * LANES)
        low = 2 * GT * i + GT
        se_out[:, at] = packed[low : low + SE_LEN, :] * (1.0 / tokens**0.5)
        gain_out[:, at] = packed[low + SE_LEN : low + SE_LEN + 1, :] * (1.0 / tokens**0.5)


def finish(packed, tokens, channels):
    return pl.pallas_call(
        functools.partial(finish_kernel, tokens),
        out_shape=[
            jax.ShapeDtypeStruct((MR_LEN, channels // GROUP), F32),
            jax.ShapeDtypeStruct((SE_LEN, channels), F32),
            jax.ShapeDtypeStruct((1, channels), F32),
        ],
        compiler_params=params(),
        cost_estimate=cost(0.9),
        name="finish",
    )(packed)


def from_peers(x, axis):
    peers = lax.axis_size(axis)
    return [lax.ppermute(x, axis, [(i, (i + k) % peers) for i in range(peers)]) for k in range(1, peers)]


def sum_over_ctx(packed, beside):
    peers = lax.axis_size("ctx")
    parts = packed.astype(WIRE).reshape(peers, packed.shape[0] // peers, packed.shape[1])
    arrived, done = lax.optimization_barrier((lax.all_to_all(parts, "ctx", 0, 0), beside(0)))
    mine = jnp.sum(arrived.astype(F32), axis=0).astype(WIRE)
    mine, done = lax.optimization_barrier((mine, done))
    everyone = lax.all_to_all(jnp.broadcast_to(mine[None], parts.shape), "ctx", 0, 0)
    everyone, done = lax.optimization_barrier((everyone, beside(1, done)))
    return everyone.reshape(packed.shape), done


def local(query, key_in, value_in, out_grad, mr_filter, se_filter, gain):
    tok, channels = query.shape
    tokens_all = tok * lax.axis_size("ctx")
    gated_halo = shifted(tail_rows(key_in, value_in), 1)
    front_table, back_table = tables(mr_filter)
    se = se_filter
    gain_row = gain[None, :]
    medium_high, short_high, wide_high, square, inner = early(
        key_in, value_in, query, out_grad, se, gain_row, front_table
    )
    medium_low, short_low, sums = late(
        gated_halo,
        key_in,
        value_in,
        query,
        out_grad,
        se,
        gain_row,
        front_table,
        short_high,
        square,
        inner,
    )
    sums = [sums] + from_peers(sums, "tp")
    wide_low = wide(gated_halo, key_in, value_in, front_table)
    sums, wide_low = lax.optimization_barrier((sums, wide_low))
    head_rows = head(sums, query, out_grad, medium_low, gain_row)
    grad_halo = shifted(head_rows, -1)
    query_grad, medium_grad, packed = grads(
        sums,
        query,
        out_grad,
        medium_low,
        medium_high,
        gain_row,
        short_low,
        short_high,
        wide_low,
        wide_high,
    )
    packed, (key_grad, value_grad) = sum_over_ctx(
        packed, functools.partial(backward, medium_grad, grad_halo, se, key_in, value_in, back_table)
    )
    mr_grad, se_grad, gain_grad = finish(packed, tokens_all, channels)
    return query_grad, key_grad, value_grad, mr_grad, se_grad, gain_grad[0]


def solution(mesh):
    return jax.shard_map(
        local,
        mesh=mesh,
        in_specs=(
            P("ctx", "tp"),
            P("ctx", "tp"),
            P("ctx", "tp"),
            P("ctx", "tp"),
            P(None, "tp"),
            P(None, "tp"),
            P("tp"),
        ),
        out_specs=(
            P("ctx", "tp"),
            P("ctx", "tp"),
            P("ctx", "tp"),
            P(None, "tp"),
            P(None, "tp"),
            P("tp"),
        ),
        check_vma=False,
    )
```

```python
import functools

import jax
import jax.numpy as jnp
from jax import lax
from jax.experimental import pallas as pl
from jax.experimental.pallas import tpu as pltpu
from jax.sharding import PartitionSpec as P

D = 8192
GROUP = 16
MR_LEN = 128
SE_LEN = 7
EPS = 1e-06

LANES = 128
HALO = 144
S = 32
W = S + MR_LEN
SG = 16
GT = LANES // GROUP
EARLY = S + MR_LEN
F32 = jnp.float32
BF16 = jnp.bfloat16


UNROLL = 8
TAIL_PARTS = 4
BW = 512
PARTS = (0, 1, 4)
WIRE = jnp.bfloat16
VMEM = pl.BlockSpec(memory_space=pltpu.VMEM)
HBM = pl.BlockSpec(memory_space=pltpu.HBM)


def params(limit=24):
    return pltpu.CompilerParams(vmem_limit_bytes=int(limit * 1024 * 1024))


def cost(micros):
    return pl.CostEstimate(flops=int(micros * 1e9), bytes_accessed=0, transcendentals=0)


def each_tile(channels, body):
    unroll = min(UNROLL, channels // LANES)

    def step(i, carry):
        for slot in range(unroll):
            tile = i * unroll + slot
            body(pl.ds(pl.multiple_of(tile * LANES, LANES), LANES), tile, slot)
        return carry

    lax.fori_loop(0, channels // LANES // unroll, step, 0)


def of_tile(tile, rows):
    return pl.ds(pl.multiple_of(tile * rows, rows), rows)


def call(body, name, micros, outs, scratch, *args, out_specs=None, places=None):
    out_specs = out_specs or [VMEM] * len(outs)
    return pl.pallas_call(
        body,
        in_specs=[VMEM] * len(args),
        out_specs=out_specs,
        out_shape=[
            (pltpu.HBM if place is HBM else jax.ShapeDtypeStruct)(shape, dtype)
            for (shape, dtype), place in zip(outs, places or out_specs)
        ],
        scratch_shapes=scratch,
        compiler_params=params(),
        cost_estimate=cost(micros),
        name=name,
    )(*args)


def shifted(x, by):
    peers = lax.axis_size("ctx")
    return lax.ppermute(x, "ctx", [(i, i + by) for i in range(peers) if 0 <= i + by < peers])


def group_of_lane(rows):
    return lax.broadcasted_iota(jnp.int32, (rows, LANES), 1) // GROUP


def toeplitz(table, windows):
    results = []
    which = group_of_lane(S)
    for first in range(0, len(windows), 2):
        pair = windows[first : first + 2]
        rhs = jnp.concatenate(pair, axis=1) if len(pair) == 2 else pair[0]
        out = jnp.dot(table, rhs, preferred_element_type=F32)
        for n in range(len(pair)):
            total = out[:S, n * LANES : (n + 1) * LANES]
            for g in range(1, GT):
                part = out[g * S : (g + 1) * S, n * LANES : (n + 1) * LANES]
                total = jnp.where(which == g, part, total)
            results.append(total)
    return results


def table_kernel(taps_ref, front_out, back_out, rows_ref, back_ref, sem):
    taps = taps_ref[...]
    row_ids = lax.broadcasted_iota(jnp.int32, (MR_LEN, 2 * LANES), 0)
    col_ids = lax.broadcasted_iota(jnp.int32, (MR_LEN, 2 * LANES), 1)
    for n, place in enumerate((MR_LEN - row_ids, row_ids)):
        pick = jnp.where(col_ids == place, 1.0, 0.0).astype(BF16)
        rows_ref[n] = lax.dot_general(taps, pick, (((0,), (0,)), ((), ())), preferred_element_type=F32)

    def fill(n, target):
        def one(g, carry):
            rows = rows_ref[n, of_tile(g, GT), :]
            for k in range(GT):
                row = jnp.broadcast_to(rows[k : k + 1, :], (S, 2 * LANES))
                turned = pltpu.roll(row, 0, 1, stride=1, stride_axis=0).astype(BF16)
                target[of_tile(g * GT + k, S), :] = turned
            return carry

        lax.fori_loop(0, taps_ref.shape[1] // GT, one, 0)

    fill(1, back_ref)
    copy = pltpu.make_async_copy(back_ref, back_out, sem)
    copy.start()
    fill(0, front_out)
    copy.wait()


def tables(mr_filter):
    groups = mr_filter.shape[1]
    shape = ((groups * S, 2 * LANES), BF16)
    scratch = [
        pltpu.VMEM((2, groups, 2 * LANES), F32),
        pltpu.VMEM((groups * S, 2 * LANES), BF16),
        pltpu.SemaphoreType.DMA,
    ]
    specs = [VMEM, HBM]
    return call(table_kernel, "filter_tables", 2.4, [shape, shape], scratch, mr_filter, out_specs=specs)


def short_filter(se_ref, at, gated_ref, first, rows):
    total = jnp.zeros((rows, LANES), F32)
    se = se_ref[:, at].astype(F32)
    for tap in range(SE_LEN):
        total = total + se[tap : tap + 1, :] * gated_ref[first - tap : first - tap + rows, :]
    return total.astype(BF16)


def gate(key_ref, value_ref, rows, at):
    return (key_ref[rows, at].astype(F32) * value_ref[rows, at].astype(F32)).astype(BF16)


def tail_kernel(key_ref, value_ref, tail_out, held_ref, sems):
    tok, channels = key_ref.shape
    width = channels // TAIL_PARTS
    copies = []
    for n in range(TAIL_PARTS):
        at = slice(n * width, (n + 1) * width)
        for m, source in enumerate((key_ref, value_ref)):
            copy = pltpu.make_async_copy(
                source.at[tok - HALO :, at], held_ref.at[m, :, at], sems.at[m, n]
            )
            copy.start()
            copies.append(copy)
    for n in range(TAIL_PARTS):
        copies[2 * n].wait()
        copies[2 * n + 1].wait()
        at = slice(n * width, (n + 1) * width)
        tail_out[:, at] = (held_ref[0, :, at].astype(F32) * held_ref[1, :, at].astype(F32)).astype(BF16)


def tail_rows(key_in, value_in):
    channels = key_in.shape[1]
    return pl.pallas_call(
        tail_kernel,
        in_specs=[HBM, HBM],
        out_specs=VMEM,
        out_shape=pltpu.VMEM((HALO, channels), BF16),
        scratch_shapes=[
            pltpu.VMEM((2, HALO, channels), BF16),
            pltpu.SemaphoreType.DMA((2, TAIL_PARTS)),
        ],
        compiler_params=params(62),
        cost_estimate=cost(1.2),
        name="tail_rows",
    )(key_in, value_in)


def early_kernel(
    key_ref,
    value_ref,
    query_ref,
    out_grad_ref,
    se_ref,
    gain_ref,
    table_ref,
    medium_out,
    short_out,
    wide_out,
    square_out,
    inner_out,
    gated_ref,
):
    tok, channels = key_ref.shape
    square_out[...] = jnp.zeros_like(square_out)
    inner_out[...] = jnp.zeros_like(inner_out)

    def body(at, tile, slot):
        wide_ref = gated_ref.at[slot]
        gated = gate(key_ref, value_ref, slice(None), at)
        wide_ref[...] = gated.astype(F32)
        short_out[:S, at] = jnp.zeros((S, LANES), BF16)
        short_out[S:, at] = short_filter(se_ref, at, wide_ref, S, tok - S)
        short_out[16:S, at] = short_filter(se_ref, at, wide_ref, 16, S - 16)
        table = table_ref[of_tile(tile, GT * S), :W]
        first = [t for t in range(EARLY, tok, S)]
        windows = [short_out[t - MR_LEN : t + S, at] for t in first]
        also = [t for t in range(MR_LEN, tok, S)]
        windows += [gated[t - MR_LEN : t + S, :] for t in also]
        parts = toeplitz(table, windows)
        gain = gain_ref[:, at]
        for t, medium in zip(first, parts):
            down = slice(t - EARLY, t - EARLY + S)
            medium_out[down, at] = medium
            mixed = query_ref[t : t + S, at].astype(F32) * medium
            norm_grad = out_grad_ref[t : t + S, at].astype(F32) * gain
            square_out[down, :] += mixed * mixed
            inner_out[down, :] += norm_grad * mixed
        for t, part in zip(also, parts[len(first) :]):
            wide_out[t - MR_LEN : t - MR_LEN + S, at] = part

    each_tile(channels, body)


def early(key_in, value_in, query, out_grad, se, gain, table):
    tok, channels = key_in.shape
    outs = [
        ((tok - EARLY, channels), F32),
        ((tok, channels), BF16),
        ((tok - MR_LEN, channels), F32),
        ((tok - EARLY, LANES), F32),
        ((tok - EARLY, LANES), F32),
    ]
    scratch = [pltpu.VMEM((UNROLL, tok, LANES), F32)]
    return call(early_kernel, "early", 4.2, outs, scratch, key_in, value_in, query, out_grad, se, gain, table)


def window(low_ref, high_ref, b, at):
    if b * S >= EARLY:
        return high_ref[b * S - MR_LEN : b * S + S, at]
    if b == 0:
        return low_ref[:, at]
    return jnp.concatenate([low_ref[S * b :, at], high_ref[S : S * b + S, at]], axis=0)


def late_kernel(
    halo_ref,
    key_ref,
    value_ref,
    query_ref,
    out_grad_ref,
    se_ref,
    gain_ref,
    table_ref,
    high_ref,
    square_in,
    inner_in,
    medium_out,
    low_out,
    sums_out,
    gated_ref,
    square_ref,
    inner_ref,
):
    channels = key_ref.shape[1]
    square_ref[:EARLY, :] = jnp.zeros((EARLY, LANES), F32)
    inner_ref[:EARLY, :] = jnp.zeros((EARLY, LANES), F32)
    square_ref[EARLY:, :] = square_in[...]
    inner_ref[EARLY:, :] = inner_in[...]

    def body(at, tile, slot):
        rows = gated_ref.at[slot]
        rows[:HALO, :] = halo_ref[:, at].astype(F32)
        rows[HALO:, :] = gate(key_ref, value_ref, slice(0, S), at).astype(F32)
        low_out[:, at] = short_filter(se_ref, at, rows, HALO - MR_LEN, MR_LEN + S)
        table = table_ref[of_tile(tile, GT * S), :W]
        windows = [window(low_out, high_ref, b, at) for b in range(EARLY // S)]
        gain = gain_ref[:, at]
        for b, medium in enumerate(toeplitz(table, windows)):
            down = slice(S * b, S * b + S)
            medium_out[down, at] = medium
            mixed = query_ref[down, at].astype(F32) * medium
            norm_grad = out_grad_ref[down, at].astype(F32) * gain
            square_ref[down, :] += mixed * mixed
            inner_ref[down, :] += norm_grad * mixed

    each_tile(channels, body)
    sums_out[0:1, :] = jnp.sum(square_ref[...].T, axis=0, keepdims=True)
    sums_out[1:2, :] = jnp.sum(inner_ref[...].T, axis=0, keepdims=True)


def late(halo, key_in, value_in, query, out_grad, se, gain, table, short_high, square, inner):
    tok, channels = key_in.shape
    outs = [((EARLY, channels), F32), ((MR_LEN + S, channels), BF16), ((2, tok), F32)]
    scratch = [
        pltpu.VMEM((UNROLL, HALO + S, LANES), F32),
        pltpu.VMEM((tok, LANES), F32),
        pltpu.VMEM((tok, LANES), F32),
    ]
    return call(
        late_kernel,
        "late",
        2.9,
        outs,
        scratch,
        halo,
        key_in,
        value_in,
        query,
        out_grad,
        se,
        gain,
        table,
        short_high,
        square,
        inner,
    )


def spread_sums(parts, scale_ref, slope_ref, rows):
    sums = functools.reduce(jnp.add, [part[...] for part in parts])
    scale = lax.rsqrt(sums[0:1, :] * (1.0 / D) + EPS)
    slope = scale * scale * scale * sums[1:2, :] * (1.0 / D)
    for line, target in ((scale, scale_ref), (slope, slope_ref)):
        target[...] = jnp.broadcast_to(line, (LANES, line.shape[1])).T[:rows]


def head_kernel(query_ref, out_grad_ref, medium_ref, gain_ref, *rest):
    sums, (head_out, scale_ref, slope_ref) = rest[:-3], rest[-3:]
    spread_sums(sums, scale_ref, slope_ref, HALO)

    def body(at, tile, slot):
        query = query_ref[:HALO, at].astype(F32)
        norm_grad = out_grad_ref[:HALO, at].astype(F32) * gain_ref[:, at]
        mixed = query * medium_ref[:HALO, at]
        mixed_grad = scale_ref[...] * norm_grad - mixed * slope_ref[...]
        head_out[:, at] = (mixed_grad * query).astype(BF16)

    each_tile(query_ref.shape[1], body)


def head(sums, query, out_grad, medium_low, gain):
    outs = [((HALO, query.shape[1]), BF16)]
    scratch = [pltpu.VMEM((HALO, LANES), F32), pltpu.VMEM((HALO, LANES), F32)]
    return call(head_kernel, "head_rows", 0.9, outs, scratch, query, out_grad, medium_low, gain, *sums)[0]


def wide_kernel(halo_ref, key_ref, value_ref, table_ref, wide_out, gated_ref):
    lead = W - HALO

    def body(at, tile, slot):
        rows = gated_ref.at[slot]
        rows[:lead, :] = jnp.zeros((lead, LANES), BF16)
        rows[lead:W, :] = halo_ref[:, at]
        rows[W:, :] = gate(key_ref, value_ref, slice(0, MR_LEN), at)
        windows = [rows[S * b : S * b + W, :] for b in range(MR_LEN // S + 1)]
        for b, part in enumerate(toeplitz(table_ref[of_tile(tile, GT * S), :W], windows)):
            wide_out[S * b : S * b + S, at] = part

    each_tile(key_ref.shape[1], body)


def wide(halo, key_in, value_in, table):
    outs = [((MR_LEN + S, key_in.shape[1]), F32)]
    scratch = [pltpu.VMEM((UNROLL, W + MR_LEN, LANES), BF16)]
    return call(wide_kernel, "wide_gated", 2.0, outs, scratch, halo, key_in, value_in, table)[0]


def grads_kernel(
    query_ref,
    out_grad_ref,
    medium_low_ref,
    medium_high_ref,
    gain_ref,
    short_low_ref,
    short_high_ref,
    wide_low_ref,
    wide_high_ref,
    *rest,
):
    query_grad_out, medium_grad_out, packed_out, scale_ref, slope_ref, cross_ref, wide_ref = rest[-7:]
    tok, channels = query_ref.shape
    spread_sums(rest[:-7], scale_ref, slope_ref, tok)
    blocks = tok // SG
    side = GT * SG

    def body(at, tile, slot):
        query = query_ref[:, at].astype(F32)
        out_grad = out_grad_ref[:, at].astype(F32)
        medium = jnp.concatenate([medium_low_ref[:, at], medium_high_ref[:, at]], axis=0)
        inv = scale_ref[...]
        norm_grad = out_grad * gain_ref[:, at]
        mixed = query * medium
        mixed_grad = inv * norm_grad - mixed * slope_ref[...]
        query_grad_out[:, at] = (mixed_grad * medium).astype(BF16)
        medium_grad = (mixed_grad * query).astype(BF16)
        medium_grad_out[:, at] = medium_grad
        gain_row = jnp.sum(out_grad * mixed * inv, axis=0, keepdims=True)
        wide_grad = medium_grad.astype(F32)
        rows = wide_ref.at[slot]
        rows[: MR_LEN + S, :] = wide_low_ref[:, at]
        rows[MR_LEN + S :, :] = wide_high_ref[:, at]
        lines = [
            jnp.sum(wide_grad * rows[S - tap : S - tap + tok, :], axis=0, keepdims=True)
            for tap in range(SE_LEN)
        ]
        lhs_rows = jnp.concatenate([medium_grad[SG * b : SG * b + SG, :] for b in range(blocks)], axis=1)
        which = lax.broadcasted_iota(jnp.int32, lhs_rows.shape, 1) % LANES // GROUP
        lhs = jnp.concatenate(
            [jnp.where(which == g, lhs_rows, jnp.zeros_like(lhs_rows)) for g in range(GT)], axis=0
        )
        short = jnp.concatenate([short_low_ref[:, at], short_high_ref[S:, at]], axis=0)
        rhs = jnp.concatenate([short[SG * b : SG * b + SG + MR_LEN, :] for b in range(blocks)], axis=1)
        cross = lax.dot_general(lhs, rhs, (((1,), (1,)), ((), ())), preferred_element_type=F32)
        held = cross_ref.at[slot]
        held[:side, :] = cross[:, :LANES]
        held[side:, :SG] = cross[:, LANES:]
        total = jnp.zeros((GT, 2 * LANES), F32)
        for s in range(SG):
            part = jnp.concatenate(
                [held[pl.ds(m * side + s, GT, stride=SG), :] for m in range(2)], axis=1
            )
            total = total + pltpu.roll(part, 2 * LANES - 1 - s, 1)
        packed_out[of_tile(tile, 2 * GT), :] = jnp.concatenate(
            [total[:, :LANES]] + lines + [gain_row], axis=0
        ).astype(WIRE)

    each_tile(channels, body)


def grads(sums, query, out_grad, medium_low, medium_high, gain, short_low, short_high, wide_low, wide_high):
    tok, channels = query.shape
    outs = [
        ((tok, channels), BF16),
        ((tok, channels), BF16),
        ((2 * GT * channels // LANES, LANES), WIRE),
    ]
    scratch = [
        pltpu.VMEM((tok, LANES), F32),
        pltpu.VMEM((tok, LANES), F32),
        pltpu.VMEM((UNROLL, 2 * GT * SG, LANES), F32),
        pltpu.VMEM((UNROLL, tok + S, LANES), F32),
    ]
    return call(
        grads_kernel,
        "gradients",
        6.6,
        outs,
        scratch,
        query,
        out_grad,
        medium_low,
        medium_high,
        gain,
        short_low,
        short_high,
        wide_low,
        wide_high,
        *sums,
        places=[HBM, HBM, VMEM],
    )


def backward_kernel(grad_ref, halo_ref, se_ref, key_ref, value_ref, table_ref, *rest):
    key_out, value_out, ext_ref, short_ref = rest[-4:]
    tok = key_ref.shape[0]

    def body(at, tile, slot):
        ext = ext_ref.at[slot]
        short = short_ref.at[slot]
        ext[:tok, :] = grad_ref[:, at]
        ext[tok : tok + HALO, :] = halo_ref[:, at]
        ext[tok + HALO :, :] = jnp.zeros((W - HALO, LANES), BF16)
        windows = [ext[S * b : S * b + W, :] for b in range(tok // S + 1)]
        for b, part in enumerate(toeplitz(table_ref[of_tile(tile, GT * S), :W], windows)):
            short[S * b : S * b + S, :] = part
        total = jnp.zeros((tok, LANES), F32)
        se = se_ref[:, at].astype(F32)
        for tap in range(SE_LEN):
            total = total + se[tap : tap + 1, :] * short[tap : tap + tok, :]
        key_out[:, at] = (total * value_ref[:, at].astype(F32)).astype(BF16)
        value_out[:, at] = (total * key_ref[:, at].astype(F32)).astype(BF16)

    each_tile(key_ref.shape[1], body)


def backward(medium_grad, halo, se, key_in, value_in, table, part, done=()):
    tok, channels = key_in.shape
    first, steps = PARTS[part], PARTS[part + 1] - PARTS[part]
    col = lambda rows: pl.BlockSpec((rows, BW), lambda i: (0, first + i))
    tiles = BW // LANES
    shape = jax.ShapeDtypeStruct((tok, channels), BF16)
    return pl.pallas_call(
        backward_kernel,
        grid=(steps,),
        in_specs=[
            col(tok),
            col(HALO),
            col(SE_LEN),
            col(tok),
            col(tok),
            pl.BlockSpec((tiles * GT * S, 2 * LANES), lambda i: (first + i, 0)),
        ]
        + [HBM] * len(done),
        out_specs=[col(tok), col(tok)],
        out_shape=[shape, shape],
        scratch_shapes=[
            pltpu.VMEM((tiles, tok + W, LANES), BF16),
            pltpu.VMEM((tiles, tok + S, LANES), F32),
        ],
        input_output_aliases={6 + n: n for n in range(len(done))},
        compiler_params=params(62),
        cost_estimate=cost(2.0 * steps),
        name="backward",
    )(medium_grad, halo, se, key_in, value_in, table, *done)


def finish_kernel(tokens, packed_ref, mr_out, se_out, gain_out):
    packed = packed_ref[...].astype(F32)
    tiles = packed.shape[0] // (2 * GT)
    rows = jnp.concatenate([packed[2 * GT * i : 2 * GT * i + GT, :] for i in range(tiles)], axis=0)
    row_ids = lax.broadcasted_iota(jnp.int32, (MR_LEN, MR_LEN), 0)
    col_ids = lax.broadcasted_iota(jnp.int32, (MR_LEN, MR_LEN), 1)
    flip = jnp.where(row_ids + col_ids == MR_LEN - 1, 1.0, 0.0).astype(WIRE)
    mr_out[...] = lax.dot_general(
        flip, rows.astype(WIRE), (((1,), (1,)), ((), ())), preferred_element_type=F32
    ) * (1.0 / (tokens * GROUP) ** 0.5)
    for i in range(tiles):
        at = slice(i * LANES, (i + 1) * LANES)
        low = 2 * GT * i + GT
        se_out[:, at] = packed[low : low + SE_LEN, :] * (1.0 / tokens**0.5)
        gain_out[:, at] = packed[low + SE_LEN : low + SE_LEN + 1, :] * (1.0 / tokens**0.5)


def finish(packed, tokens, channels):
    return pl.pallas_call(
        functools.partial(finish_kernel, tokens),
        out_shape=[
            jax.ShapeDtypeStruct((MR_LEN, channels // GROUP), F32),
            jax.ShapeDtypeStruct((SE_LEN, channels), F32),
            jax.ShapeDtypeStruct((1, channels), F32),
        ],
        compiler_params=params(),
        cost_estimate=cost(0.9),
        name="finish",
    )(packed)


def from_peers(x, axis):
    peers = lax.axis_size(axis)
    return [lax.ppermute(x, axis, [(i, (i + k) % peers) for i in range(peers)]) for k in range(1, peers)]


def sum_over_ctx(packed, beside):
    peers = lax.axis_size("ctx")
    parts = packed.astype(WIRE).reshape(peers, packed.shape[0] // peers, packed.shape[1])
    arrived, done = lax.optimization_barrier((lax.all_to_all(parts, "ctx", 0, 0), beside(0)))
    mine = jnp.sum(arrived.astype(F32), axis=0).astype(WIRE)
    mine, done = lax.optimization_barrier((mine, done))
    everyone = lax.all_to_all(jnp.broadcast_to(mine[None], parts.shape), "ctx", 0, 0)
    everyone, done = lax.optimization_barrier((everyone, beside(1, done)))
    return everyone.reshape(packed.shape), done


def local(query, key_in, value_in, out_grad, mr_filter, se_filter, gain):
    tok, channels = query.shape
    tokens_all = tok * lax.axis_size("ctx")
    gated_halo = shifted(tail_rows(key_in, value_in), 1)
    front_table, back_table = tables(mr_filter)
    se = se_filter
    gain_row = gain[None, :]
    medium_high, short_high, wide_high, square, inner = early(
        key_in, value_in, query, out_grad, se, gain_row, front_table
    )
    medium_low, short_low, sums = late(
        gated_halo,
        key_in,
        value_in,
        query,
        out_grad,
        se,
        gain_row,
        front_table,
        short_high,
        square,
        inner,
    )
    sums = [sums] + from_peers(sums, "tp")
    wide_low = wide(gated_halo, key_in, value_in, front_table)
    sums, wide_low = lax.optimization_barrier((sums, wide_low))
    head_rows = head(sums, query, out_grad, medium_low, gain_row)
    grad_halo = shifted(head_rows, -1)
    query_grad, medium_grad, packed = grads(
        sums,
        query,
        out_grad,
        medium_low,
        medium_high,
        gain_row,
        short_low,
        short_high,
        wide_low,
        wide_high,
    )
    packed, (key_grad, value_grad) = sum_over_ctx(
        packed, functools.partial(backward, medium_grad, grad_halo, se, key_in, value_in, back_table)
    )
    mr_grad, se_grad, gain_grad = finish(packed, tokens_all, channels)
    return query_grad, key_grad, value_grad, mr_grad, se_grad, gain_grad[0]


def solution(mesh):
    return jax.shard_map(
        local,
        mesh=mesh,
        in_specs=(
            P("ctx", "tp"),
            P("ctx", "tp"),
            P("ctx", "tp"),
            P("ctx", "tp"),
            P(None, "tp"),
            P(None, "tp"),
            P("tp"),
        ),
        out_specs=(
            P("ctx", "tp"),
            P("ctx", "tp"),
            P("ctx", "tp"),
            P(None, "tp"),
            P(None, "tp"),
            P("tp"),
        ),
        check_vma=False,
    )
```

```python
import functools

import jax
import jax.numpy as jnp
from jax import lax
from jax.experimental import pallas as pl
from jax.experimental.pallas import tpu as pltpu
from jax.sharding import PartitionSpec as P

D = 8192
GROUP = 16
MR_LEN = 128
SE_LEN = 7
EPS = 1e-06

LANES = 128
HALO = 144
S = 32
W = S + MR_LEN
SG = 16
GT = LANES // GROUP
EARLY = S + MR_LEN
F32 = jnp.float32
BF16 = jnp.bfloat16


UNROLL = 8
TAIL_PARTS = 2
BW = 512
PARTS = (0, 1, 4)
WIRE = jnp.bfloat16
VMEM = pl.BlockSpec(memory_space=pltpu.VMEM)
HBM = pl.BlockSpec(memory_space=pltpu.HBM)


def params(limit=24):
    return pltpu.CompilerParams(vmem_limit_bytes=int(limit * 1024 * 1024))


def cost(micros):
    return pl.CostEstimate(flops=int(micros * 1e9), bytes_accessed=0, transcendentals=0)


def each_tile(channels, body):
    unroll = min(UNROLL, channels // LANES)

    def step(i, carry):
        for slot in range(unroll):
            tile = i * unroll + slot
            body(pl.ds(pl.multiple_of(tile * LANES, LANES), LANES), tile, slot)
        return carry

    lax.fori_loop(0, channels // LANES // unroll, step, 0)


def of_tile(tile, rows):
    return pl.ds(pl.multiple_of(tile * rows, rows), rows)


def call(body, name, micros, outs, scratch, *args, out_specs=None, places=None):
    out_specs = out_specs or [VMEM] * len(outs)
    return pl.pallas_call(
        body,
        in_specs=[VMEM] * len(args),
        out_specs=out_specs,
        out_shape=[
            (pltpu.HBM if place is HBM else jax.ShapeDtypeStruct)(shape, dtype)
            for (shape, dtype), place in zip(outs, places or out_specs)
        ],
        scratch_shapes=scratch,
        compiler_params=params(),
        cost_estimate=cost(micros),
        name=name,
    )(*args)


def shifted(x, by):
    peers = lax.axis_size("ctx")
    return lax.ppermute(x, "ctx", [(i, i + by) for i in range(peers) if 0 <= i + by < peers])


def group_of_lane(rows):
    return lax.broadcasted_iota(jnp.int32, (rows, LANES), 1) // GROUP


def toeplitz(table, windows):
    results = []
    which = group_of_lane(S)
    for first in range(0, len(windows), 2):
        pair = windows[first : first + 2]
        rhs = jnp.concatenate(pair, axis=1) if len(pair) == 2 else pair[0]
        out = jnp.dot(table, rhs, preferred_element_type=F32)
        for n in range(len(pair)):
            total = out[:S, n * LANES : (n + 1) * LANES]
            for g in range(1, GT):
                part = out[g * S : (g + 1) * S, n * LANES : (n + 1) * LANES]
                total = jnp.where(which == g, part, total)
            results.append(total)
    return results


def table_kernel(taps_ref, front_out, back_out, rows_ref, back_ref, sem):
    taps = taps_ref[...]
    row_ids = lax.broadcasted_iota(jnp.int32, (MR_LEN, 2 * LANES), 0)
    col_ids = lax.broadcasted_iota(jnp.int32, (MR_LEN, 2 * LANES), 1)
    for n, place in enumerate((MR_LEN - row_ids, row_ids)):
        pick = jnp.where(col_ids == place, 1.0, 0.0).astype(BF16)
        rows_ref[n] = lax.dot_general(taps, pick, (((0,), (0,)), ((), ())), preferred_element_type=F32)

    def fill(n, target):
        def one(g, carry):
            rows = rows_ref[n, of_tile(g, GT), :]
            for k in range(GT):
                row = jnp.broadcast_to(rows[k : k + 1, :], (S, 2 * LANES))
                turned = pltpu.roll(row, 0, 1, stride=1, stride_axis=0).astype(BF16)
                target[of_tile(g * GT + k, S), :] = turned
            return carry

        lax.fori_loop(0, taps_ref.shape[1] // GT, one, 0)

    fill(1, back_ref)
    copy = pltpu.make_async_copy(back_ref, back_out, sem)
    copy.start()
    fill(0, front_out)
    copy.wait()


def tables(mr_filter):
    groups = mr_filter.shape[1]
    shape = ((groups * S, 2 * LANES), BF16)
    scratch = [
        pltpu.VMEM((2, groups, 2 * LANES), F32),
        pltpu.VMEM((groups * S, 2 * LANES), BF16),
        pltpu.SemaphoreType.DMA,
    ]
    specs = [VMEM, HBM]
    return call(table_kernel, "filter_tables", 2.4, [shape, shape], scratch, mr_filter, out_specs=specs)


def short_filter(se_ref, at, gated_ref, first, rows):
    total = jnp.zeros((rows, LANES), F32)
    se = se_ref[:, at].astype(F32)
    for tap in range(SE_LEN):
        total = total + se[tap : tap + 1, :] * gated_ref[first - tap : first - tap + rows, :]
    return total.astype(BF16)


def gate(key_ref, value_ref, rows, at):
    return (key_ref[rows, at].astype(F32) * value_ref[rows, at].astype(F32)).astype(BF16)


def tail_kernel(key_ref, value_ref, tail_out, held_ref, sems):
    tok, channels = key_ref.shape
    width = channels // TAIL_PARTS
    copies = []
    for n in range(TAIL_PARTS):
        at = slice(n * width, (n + 1) * width)
        for m, source in enumerate((key_ref, value_ref)):
            copy = pltpu.make_async_copy(
                source.at[tok - HALO :, at], held_ref.at[m, :, at], sems.at[m, n]
            )
            copy.start()
            copies.append(copy)
    for n in range(TAIL_PARTS):
        copies[2 * n].wait()
        copies[2 * n + 1].wait()
        at = slice(n * width, (n + 1) * width)
        tail_out[:, at] = (held_ref[0, :, at].astype(F32) * held_ref[1, :, at].astype(F32)).astype(BF16)


def tail_rows(key_in, value_in):
    channels = key_in.shape[1]
    return pl.pallas_call(
        tail_kernel,
        in_specs=[HBM, HBM],
        out_specs=VMEM,
        out_shape=pltpu.VMEM((HALO, channels), BF16),
        scratch_shapes=[
            pltpu.VMEM((2, HALO, channels), BF16),
            pltpu.SemaphoreType.DMA((2, TAIL_PARTS)),
        ],
        compiler_params=params(62),
        cost_estimate=cost(1.2),
        name="tail_rows",
    )(key_in, value_in)


def early_kernel(
    key_ref,
    value_ref,
    query_ref,
    out_grad_ref,
    se_ref,
    gain_ref,
    table_ref,
    medium_out,
    short_out,
    wide_out,
    square_out,
    inner_out,
    gated_ref,
):
    tok, channels = key_ref.shape
    square_out[...] = jnp.zeros_like(square_out)
    inner_out[...] = jnp.zeros_like(inner_out)

    def body(at, tile, slot):
        wide_ref = gated_ref.at[slot]
        gated = gate(key_ref, value_ref, slice(None), at)
        wide_ref[...] = gated.astype(F32)
        short_out[:S, at] = jnp.zeros((S, LANES), BF16)
        short_out[S:, at] = short_filter(se_ref, at, wide_ref, S, tok - S)
        short_out[16:S, at] = short_filter(se_ref, at, wide_ref, 16, S - 16)
        table = table_ref[of_tile(tile, GT * S), :W]
        first = [t for t in range(EARLY, tok, S)]
        windows = [short_out[t - MR_LEN : t + S, at] for t in first]
        also = [t for t in range(MR_LEN, tok, S)]
        windows += [gated[t - MR_LEN : t + S, :] for t in also]
        parts = toeplitz(table, windows)
        gain = gain_ref[:, at]
        for t, medium in zip(first, parts):
            down = slice(t - EARLY, t - EARLY + S)
            medium_out[down, at] = medium
            mixed = query_ref[t : t + S, at].astype(F32) * medium
            norm_grad = out_grad_ref[t : t + S, at].astype(F32) * gain
            square_out[down, :] += mixed * mixed
            inner_out[down, :] += norm_grad * mixed
        for t, part in zip(also, parts[len(first) :]):
            wide_out[t - MR_LEN : t - MR_LEN + S, at] = part

    each_tile(channels, body)


def early(key_in, value_in, query, out_grad, se, gain, table):
    tok, channels = key_in.shape
    outs = [
        ((tok - EARLY, channels), F32),
        ((tok, channels), BF16),
        ((tok - MR_LEN, channels), F32),
        ((tok - EARLY, LANES), F32),
        ((tok - EARLY, LANES), F32),
    ]
    scratch = [pltpu.VMEM((UNROLL, tok, LANES), F32)]
    return call(early_kernel, "early", 4.2, outs, scratch, key_in, value_in, query, out_grad, se, gain, table)


def window(low_ref, high_ref, b, at):
    if b * S >= EARLY:
        return high_ref[b * S - MR_LEN : b * S + S, at]
    if b == 0:
        return low_ref[:, at]
    return jnp.concatenate([low_ref[S * b :, at], high_ref[S : S * b + S, at]], axis=0)


def late_kernel(
    halo_ref,
    key_ref,
    value_ref,
    query_ref,
    out_grad_ref,
    se_ref,
    gain_ref,
    table_ref,
    high_ref,
    square_in,
    inner_in,
    medium_out,
    low_out,
    sums_out,
    gated_ref,
    square_ref,
    inner_ref,
):
    channels = key_ref.shape[1]
    square_ref[:EARLY, :] = jnp.zeros((EARLY, LANES), F32)
    inner_ref[:EARLY, :] = jnp.zeros((EARLY, LANES), F32)
    square_ref[EARLY:, :] = square_in[...]
    inner_ref[EARLY:, :] = inner_in[...]

    def body(at, tile, slot):
        rows = gated_ref.at[slot]
        rows[:HALO, :] = halo_ref[:, at].astype(F32)
        rows[HALO:, :] = gate(key_ref, value_ref, slice(0, S), at).astype(F32)
        low_out[:, at] = short_filter(se_ref, at, rows, HALO - MR_LEN, MR_LEN + S)
        table = table_ref[of_tile(tile, GT * S), :W]
        windows = [window(low_out, high_ref, b, at) for b in range(EARLY // S)]
        gain = gain_ref[:, at]
        for b, medium in enumerate(toeplitz(table, windows)):
            down = slice(S * b, S * b + S)
            medium_out[down, at] = medium
            mixed = query_ref[down, at].astype(F32) * medium
            norm_grad = out_grad_ref[down, at].astype(F32) * gain
            square_ref[down, :] += mixed * mixed
            inner_ref[down, :] += norm_grad * mixed

    each_tile(channels, body)
    sums_out[0:1, :] = jnp.sum(square_ref[...].T, axis=0, keepdims=True)
    sums_out[1:2, :] = jnp.sum(inner_ref[...].T, axis=0, keepdims=True)


def late(halo, key_in, value_in, query, out_grad, se, gain, table, short_high, square, inner):
    tok, channels = key_in.shape
    outs = [((EARLY, channels), F32), ((MR_LEN + S, channels), BF16), ((2, tok), F32)]
    scratch = [
        pltpu.VMEM((UNROLL, HALO + S, LANES), F32),
        pltpu.VMEM((tok, LANES), F32),
        pltpu.VMEM((tok, LANES), F32),
    ]
    return call(
        late_kernel,
        "late",
        2.9,
        outs,
        scratch,
        halo,
        key_in,
        value_in,
        query,
        out_grad,
        se,
        gain,
        table,
        short_high,
        square,
        inner,
    )


def spread_sums(parts, scale_ref, slope_ref, rows):
    sums = functools.reduce(jnp.add, [part[...] for part in parts])
    scale = lax.rsqrt(sums[0:1, :] * (1.0 / D) + EPS)
    slope = scale * scale * scale * sums[1:2, :] * (1.0 / D)
    for line, target in ((scale, scale_ref), (slope, slope_ref)):
        target[...] = jnp.broadcast_to(line, (LANES, line.shape[1])).T[:rows]


def head_kernel(query_ref, out_grad_ref, medium_ref, gain_ref, *rest):
    sums, (head_out, scale_ref, slope_ref) = rest[:-3], rest[-3:]
    spread_sums(sums, scale_ref, slope_ref, HALO)

    def body(at, tile, slot):
        query = query_ref[:HALO, at].astype(F32)
        norm_grad = out_grad_ref[:HALO, at].astype(F32) * gain_ref[:, at]
        mixed = query * medium_ref[:HALO, at]
        mixed_grad = scale_ref[...] * norm_grad - mixed * slope_ref[...]
        head_out[:, at] = (mixed_grad * query).astype(BF16)

    each_tile(query_ref.shape[1], body)


def head(sums, query, out_grad, medium_low, gain):
    outs = [((HALO, query.shape[1]), BF16)]
    scratch = [pltpu.VMEM((HALO, LANES), F32), pltpu.VMEM((HALO, LANES), F32)]
    return call(head_kernel, "head_rows", 0.9, outs, scratch, query, out_grad, medium_low, gain, *sums)[0]


def wide_kernel(halo_ref, key_ref, value_ref, table_ref, wide_out, gated_ref):
    lead = W - HALO

    def body(at, tile, slot):
        rows = gated_ref.at[slot]
        rows[:lead, :] = jnp.zeros((lead, LANES), BF16)
        rows[lead:W, :] = halo_ref[:, at]
        rows[W:, :] = gate(key_ref, value_ref, slice(0, MR_LEN), at)
        windows = [rows[S * b : S * b + W, :] for b in range(MR_LEN // S + 1)]
        for b, part in enumerate(toeplitz(table_ref[of_tile(tile, GT * S), :W], windows)):
            wide_out[S * b : S * b + S, at] = part

    each_tile(key_ref.shape[1], body)


def wide(halo, key_in, value_in, table):
    outs = [((MR_LEN + S, key_in.shape[1]), F32)]
    scratch = [pltpu.VMEM((UNROLL, W + MR_LEN, LANES), BF16)]
    return call(wide_kernel, "wide_gated", 2.0, outs, scratch, halo, key_in, value_in, table)[0]


def grads_kernel(
    query_ref,
    out_grad_ref,
    medium_low_ref,
    medium_high_ref,
    gain_ref,
    short_low_ref,
    short_high_ref,
    wide_low_ref,
    wide_high_ref,
    *rest,
):
    query_grad_out, medium_grad_out, packed_out, scale_ref, slope_ref, cross_ref, wide_ref = rest[-7:]
    tok, channels = query_ref.shape
    spread_sums(rest[:-7], scale_ref, slope_ref, tok)
    blocks = tok // SG
    side = GT * SG

    def body(at, tile, slot):
        query = query_ref[:, at].astype(F32)
        out_grad = out_grad_ref[:, at].astype(F32)
        medium = jnp.concatenate([medium_low_ref[:, at], medium_high_ref[:, at]], axis=0)
        inv = scale_ref[...]
        norm_grad = out_grad * gain_ref[:, at]
        mixed = query * medium
        mixed_grad = inv * norm_grad - mixed * slope_ref[...]
        query_grad_out[:, at] = (mixed_grad * medium).astype(BF16)
        medium_grad = (mixed_grad * query).astype(BF16)
        medium_grad_out[:, at] = medium_grad
        gain_row = jnp.sum(out_grad * mixed * inv, axis=0, keepdims=True)
        wide_grad = medium_grad.astype(F32)
        rows = wide_ref.at[slot]
        rows[: MR_LEN + S, :] = wide_low_ref[:, at]
        rows[MR_LEN + S :, :] = wide_high_ref[:, at]
        lines = [
            jnp.sum(wide_grad * rows[S - tap : S - tap + tok, :], axis=0, keepdims=True)
            for tap in range(SE_LEN)
        ]
        lhs_rows = jnp.concatenate([medium_grad[SG * b : SG * b + SG, :] for b in range(blocks)], axis=1)
        which = lax.broadcasted_iota(jnp.int32, lhs_rows.shape, 1) % LANES // GROUP
        lhs = jnp.concatenate(
            [jnp.where(which == g, lhs_rows, jnp.zeros_like(lhs_rows)) for g in range(GT)], axis=0
        )
        short = jnp.concatenate([short_low_ref[:, at], short_high_ref[S:, at]], axis=0)
        rhs = jnp.concatenate([short[SG * b : SG * b + SG + MR_LEN, :] for b in range(blocks)], axis=1)
        cross = lax.dot_general(lhs, rhs, (((1,), (1,)), ((), ())), preferred_element_type=F32)
        held = cross_ref.at[slot]
        held[:side, :] = cross[:, :LANES]
        held[side:, :SG] = cross[:, LANES:]
        total = jnp.zeros((GT, 2 * LANES), F32)
        for s in range(SG):
            part = jnp.concatenate(
                [held[pl.ds(m * side + s, GT, stride=SG), :] for m in range(2)], axis=1
            )
            total = total + pltpu.roll(part, 2 * LANES - 1 - s, 1)
        packed_out[of_tile(tile, 2 * GT), :] = jnp.concatenate(
            [total[:, :LANES]] + lines + [gain_row], axis=0
        ).astype(WIRE)

    each_tile(channels, body)


def grads(sums, query, out_grad, medium_low, medium_high, gain, short_low, short_high, wide_low, wide_high):
    tok, channels = query.shape
    outs = [
        ((tok, channels), BF16),
        ((tok, channels), BF16),
        ((2 * GT * channels // LANES, LANES), WIRE),
    ]
    scratch = [
        pltpu.VMEM((tok, LANES), F32),
        pltpu.VMEM((tok, LANES), F32),
        pltpu.VMEM((UNROLL, 2 * GT * SG, LANES), F32),
        pltpu.VMEM((UNROLL, tok + S, LANES), F32),
    ]
    return call(
        grads_kernel,
        "gradients",
        6.6,
        outs,
        scratch,
        query,
        out_grad,
        medium_low,
        medium_high,
        gain,
        short_low,
        short_high,
        wide_low,
        wide_high,
        *sums,
        places=[HBM, HBM, VMEM],
    )


def backward_kernel(grad_ref, halo_ref, se_ref, key_ref, value_ref, table_ref, *rest):
    key_out, value_out, ext_ref, short_ref = rest[-4:]
    tok = key_ref.shape[0]

    def body(at, tile, slot):
        ext = ext_ref.at[slot]
        short = short_ref.at[slot]
        ext[:tok, :] = grad_ref[:, at]
        ext[tok : tok + HALO, :] = halo_ref[:, at]
        ext[tok + HALO :, :] = jnp.zeros((W - HALO, LANES), BF16)
        windows = [ext[S * b : S * b + W, :] for b in range(tok // S + 1)]
        for b, part in enumerate(toeplitz(table_ref[of_tile(tile, GT * S), :W], windows)):
            short[S * b : S * b + S, :] = part
        total = jnp.zeros((tok, LANES), F32)
        se = se_ref[:, at].astype(F32)
        for tap in range(SE_LEN):
            total = total + se[tap : tap + 1, :] * short[tap : tap + tok, :]
        key_out[:, at] = (total * value_ref[:, at].astype(F32)).astype(BF16)
        value_out[:, at] = (total * key_ref[:, at].astype(F32)).astype(BF16)

    each_tile(key_ref.shape[1], body)


def backward(medium_grad, halo, se, key_in, value_in, table, part, done=()):
    tok, channels = key_in.shape
    first, steps = PARTS[part], PARTS[part + 1] - PARTS[part]
    col = lambda rows: pl.BlockSpec((rows, BW), lambda i: (0, first + i))
    tiles = BW // LANES
    shape = jax.ShapeDtypeStruct((tok, channels), BF16)
    return pl.pallas_call(
        backward_kernel,
        grid=(steps,),
        in_specs=[
            col(tok),
            col(HALO),
            col(SE_LEN),
            col(tok),
            col(tok),
            pl.BlockSpec((tiles * GT * S, 2 * LANES), lambda i: (first + i, 0)),
        ]
        + [HBM] * len(done),
        out_specs=[col(tok), col(tok)],
        out_shape=[shape, shape],
        scratch_shapes=[
            pltpu.VMEM((tiles, tok + W, LANES), BF16),
            pltpu.VMEM((tiles, tok + S, LANES), F32),
        ],
        input_output_aliases={6 + n: n for n in range(len(done))},
        compiler_params=params(62),
        cost_estimate=cost(2.0 * steps),
        name="backward",
    )(medium_grad, halo, se, key_in, value_in, table, *done)


def finish_kernel(tokens, packed_ref, mr_out, se_out, gain_out):
    packed = packed_ref[...].astype(F32)
    tiles = packed.shape[0] // (2 * GT)
    rows = jnp.concatenate([packed[2 * GT * i : 2 * GT * i + GT, :] for i in range(tiles)], axis=0)
    row_ids = lax.broadcasted_iota(jnp.int32, (MR_LEN, MR_LEN), 0)
    col_ids = lax.broadcasted_iota(jnp.int32, (MR_LEN, MR_LEN), 1)
    flip = jnp.where(row_ids + col_ids == MR_LEN - 1, 1.0, 0.0).astype(WIRE)
    mr_out[...] = lax.dot_general(
        flip, rows.astype(WIRE), (((1,), (1,)), ((), ())), preferred_element_type=F32
    ) * (1.0 / (tokens * GROUP) ** 0.5)
    for i in range(tiles):
        at = slice(i * LANES, (i + 1) * LANES)
        low = 2 * GT * i + GT
        se_out[:, at] = packed[low : low + SE_LEN, :] * (1.0 / tokens**0.5)
        gain_out[:, at] = packed[low + SE_LEN : low + SE_LEN + 1, :] * (1.0 / tokens**0.5)


def finish(packed, tokens, channels):
    return pl.pallas_call(
        functools.partial(finish_kernel, tokens),
        out_shape=[
            jax.ShapeDtypeStruct((MR_LEN, channels // GROUP), F32),
            jax.ShapeDtypeStruct((SE_LEN, channels), F32),
            jax.ShapeDtypeStruct((1, channels), F32),
        ],
        compiler_params=params(),
        cost_estimate=cost(0.9),
        name="finish",
    )(packed)


def from_peers(x, axis):
    peers = lax.axis_size(axis)
    return [lax.ppermute(x, axis, [(i, (i + k) % peers) for i in range(peers)]) for k in range(1, peers)]


def sum_over_ctx(packed, beside):
    peers = lax.axis_size("ctx")
    parts = packed.astype(WIRE).reshape(peers, packed.shape[0] // peers, packed.shape[1])
    arrived, done = lax.optimization_barrier((lax.all_to_all(parts, "ctx", 0, 0), beside(0)))
    mine = jnp.sum(arrived.astype(F32), axis=0).astype(WIRE)
    mine, done = lax.optimization_barrier((mine, done))
    everyone = lax.all_to_all(jnp.broadcast_to(mine[None], parts.shape), "ctx", 0, 0)
    everyone, done = lax.optimization_barrier((everyone, beside(1, done)))
    return everyone.reshape(packed.shape), done


def local(query, key_in, value_in, out_grad, mr_filter, se_filter, gain):
    tok, channels = query.shape
    tokens_all = tok * lax.axis_size("ctx")
    gated_halo = shifted(tail_rows(key_in, value_in), 1)
    front_table, back_table = tables(mr_filter)
    se = se_filter
    gain_row = gain[None, :]
    medium_high, short_high, wide_high, square, inner = early(
        key_in, value_in, query, out_grad, se, gain_row, front_table
    )
    medium_low, short_low, sums = late(
        gated_halo,
        key_in,
        value_in,
        query,
        out_grad,
        se,
        gain_row,
        front_table,
        short_high,
        square,
        inner,
    )
    sums = [sums] + from_peers(sums, "tp")
    wide_low = wide(gated_halo, key_in, value_in, front_table)
    sums, wide_low = lax.optimization_barrier((sums, wide_low))
    head_rows = head(sums, query, out_grad, medium_low, gain_row)
    grad_halo = shifted(head_rows, -1)
    query_grad, medium_grad, packed = grads(
        sums,
        query,
        out_grad,
        medium_low,
        medium_high,
        gain_row,
        short_low,
        short_high,
        wide_low,
        wide_high,
    )
    packed, (key_grad, value_grad) = sum_over_ctx(
        packed, functools.partial(backward, medium_grad, grad_halo, se, key_in, value_in, back_table)
    )
    mr_grad, se_grad, gain_grad = finish(packed, tokens_all, channels)
    return query_grad, key_grad, value_grad, mr_grad, se_grad, gain_grad[0]


def solution(mesh):
    return jax.shard_map(
        local,
        mesh=mesh,
        in_specs=(
            P("ctx", "tp"),
            P("ctx", "tp"),
            P("ctx", "tp"),
            P("ctx", "tp"),
            P(None, "tp"),
            P(None, "tp"),
            P("tp"),
        ),
        out_specs=(
            P("ctx", "tp"),
            P("ctx", "tp"),
            P("ctx", "tp"),
            P(None, "tp"),
            P(None, "tp"),
            P("tp"),
        ),
        check_vma=False,
    )
```
